256 devices in a mesh: seq: 64 (over z, x, core), chan: 4 (over y).
Axes of the slice: x: 4, y: 4, z: 8, core: 2. Of those that a mesh axis runs over, the one named last changes fastest.
Arguments:
- q_in: bfloat16 [4096, 8192], P('chan', 'seq'), may hold values from -6 to 6
- k_in: bfloat16 [4096, 8192], P('chan', 'seq'), may hold values from -6 to 6
- v_in: bfloat16 [4096, 8192], P('chan', 'seq'), may hold values from -6 to 6
- cotangent: bfloat16 [4096, 8192], P('chan', 'seq'), may hold values from -6 to 6
- taps_short: float32 [4096, 7], P('chan'), may hold values from -2 to 2
- residues: float32 [1024, 16], replicated, may hold values from -1.5 to 1.5
- rates: float32 [1024, 16], replicated, may hold values from 3.0517578e-05 to 0.03
Outputs:
- grad_q: bfloat16 [4096, 8192], P('chan', 'seq')
- grad_k: bfloat16 [4096, 8192], P('chan', 'seq')
- grad_v: bfloat16 [4096, 8192], P('chan', 'seq')
- grad_short: float32 [4096, 7], P('chan')
- grad_residues: float32 [1024, 16], replicated
The draws below stay inside these ranges and needn't reach their ends.
All inputs are finite; a program needn't handle non-finite values.
Results may differ from the reference program's by a relative error of at most 0.008.
Values may be sent and summed in bfloat16 or wider, within the bound.
No kernel may reach another device: no remote copies, remote signals or barrier semaphores. Data moves between devices by JAX's collectives and lax.ppermute only.
A program may use at most 128 MiB of HBM per device.

```python
import math
import jax
import jax.numpy as jnp
from jax import lax

CH_DEV = 1024
POLES = 16
SHORT_TAPS = 7
CHANNELS = 4096
GROUPS = 1024
SEQ = 8192
N_CHAN = 4


def level_of(key, extent, pieces, smallest, top_value):
    gain = 1.0
    for axis_at, blocks in pieces:
        heights = jax.random.uniform(jax.random.fold_in(jax.random.fold_in(key, 6), axis_at), (blocks,), jnp.float32, smallest / len(pieces), top_value / len(pieces))
        gain = gain * jnp.repeat(jnp.exp(heights), extent[axis_at] // blocks).reshape((-1,) + (1,) * (len(extent) - 1 - axis_at))
    return gain


def gaussian(rng, shape, width, limit, pieces=(), held_as=jnp.bfloat16):
    drawn = width * jax.random.normal(rng, shape, jnp.float32)
    if pieces:
        drawn = drawn * level_of(rng, shape, pieces, -0.22, 0.18)
    return jnp.clip(drawn, -limit, limit).astype(held_as)


def setup_inputs(seed: int = 0) -> dict:
    key_of = jax.random.split(jax.random.key(seed), 8)
    q_in = gaussian(key_of[0], (CHANNELS, SEQ), 1.0, 6.0, ((0, 4), (1, 64)))
    k_in = gaussian(key_of[1], (CHANNELS, SEQ), 1.0, 6.0, ((0, 4), (1, 64)))
    v_in = gaussian(key_of[2], (CHANNELS, SEQ), 1.0, 6.0, ((0, 4), (1, 64)))
    cotangent = gaussian(key_of[3], (CHANNELS, SEQ), 1.0, 6.0, ((0, 4), (1, 64)))
    taps_short = gaussian(key_of[4], (CHANNELS, SHORT_TAPS), SHORT_TAPS ** -0.5, 2.0, ((0, 4),), jnp.float32)
    residues = gaussian(key_of[5], (GROUPS, POLES), POLES ** -0.5, 1.5, (), jnp.float32)
    rates = jnp.clip(jnp.exp(jax.random.uniform(key_of[6], (GROUPS, POLES), jnp.float32, math.log(3.0517578125e-05), math.log(0.03))), 3.0517578125e-05, 0.03)
    return dict(q_in=q_in, k_in=k_in, v_in=v_in, cotangent=cotangent, taps_short=taps_short, residues=residues, rates=rates)


def delayed(signal, offset):
    padded = jnp.pad(signal, ((0, 0), (128, 0)))
    return lax.dynamic_slice_in_dim(padded, (128 - offset).astype(jnp.int32), signal.shape[1], 1)

def advanced(signal, offset):
    padded = jnp.pad(signal, ((0, 0), (0, 128)))
    return lax.dynamic_slice_in_dim(padded, offset.astype(jnp.int32), signal.shape[1], 1)

def long_channel(item):
    gated_row, grad_row, coef_row, rate_row = item
    step_axis = jnp.arange(SEQ).astype(jnp.float32)
    weight = jnp.sqrt(-jnp.expm1(-2.0 * rate_row))
    decay = jnp.exp(-rate_row[:, None] * step_axis[None, :])
    kernel = lax.optimization_barrier(jnp.sum((coef_row * weight)[:, None] * decay, axis=0))
    length = 2 * SEQ
    kernel_freq = jnp.fft.fft(kernel, n=length)
    gated_freq = jnp.fft.fft(gated_row, n=length)
    grad_freq = jnp.fft.fft(grad_row, n=length)
    long_out = jnp.real(jnp.fft.ifft(gated_freq * kernel_freq))[:SEQ].astype(jnp.float32)
    long_grad = jnp.real(jnp.fft.ifft(grad_freq * jnp.conj(kernel_freq)))[:SEQ].astype(jnp.float32)
    corr = jnp.real(jnp.fft.ifft(grad_freq * jnp.conj(gated_freq)))[:SEQ].astype(jnp.float32)
    pole_grad = weight * jnp.dot(decay, corr, precision=lax.Precision.HIGHEST)
    return (long_out, long_grad, pole_grad)

def reference(q_in, k_in, v_in, cotangent, taps_short, residues, rates):
    queries = q_in.astype(jnp.float32)
    key_data = k_in.astype(jnp.float32)
    value_data = v_in.astype(jnp.float32)
    grads_out = cotangent.astype(jnp.float32)
    gate = taps_short[:, 0:1] * delayed(key_data, jnp.int32(0))
    for offset in range(1, 7):
        gate = gate + taps_short[:, offset:offset + 1] * delayed(key_data, jnp.int32(offset))
    gated = gate * value_data
    grad_z = grads_out * queries
    coef_all = jnp.tile(residues, (N_CHAN, 1))
    rate_all = jnp.tile(rates, (N_CHAN, 1))
    long_out, long_grad, pole_grad = lax.map(long_channel, (gated, grad_z, coef_all, rate_all))
    scale_grad = SEQ ** (-0.5)
    grad_q = (grads_out * long_out).astype(jnp.bfloat16)
    grad_gated = long_grad
    grad_v = (grad_gated * gate).astype(jnp.bfloat16)
    grad_gate = grad_gated * value_data
    grad_k = taps_short[:, 0:1] * advanced(grad_gate, jnp.int32(0))
    for offset in range(1, 7):
        grad_k = grad_k + taps_short[:, offset:offset + 1] * advanced(grad_gate, jnp.int32(offset))
    grad_k = grad_k.astype(jnp.bfloat16)
    grad_short = jnp.stack([lax.optimization_barrier(jnp.sum(grad_gate * delayed(key_data, jnp.int32(offset)), axis=1)) for offset in range(7)], axis=1) * scale_grad
    grad_residues = lax.optimization_barrier(jnp.sum(pole_grad.reshape(N_CHAN, CH_DEV, POLES), axis=0)) * scale_grad
    return (grad_q, grad_k, grad_v, grad_short, grad_residues)
```

```python
import functools

import jax
import jax.numpy as jnp
from jax import lax
from jax.experimental import pallas as pl
from jax.experimental.pallas import tpu as pltpu
from jax.sharding import PartitionSpec as P

F32 = jnp.float32
BF16 = jnp.bfloat16
LANES = 128
SUB = 8
LEN = 128
POLES = 16
TAPS = 7
HALO = TAPS - 1
EDGE = 8
CARRY = 4 + TAPS
ROWS_OUT = 24
ROWS_BACK = 8
VMEM = 48 * 1024 * 1024


def one_minus_exp(x):
    series = 1.0 - x * (1.0 / 7.0)
    for order in (6.0, 5.0, 4.0, 3.0, 2.0):
        series = 1.0 - x * (1.0 / order) * series
    return x * series


def tile(index):
    if isinstance(index, int):
        return pl.ds(SUB * index, SUB)
    return pl.ds(pl.multiple_of(SUB * index, SUB), SUB)


def across(block):
    return pl.ds(block, LEN, stride=SUB)


def lane_group():
    return lax.broadcasted_iota(jnp.int32, (SUB, LANES), 1) // 16


def to_owner(x):
    y = pltpu.roll(x, 0, 1, stride=16, stride_axis=0)
    group = lane_group()
    for bit in (1, 2, 4):
        y = jnp.where((group & bit) != 0, pltpu.roll(y, SUB - bit, 0), y)
    return pltpu.roll(y, 0, 1, stride=16, stride_axis=0)


def skew_left(x):
    row = lax.broadcasted_iota(jnp.int32, (SUB, LANES), 0)
    for bit in (1, 2, 4):
        x = jnp.where((row & bit) != 0, pltpu.roll(x, LANES - 16 * bit, 1), x)
    return x


def from_owner(x):
    y = skew_left(x)
    group = lane_group()
    for bit in (1, 2, 4):
        y = jnp.where((group & bit) != 0, pltpu.roll(y, bit, 0), y)
    return skew_left(y)


def enter_kernel(q, k, v, cot, rates, residues, taps, kt, vt, zt, tail, head, par):
    for s in range(SUB):
        rows = slice(s * LANES, (s + 1) * LANES)
        kt[across(s), :] = k[rows, :].astype(F32).T
        vt[across(s), :] = v[rows, :].astype(F32).T
        zt[across(s), :] = (q[rows, :].astype(F32) * cot[rows, :].astype(F32)).T
        rate = rates[rows, :].T
        par[pl.ds(s, POLES, stride=SUB), :] = jnp.exp(-rate)
        par[pl.ds(SUB * POLES + s, POLES, stride=SUB), :] = residues[rows, :].T * jnp.sqrt(
            one_minus_exp(2.0 * rate)
        )
        par[pl.ds(2 * SUB * POLES + s, TAPS, stride=SUB), :] = taps[rows, :].T
    tail[...] = kt[SUB * (LEN - HALO) : SUB * LEN, :]
    head[0 : SUB * HALO, :] = zt[0 : SUB * HALO, :]
    head[SUB * HALO : 2 * SUB * HALO, :] = vt[0 : SUB * HALO, :]


def decay_of(par, r):
    return par[tile(r), :]


def coef_of(par, r):
    return par[tile(POLES + r), :]


def tap_of(par, j):
    return par[tile(2 * POLES + j), :]


def scan_down(par, z, gated, w, local, count, base, first, read, write, unroll):
    for pair in range(POLES // 2):
        modes = (2 * pair, 2 * pair + 1)
        decay = [decay_of(par, r) for r in modes]
        coef = [coef_of(par, r) for r in modes]
        final = pair == POLES // 2 - 1
        state = tuple(tuple(read(r, n) for n in range(CARRY)) for r in modes)
        sums = tuple(read(POLES, j) for j in range(TAPS)) if final else ()

        def step(i, carry, pair=pair, decay=decay, coef=coef, final=final):
            state, sums = carry
            t = count - 1 - i
            z_now = z[tile(t + base), :]
            g_now = gated[tile(t), :]
            w_now = [w[j, tile(t), :] for j in range(TAPS)]
            total = None if pair == 0 else local[tile(t), :]
            after = []
            for n in range(2):
                back, pole, ahead, power, *moments = state[n]
                back = back * decay[n] + z_now
                pole = pole + g_now * back
                ahead = ahead + power * g_now
                moments = [m + power * x for m, x in zip(moments, w_now)]
                power = power * decay[n]
                term = coef[n] * back
                total = term if total is None else total + term
                after.append((back, pole, ahead, power, *moments))
            local[tile(t), :] = total
            if final:
                sums = tuple(a + total * x for a, x in zip(sums, w_now))
            return tuple(after), sums

        state, sums = lax.fori_loop(0, count, step, (state, sums), unroll=unroll)
        for n, r in enumerate(modes):
            for m in range(CARRY):
                write(r, m, state[n][m])
        for j, value in enumerate(sums):
            write(POLES, j, value)


def inner_kernel(kt, vt, zt, par, gated, gate, local, carry, w):
    count = LEN - EDGE
    taps = [tap_of(par, j) for j in range(TAPS)]

    def prepare(i, before):
        keys = (kt[tile(i + EDGE), :], *before)
        now = taps[0] * keys[0]
        for j in range(1, TAPS):
            now = now + taps[j] * keys[j]
        value = vt[tile(i + EDGE), :]
        gate[tile(i), :] = now
        gated[tile(i), :] = now * value
        for j in range(TAPS):
            w[j, tile(i), :] = value * keys[j]
        return keys[:HALO]

    lax.fori_loop(0, count, prepare, tuple(kt[tile(EDGE - 1 - j), :] for j in range(HALO)), unroll=4)
    zero = jnp.zeros((SUB, LANES), F32)

    def read(r, n):
        return decay_of(par, r) if r < POLES and n == 3 else zero

    def write(r, n, value):
        carry[tile(r * CARRY + n), :] = value

    scan_down(par, zt, gated, w, local, count, EDGE, True, read, write, 4)


def edge_kernel(kt, tail, vt, zt, par, carry, gated, gate, local, out, w, gather, spread):
    keys = [tail[tile(n), :] for n in range(HALO)] + [kt[tile(n), :] for n in range(EDGE)]
    taps = [tap_of(par, j) for j in range(TAPS)]
    for t in range(EDGE):
        now = taps[0] * keys[t + HALO]
        for j in range(1, TAPS):
            now = now + taps[j] * keys[t + HALO - j]
        value = vt[tile(t), :]
        gate[tile(t), :] = now
        gated[tile(t), :] = now * value
        for j in range(TAPS):
            w[j, tile(t), :] = value * keys[t + HALO - j]

    def read(r, n):
        return carry[tile(r * CARRY + n), :]

    def write(r, n, value):
        if r == POLES:
            row, slot = 6, n
        elif n == 3:
            return
        else:
            half, slot = divmod(r, SUB)
            row = {2: 0, 0: 2, 1: 4}.get(n, 8 + 2 * (n - 4)) + half
        gather[tile(row * SUB + slot), :] = value

    scan_down(par, zt, gated, w, local, EDGE, 0, False, read, write, EDGE)
    zero = jnp.zeros((SUB, LANES), F32)
    gather[tile(6 * SUB + TAPS), :] = zero
    for row in range(ROWS_OUT):
        for s in range(SUB):
            if row in (7, 22, 23):
                block = zero
            else:
                block = to_owner(gather[pl.ds(row * SUB * SUB + s, SUB, stride=SUB), :])
            spread[pl.ds(s * SUB * ROWS_OUT + row, SUB, stride=ROWS_OUT), :] = block
    out[...] = spread[...].astype(BF16)


def owner_kernel(count, scale, arrived, mine, out, x, y):
    x[...] = arrived[...].astype(F32)
    even = lax.broadcasted_iota(jnp.int32, (SUB, LANES), 0) % 2 == 0

    def pattern(ref, row):
        return jnp.where(even, ref[pl.ds(row, 1), :], ref[pl.ds(row + 1, 1), :])

    rate = pattern(mine, 0)
    weight = jnp.sqrt(one_minus_exp(2.0 * rate))
    coef = pattern(mine, 2) * weight
    leap = jnp.exp(-float(LEN) * rate)
    zero = jnp.zeros((SUB, LANES), F32)
    ahead, pole, total = zero, zero, zero
    for d in range(count):
        y[pl.ds(d * ROWS_BACK, 2), :] = ahead[0:2, :]
        now = x[pl.ds(d * ROWS_OUT, SUB), :]
        pole = pole + ahead * pattern(x, d * ROWS_OUT + 2)
        total = total + now
        ahead = ahead * leap + now
    back, low, high = zero, zero, zero
    for d in reversed(range(count)):
        y[pl.ds(d * ROWS_BACK + 2, 2), :] = back[0:2, :]
        low = low + back * x[pl.ds(d * ROWS_OUT + SUB, SUB), :]
        high = high + back * x[pl.ds(d * ROWS_OUT + 2 * SUB, SUB), :]
        back = back * leap + pattern(x, d * ROWS_OUT + 2)
    poles = (pole[0:2, :] + total[4:6, :]) * weight[0:2, :] * scale
    group = lane_group()[0:1, :]
    short = total[6:7, :]
    for part, first in ((low * coef, 0), (high * coef, 4)):
        part = part + pltpu.roll(part, SUB - 1, 0)
        for shift in (16, 32, 64):
            part = part + pltpu.roll(part, shift, 1)
        for n in range(min(4, TAPS - first)):
            short = short + jnp.where(group == first + n, part[2 * n : 2 * n + 1, :], 0.0)
    short = short * scale
    coarse = short.astype(BF16).astype(F32)
    fine = short - coarse
    for d in range(count):
        y[pl.ds(d * ROWS_BACK + 4, 2), :] = poles
        y[pl.ds(d * ROWS_BACK + 6, 1), :] = coarse
        y[pl.ds(d * ROWS_BACK + 7, 1), :] = fine
    out[...] = y[...].astype(BF16)


def leave_kernel(
    arrived, gated_a, gated_b, gate_a, gate_b, local_a, local_b, vt, head, par, cot,
    grad_q, grad_k, grad_v, grad_short, x, state, long_out, slope, vals,
):
    x[...] = arrived[...].astype(F32)
    for s in range(SUB):
        for row in range(4):
            block = x[pl.ds(s * SUB * ROWS_BACK + row, SUB, stride=ROWS_BACK), :]
            state[pl.ds(row * SUB * SUB + s, SUB, stride=SUB), :] = from_owner(block)
        coarse = x[pl.ds(s * SUB * ROWS_BACK + 6, SUB, stride=ROWS_BACK), :]
        fine = x[pl.ds(s * SUB * ROWS_BACK + 7, SUB, stride=ROWS_BACK), :]
        grad_short[s * LANES : (s + 1) * LANES, :] = from_owner(coarse + fine)[0:TAPS, :].T

    half = POLES // 2
    for part in range(2):
        modes = range(part * half, (part + 1) * half)
        decay = [decay_of(par, r) for r in modes]
        coef = [coef_of(par, r) for r in modes]
        ahead = tuple(state[tile(r), :] for r in modes)

        def forward(i, ahead, source, base, part=part, decay=decay, coef=coef):
            now = source[tile(i), :]
            total = None if part == 0 else long_out[tile(i + base), :]
            after = []
            for h, d, c in zip(ahead, decay, coef):
                h = h + now
                term = c * h
                total = term if total is None else total + term
                after.append(h * d)
            long_out[tile(i + base), :] = total
            return tuple(after)

        ahead = lax.fori_loop(
            0, EDGE, functools.partial(forward, source=gated_b, base=0), ahead, unroll=EDGE
        )
        lax.fori_loop(
            0, LEN - EDGE, functools.partial(forward, source=gated_a, base=EDGE), ahead, unroll=4
        )

    decay = [decay_of(par, r) for r in range(POLES)]
    back = [state[tile(POLES + r), :] for r in range(POLES)]
    for n in range(HALO):
        total = coef_of(par, 0) * back[0]
        for r in range(1, POLES):
            total = total + coef_of(par, r) * back[r]
        slope[tile(LEN + n), :] = total * head[tile(HALO + n), :]
        if n < HALO - 1:
            z_now = head[tile(n), :]
            back = [(b - z_now) / d for b, d in zip(back, decay)]

    def backward(i, terms, local, gate, count, base):
        t = count - 1 - i
        terms = tuple(q * d for q, d in zip(terms, decay))
        total = local[tile(t), :]
        sums = list(terms)
        while len(sums) > 1:
            sums = [a + b for a, b in zip(sums[0::2], sums[1::2])]
        total = total + sums[0]
        slope[tile(t + base), :] = total * vt[tile(t + base), :]
        vals[tile(t + base), :] = total * gate[tile(t), :]
        return terms

    terms = tuple(coef_of(par, r) * state[tile(POLES + r), :] for r in range(POLES))
    terms = lax.fori_loop(
        0, LEN - EDGE,
        functools.partial(backward, local=local_a, gate=gate_a, count=LEN - EDGE, base=EDGE),
        terms, unroll=4,
    )
    lax.fori_loop(
        0, EDGE,
        functools.partial(backward, local=local_b, gate=gate_b, count=EDGE, base=0),
        terms, unroll=EDGE,
    )

    taps = [tap_of(par, j) for j in range(TAPS)]

    def spread_taps(i, after):
        t = LEN - 1 - i
        slopes = (slope[tile(t), :], *after)
        total = taps[0] * slopes[0]
        for j in range(1, TAPS):
            total = total + taps[j] * slopes[j]
        slope[tile(t), :] = total
        return slopes[:HALO]

    lax.fori_loop(
        0, LEN, spread_taps, tuple(slope[tile(LEN + n), :] for n in range(HALO)), unroll=4
    )
    for s in range(SUB):
        rows = slice(s * LANES, (s + 1) * LANES)
        grad_q[rows, :] = (cot[rows, :].astype(F32) * long_out[across(s), :].T).astype(BF16)
        grad_k[rows, :] = slope[across(s), :].T.astype(BF16)
        grad_v[rows, :] = vals[across(s), :].T.astype(BF16)


def pole_kernel(a, b, c, d, out, x, y):
    x[...] = (a[...].astype(F32) + b[...].astype(F32)) + (c[...].astype(F32) + d[...].astype(F32))
    for s in range(SUB):
        for half in range(2):
            block = x[pl.ds(s * SUB * 2 + half, SUB, stride=2), :]
            y[half * SUB : (half + 1) * SUB, :] = from_owner(block)
        out[s * LANES : (s + 1) * LANES, :] = y[...].T


def call(kernel, name, outs, scratch, operands, in_specs=None, flops=0, moved=0):
    return pl.pallas_call(
        kernel,
        grid=(1,) if in_specs else (),
        out_shape=outs,
        in_specs=in_specs or [pl.BlockSpec(memory_space=pltpu.VMEM)] * len(operands),
        out_specs=[pl.BlockSpec(memory_space=pltpu.VMEM)] * len(outs),
        scratch_shapes=scratch,
        compiler_params=pltpu.CompilerParams(vmem_limit_bytes=VMEM),
        cost_estimate=pl.CostEstimate(flops=flops, bytes_accessed=moved, transcendentals=0),
        name=name,
    )(*operands)


def shape(rows, dtype=F32, lanes=LANES):
    return jax.ShapeDtypeStruct((rows, lanes), dtype)


def per_device(q_in, k_in, v_in, cotangent, taps_short, residues, rates):
    channels, length = q_in.shape
    count = lax.axis_size("seq")
    index = lax.axis_index("seq")
    chans = lax.axis_size("chan")
    assert (channels, length, count) == (SUB * LANES, LEN, SUB * SUB)
    scale = (length * count) ** (-0.5)
    full, edge = SUB * LEN, SUB * EDGE
    inner = full - edge
    tile_bytes = SUB * LANES * 4

    kt, vt, zt, tail, head, par = call(
        enter_kernel,
        "enter",
        [shape(full)] * 3 + [shape(SUB * HALO), shape(2 * SUB * HALO), shape(SUB * 40)],
        [],
        (q_in, k_in, v_in, cotangent, rates, residues, taps_short),
        flops=4 * 10**6,
        moved=3 * 10**6,
    )
    tail = lax.ppermute(tail, "seq", [(i, i + 1) for i in range(count - 1)])
    head = lax.ppermute(head, "seq", [(i + 1, i) for i in range(count - 1)])

    gated_a, gate_a, local_a, carry = call(
        inner_kernel,
        "inner",
        [shape(inner)] * 3 + [shape(SUB * (POLES * CARRY + TAPS))],
        [pltpu.VMEM((TAPS, inner, LANES), F32)],
        (kt, vt, zt, par),
        flops=48 * 10**6,
        moved=4 * 10**6,
    )
    first = pl.BlockSpec((edge, LANES), lambda i: (0, 0), memory_space=pltpu.VMEM)
    whole = pl.BlockSpec(memory_space=pltpu.VMEM)
    gated_b, gate_b, local_b, message = call(
        edge_kernel,
        "edge",
        [shape(edge)] * 3 + [shape(count * ROWS_OUT, BF16)],
        [
            pltpu.VMEM((TAPS, edge, LANES), F32),
            pltpu.VMEM((SUB * SUB * ROWS_OUT, LANES), F32),
            pltpu.VMEM((count * ROWS_OUT, LANES), F32),
        ],
        (kt, tail, vt, zt, par, carry),
        [first, whole, first, first, whole, whole],
        flops=6 * 10**6,
        moved=2 * 10**6,
    )

    def exchange(x, rows):
        x = x.reshape(count, rows, LANES)
        return lax.all_to_all(x, "seq", split_axis=0, concat_axis=0, tiled=True)

    arrived = exchange(message, ROWS_OUT).reshape(count * ROWS_OUT, LANES)
    start = (index // SUB) * LANES + ((SUB - index % SUB) % SUB) * 16
    mine = jnp.concatenate(
        [
            lax.dynamic_slice(a, (start, 0), (16, POLES)).T.reshape(2, LANES)
            for a in (rates, residues)
        ]
    )
    (back,) = call(
        functools.partial(owner_kernel, count, scale),
        "owner",
        [shape(count * ROWS_BACK, BF16)],
        [pltpu.VMEM((count * ROWS_OUT, LANES), F32), pltpu.VMEM((count * ROWS_BACK, LANES), F32)],
        (arrived, mine),
        flops=2 * 10**6,
        moved=10**6,
    )
    returned = exchange(back, ROWS_BACK)
    poles = returned[:, 4:6, :].reshape(2 * count, LANES)
    others = [
        lax.ppermute(poles, "chan", [(i, (i + n) % chans) for i in range(chans)])
        for n in range(1, chans)
    ]
    grad_q, grad_k, grad_v, grad_short = call(
        leave_kernel,
        "leave",
        [shape(channels, BF16)] * 3 + [shape(channels, F32, TAPS)],
        [
            pltpu.VMEM((count * ROWS_BACK, LANES), F32),
            pltpu.VMEM((SUB * 2 * POLES, LANES), F32),
            pltpu.VMEM((full, LANES), F32),
            pltpu.VMEM((full + SUB * HALO, LANES), F32),
            pltpu.VMEM((full, LANES), F32),
        ],
        (
            returned.reshape(count * ROWS_BACK, LANES),
            gated_a, gated_b, gate_a, gate_b, local_a, local_b, vt, head, par, cotangent,
        ),
        flops=16 * 10**6,
        moved=3 * 10**6,
    )
    (grad_residues,) = call(
        pole_kernel,
        "poles",
        [shape(channels, F32, POLES)],
        [pltpu.VMEM((2 * count, LANES), F32), pltpu.VMEM((POLES, LANES), F32)],
        (poles, *others),
        flops=10**5,
        moved=10**5,
    )
    return grad_q, grad_k, grad_v, grad_short, grad_residues


def solution(mesh):
    streams = P("chan", "seq")
    return jax.shard_map(
        per_device,
        mesh=mesh,
        in_specs=(streams,) * 4 + (P("chan", None), P(), P()),
        out_specs=(streams,) * 3 + (P("chan", None), P()),
        check_vma=False,
    )
```

```python
import functools

import jax
import jax.numpy as jnp
from jax import lax
from jax.experimental import pallas as pl
from jax.experimental.pallas import tpu as pltpu
from jax.sharding import PartitionSpec as P

F32 = jnp.float32
BF16 = jnp.bfloat16
LANES = 128
SUB = 8
LEN = 128
POLES = 16
TAPS = 7
HALO = TAPS - 1
EDGE = 8
CARRY = 4 + TAPS
ROWS_OUT = 22
ROWS_BACK = 8
VMEM = 48 * 1024 * 1024


def one_minus_exp(x):
    series = 1.0 - x * (1.0 / 7.0)
    for order in (6.0, 5.0, 4.0, 3.0, 2.0):
        series = 1.0 - x * (1.0 / order) * series
    return x * series


def tile(index):
    if isinstance(index, int):
        return pl.ds(SUB * index, SUB)
    return pl.ds(pl.multiple_of(SUB * index, SUB), SUB)


def across(block):
    return pl.ds(block, LEN, stride=SUB)


def lane_group():
    return lax.broadcasted_iota(jnp.int32, (SUB, LANES), 1) // 16


def to_owner(x):
    y = pltpu.roll(x, 0, 1, stride=16, stride_axis=0)
    group = lane_group()
    for bit in (1, 2, 4):
        y = jnp.where((group & bit) != 0, pltpu.roll(y, SUB - bit, 0), y)
    return pltpu.roll(y, 0, 1, stride=16, stride_axis=0)


def skew_left(x):
    row = lax.broadcasted_iota(jnp.int32, (SUB, LANES), 0)
    for bit in (1, 2, 4):
        x = jnp.where((row & bit) != 0, pltpu.roll(x, LANES - 16 * bit, 1), x)
    return x


def from_owner(x):
    y = skew_left(x)
    group = lane_group()
    for bit in (1, 2, 4):
        y = jnp.where((group & bit) != 0, pltpu.roll(y, bit, 0), y)
    return skew_left(y)


def decay_of(par, r):
    return par[tile(r), :]


def coef_of(par, r):
    return par[tile(POLES + r), :]


def tap_of(par, j):
    return par[tile(2 * POLES + j), :]


def scan_down(par, z, gated, w, local, count, base, first, read, write, unroll):
    for pair in range(POLES // 2):
        modes = (2 * pair, 2 * pair + 1)
        decay = [decay_of(par, r) for r in modes]
        coef = [coef_of(par, r) for r in modes]
        final = pair == POLES // 2 - 1
        state = tuple(tuple(read(r, n) for n in range(CARRY)) for r in modes)
        sums = tuple(read(POLES, j) for j in range(TAPS)) if final else ()

        def step(i, carry, pair=pair, decay=decay, coef=coef, final=final):
            state, sums = carry
            t = count - 1 - i
            z_now = z[tile(t + base), :]
            g_now = gated[tile(t), :]
            w_now = [w[j, tile(t), :] for j in range(TAPS)]
            total = None if pair == 0 else local[tile(t), :]
            after = []
            for n in range(2):
                back, pole, ahead, power, *moments = state[n]
                back = back * decay[n] + z_now
                pole = pole + g_now * back
                ahead = ahead + power * g_now
                moments = [m + power * x for m, x in zip(moments, w_now)]
                power = power * decay[n]
                term = coef[n] * back
                total = term if total is None else total + term
                after.append((back, pole, ahead, power, *moments))
            local[tile(t), :] = total
            if final:
                sums = tuple(a + total * x for a, x in zip(sums, w_now))
            return tuple(after), sums

        state, sums = lax.fori_loop(0, count, step, (state, sums), unroll=unroll)
        for n, r in enumerate(modes):
            for m in range(CARRY):
                write(r, m, state[n][m])
        for j, value in enumerate(sums):
            write(POLES, j, value)


def inner_kernel(
    small, k, v, z, vt, edge, par, gated, gate, local, carry, kt, zt, w
):
    for s in range(SUB):
        rows = slice(s * LANES, (s + 1) * LANES)
        kt[across(s), :] = k[rows, :].astype(F32).T
        vt[across(s), :] = v[rows, :].astype(F32).T
        zt[across(s), :] = z[rows, :].T
        rate = small[0:POLES, rows]
        par[pl.ds(s, POLES, stride=SUB), :] = jnp.exp(-rate)
        par[pl.ds(SUB * POLES + s, POLES, stride=SUB), :] = small[
            POLES : 2 * POLES, rows
        ] * jnp.sqrt(
            one_minus_exp(2.0 * rate)
        )
        par[pl.ds(2 * SUB * POLES + s, TAPS, stride=SUB), :] = small[
            2 * POLES : 2 * POLES + TAPS, rows
        ]
    for n, ref in enumerate((kt, zt, vt)):
        edge[n * SUB * EDGE : (n + 1) * SUB * EDGE, :] = ref[0 : SUB * EDGE, :]
    count = LEN - EDGE
    taps = [tap_of(par, j) for j in range(TAPS)]

    def prepare(i, before):
        keys = (kt[tile(i + EDGE), :], *before)
        now = taps[0] * keys[0]
        for j in range(1, TAPS):
            now = now + taps[j] * keys[j]
        value = vt[tile(i + EDGE), :]
        gate[tile(i), :] = now
        gated[tile(i), :] = now * value
        for j in range(TAPS):
            w[j, tile(i), :] = value * keys[j]
        return keys[:HALO]

    lax.fori_loop(0, count, prepare, tuple(kt[tile(EDGE - 1 - j), :] for j in range(HALO)), unroll=4)
    zero = jnp.zeros((SUB, LANES), F32)

    def read(r, n):
        return decay_of(par, r) if r < POLES and n == 3 else zero

    def write(r, n, value):
        carry[tile(r * CARRY + n), :] = value

    scan_down(par, zt, gated, w, local, count, EDGE, True, read, write, 4)


def edge_kernel(edge, tail, par, carry, gated, gate, local, out, w, gather, spread, held):
    held[...] = tail[...].astype(F32)
    rows = SUB * EDGE
    kt, zt, vt = (edge.at[pl.ds(n * rows, rows), :] for n in range(3))
    keys = [held[tile(n), :] for n in range(HALO)] + [kt[tile(n), :] for n in range(EDGE)]
    taps = [tap_of(par, j) for j in range(TAPS)]
    for t in range(EDGE):
        now = taps[0] * keys[t + HALO]
        for j in range(1, TAPS):
            now = now + taps[j] * keys[t + HALO - j]
        value = vt[tile(t), :]
        gate[tile(t), :] = now
        gated[tile(t), :] = now * value
        for j in range(TAPS):
            w[j, tile(t), :] = value * keys[t + HALO - j]

    def read(r, n):
        return carry[tile(r * CARRY + n), :]

    def write(r, n, value):
        if r == POLES:
            row, slot = 20, n
        elif n == 3:
            return
        else:
            half, slot = divmod(r, SUB)
            row = {2: 0, 0: 2, 1: 4}.get(n, 6 + 2 * (n - 4)) + half
        gather[tile(row * SUB + slot), :] = value

    scan_down(par, zt, gated, w, local, EDGE, 0, False, read, write, EDGE)
    zero = jnp.zeros((SUB, LANES), F32)
    gather[tile(20 * SUB + TAPS), :] = zero
    for row in range(ROWS_OUT):
        for s in range(SUB):
            if row == ROWS_OUT - 1:
                block = zero
            else:
                block = to_owner(gather[pl.ds(row * SUB * SUB + s, SUB, stride=SUB), :])
            spread[pl.ds(s * SUB * ROWS_OUT + row, SUB, stride=ROWS_OUT), :] = block
    out[...] = spread[...].astype(BF16)


def owner_kernel(count, scale, arrived, mine, out, x, y):
    x[...] = arrived[...].astype(F32)
    even = lax.broadcasted_iota(jnp.int32, (SUB, LANES), 0) % 2 == 0

    def pattern(ref, row):
        return jnp.where(even, ref[pl.ds(row, 1), :], ref[pl.ds(row + 1, 1), :])

    rate = pattern(mine, 0)
    weight = jnp.sqrt(one_minus_exp(2.0 * rate))
    coef = pattern(mine, 2) * weight
    leap = jnp.exp(-float(LEN) * rate)
    zero = jnp.zeros((SUB, LANES), F32)
    ahead, pole, total, taps = zero, zero, zero, zero
    for d in range(count):
        y[pl.ds(d * ROWS_BACK, 2), :] = ahead[0:2, :]
        now = x[pl.ds(d * ROWS_OUT, SUB), :]
        pole = pole + ahead * pattern(x, d * ROWS_OUT + 2)
        total = total + now
        ahead = ahead * leap + now
    back, low, high = zero, zero, zero
    for d in reversed(range(count)):
        y[pl.ds(d * ROWS_BACK + 2, 2), :] = back[0:2, :]
        low = low + back * x[pl.ds(d * ROWS_OUT + 6, SUB), :]
        last = x[pl.ds(d * ROWS_OUT + 14, SUB), :]
        high = high + back * last
        taps = taps + last
        back = back * leap + pattern(x, d * ROWS_OUT + 2)
    poles = (pole[0:2, :] + total[4:6, :]) * weight[0:2, :] * scale
    group = lane_group()[0:1, :]
    short = taps[6:7, :]
    for part, first in ((low * coef, 0), (high * coef, 4)):
        part = part + pltpu.roll(part, SUB - 1, 0)
        for shift in (16, 32, 64):
            part = part + pltpu.roll(part, shift, 1)
        for n in range(min(4, TAPS - first)):
            short = short + jnp.where(group == first + n, part[2 * n : 2 * n + 1, :], 0.0)
    short = short * scale
    coarse = short.astype(BF16).astype(F32)
    fine = short - coarse
    for d in range(count):
        y[pl.ds(d * ROWS_BACK + 4, 2), :] = poles
        y[pl.ds(d * ROWS_BACK + 6, 1), :] = coarse
        y[pl.ds(d * ROWS_BACK + 7, 1), :] = fine
    out[...] = y[...].astype(BF16)


def forward_kernel(gated_a, gated_b, par, own_out):
    half = POLES // 2
    for part in range(2):
        modes = range(part * half, (part + 1) * half)
        decay = [decay_of(par, r) for r in modes]
        coef = [coef_of(par, r) for r in modes]
        ahead = (jnp.zeros((SUB, LANES), F32),) * half

        def forward(i, ahead, source, base, part=part, decay=decay, coef=coef):
            now = source[tile(i), :]
            total = None if part == 0 else own_out[tile(i + base), :]
            after = []
            for h, d, c in zip(ahead, decay, coef):
                h = h + now
                term = c * h
                total = term if total is None else total + term
                after.append(h * d)
            own_out[tile(i + base), :] = total
            return tuple(after)

        ahead = lax.fori_loop(
            0, EDGE, functools.partial(forward, source=gated_b, base=0), ahead, unroll=EDGE
        )
        lax.fori_loop(
            0, LEN - EDGE, functools.partial(forward, source=gated_a, base=EDGE), ahead, unroll=4
        )


def add_up(terms):
    terms = list(terms)
    while len(terms) > 1:
        terms = [a + b for a, b in zip(terms[0::2], terms[1::2])]
    return terms[0]


def unpack(arrived, x, state, first):
    x[...] = arrived[...].astype(F32)
    for s in range(SUB):
        for row in range(2):
            block = x[pl.ds(s * SUB * ROWS_BACK + first + row, SUB, stride=ROWS_BACK), :]
            state[pl.ds(row * SUB * SUB + s, SUB, stride=SUB), :] = from_owner(block)


def query_kernel(arrived, own_out, par, cot, grad_q, grad_short, x, state, long_out):
    unpack(arrived, x, state, 0)
    for s in range(SUB):
        coarse = x[pl.ds(s * SUB * ROWS_BACK + 6, SUB, stride=ROWS_BACK), :]
        fine = x[pl.ds(s * SUB * ROWS_BACK + 7, SUB, stride=ROWS_BACK), :]
        grad_short[:, s * LANES : (s + 1) * LANES] = from_owner(coarse + fine)[0:TAPS, :]
    decay = [decay_of(par, r) for r in range(POLES)]

    def forward(t, terms):
        long_out[tile(t), :] = own_out[tile(t), :] + add_up(terms)
        return tuple(q * d for q, d in zip(terms, decay))

    terms = tuple(coef_of(par, r) * state[tile(r), :] for r in range(POLES))
    lax.fori_loop(0, LEN, forward, terms, unroll=4)
    for s in range(SUB):
        rows = slice(s * LANES, (s + 1) * LANES)
        grad_q[rows, :] = (cot[rows, :].astype(F32) * long_out[across(s), :].T).astype(BF16)


def key_kernel(
    arrived, gate_a, gate_b, local_a, local_b, vt, head, par, grad_k, grad_v, x, state, slope, vals
):
    unpack(arrived, x, state, 2)
    decay = [decay_of(par, r) for r in range(POLES)]
    back = [state[tile(r), :] for r in range(POLES)]
    growth = [1.0 / d for d in decay]
    ahead = []
    for n in range(HALO):
        ahead.append(
            add_up(coef_of(par, r) * back[r] for r in range(POLES)) * head[tile(EDGE + n), :]
        )
        if n < HALO - 1:
            z_now = head[tile(n), :]
            back = [(b - z_now) * g for b, g in zip(back, growth)]
    taps = [tap_of(par, j) for j in range(TAPS)]

    def backward(i, carry, local, gate, count, base):
        terms, ahead = carry
        t = count - 1 - i
        terms = tuple(q * d for q, d in zip(terms, decay))
        total = local[tile(t), :] + add_up(terms)
        vals[tile(t + base), :] = total * gate[tile(t), :]
        slopes = (total * vt[tile(t + base), :], *ahead)
        slope[tile(t + base), :] = functools.reduce(
            lambda a, b: a + b, [taps[j] * slopes[j] for j in range(TAPS)]
        )
        return terms, slopes[:HALO]

    terms = tuple(coef_of(par, r) * state[tile(r), :] for r in range(POLES))
    carry = (terms, tuple(ahead))
    carry = lax.fori_loop(
        0, LEN - EDGE,
        functools.partial(backward, local=local_a, gate=gate_a, count=LEN - EDGE, base=EDGE),
        carry, unroll=4,
    )
    lax.fori_loop(
        0, EDGE,
        functools.partial(backward, local=local_b, gate=gate_b, count=EDGE, base=0),
        carry, unroll=EDGE,
    )
    for s in range(SUB):
        rows = slice(s * LANES, (s + 1) * LANES)
        grad_k[rows, :] = slope[across(s), :].T.astype(BF16)
        grad_v[rows, :] = vals[across(s), :].T.astype(BF16)


def pole_kernel(near, far, out, x):
    x[...] = near[...].astype(F32) + far[...].astype(F32)
    for s in range(SUB):
        for half in range(2):
            block = x[pl.ds(s * SUB * 2 + half, SUB, stride=2), :]
            out[half * SUB : (half + 1) * SUB, s * LANES : (s + 1) * LANES] = from_owner(block)


def call(kernel, name, outs, scratch, operands, in_specs=None, flops=0, moved=0):
    return pl.pallas_call(
        kernel,
        grid=(1,) if in_specs else (),
        out_shape=outs,
        in_specs=in_specs or [pl.BlockSpec(memory_space=pltpu.VMEM)] * len(operands),
        out_specs=[pl.BlockSpec(memory_space=pltpu.VMEM)] * len(outs),
        scratch_shapes=scratch,
        compiler_params=pltpu.CompilerParams(vmem_limit_bytes=VMEM),
        cost_estimate=pl.CostEstimate(flops=flops, bytes_accessed=moved, transcendentals=0),
        name=name,
    )(*operands)


def shape(rows, dtype=F32, lanes=LANES):
    return jax.ShapeDtypeStruct((rows, lanes), dtype)


def per_device(q_in, k_in, v_in, cotangent, taps_short, residues, rates):
    channels, length = q_in.shape
    count = lax.axis_size("seq")
    index = lax.axis_index("seq")
    chans = lax.axis_size("chan")
    assert (channels, length, count) == (SUB * LANES, LEN, SUB * SUB)
    scale = (length * count) ** (-0.5)
    full, edge = SUB * LEN, SUB * EDGE
    inner = full - edge

    tail = k_in[:, length - HALO :].T.reshape(SUB * HALO, LANES)
    tail = lax.ppermute(tail, "seq", [(i, i + 1) for i in range(count - 1)])
    grad_z = q_in.astype(F32) * cotangent.astype(F32)
    small = jnp.concatenate([rates.T, residues.T, taps_short.T])
    vt, ends, par, gated_a, gate_a, local_a, carry = call(
        inner_kernel,
        "inner",
        [shape(full), shape(3 * edge), shape(SUB * 40)]
        + [shape(inner)] * 3
        + [shape(SUB * (POLES * CARRY + TAPS))],
        [
            pltpu.VMEM((full, LANES), F32),
            pltpu.VMEM((full, LANES), F32),
            pltpu.VMEM((TAPS, inner, LANES), F32),
        ],
        (small, k_in, v_in, grad_z),
        flops=48 * 10**6,
        moved=4 * 10**6,
    )
    head = lax.ppermute(ends[edge:], "seq", [(i + 1, i) for i in range(count - 1)])
    gated_b, gate_b, local_b, message = call(
        edge_kernel,
        "edge",
        [shape(edge)] * 3 + [shape(count * ROWS_OUT, BF16)],
        [
            pltpu.VMEM((TAPS, edge, LANES), F32),
            pltpu.VMEM((SUB * SUB * ROWS_OUT, LANES), F32),
            pltpu.VMEM((count * ROWS_OUT, LANES), F32),
            pltpu.VMEM((SUB * HALO, LANES), F32),
        ],
        (ends, tail, par, carry),
        flops=6 * 10**6,
        moved=2 * 10**6,
    )

    def exchange(x, rows):
        x = x.reshape(count, rows // 2, 2, LANES)
        return lax.all_to_all(x, "seq", split_axis=0, concat_axis=0, tiled=True)

    arrived = exchange(message, ROWS_OUT).reshape(count * ROWS_OUT, LANES)
    (own_out,) = call(
        forward_kernel,
        "forward",
        [shape(full)],
        [],
        (gated_a, gated_b, par),
        flops=10 * 10**6,
        moved=10**6,
    )
    start = (index // SUB) * LANES + ((SUB - index % SUB) % SUB) * 16
    mine = jnp.concatenate(
        [
            lax.dynamic_slice(a.T, (0, start), (POLES, 16)).reshape(2, LANES)
            for a in (rates, residues)
        ]
    )
    arrived, own_out, head, mine = lax.optimization_barrier((arrived, own_out, head, mine))
    (back,) = call(
        functools.partial(owner_kernel, count, scale),
        "owner",
        [shape(count * ROWS_BACK, BF16)],
        [pltpu.VMEM((count * ROWS_OUT, LANES), F32), pltpu.VMEM((count * ROWS_BACK, LANES), F32)],
        (arrived, mine),
        flops=2 * 10**6,
        moved=10**6,
    )
    returned = exchange(back, ROWS_BACK)
    poles = returned[:, 2].reshape(2 * count, LANES)
    returned = returned.reshape(count * ROWS_BACK, LANES)

    def other(x, bit):
        return lax.ppermute(x, "chan", [(i, i ^ bit) for i in range(chans)])

    swap = [
        pltpu.VMEM((count * ROWS_BACK, LANES), F32),
        pltpu.VMEM((SUB * POLES, LANES), F32),
    ]
    poles_near = other(poles, 1)
    grad_q, grad_short = call(
        query_kernel,
        "query",
        [shape(channels, BF16), shape(TAPS, F32, channels)],
        [*swap, pltpu.VMEM((full, LANES), F32)],
        (returned, own_out, par, cotangent),
        flops=5 * 10**6,
        moved=10**6,
    )
    poles_near, grad_q = lax.optimization_barrier((poles_near, grad_q))
    poles = (poles.astype(F32) + poles_near.astype(F32)).astype(BF16)
    poles_far = other(poles, 2)
    grad_k, grad_v = call(
        key_kernel,
        "key",
        [shape(channels, BF16)] * 2,
        [*swap, pltpu.VMEM((full, LANES), F32), pltpu.VMEM((full, LANES), F32)],
        (returned, gate_a, gate_b, local_a, local_b, vt, head, par),
        flops=8 * 10**6,
        moved=2 * 10**6,
    )
    (grad_residues,) = call(
        pole_kernel,
        "poles",
        [shape(POLES, F32, channels)],
        [pltpu.VMEM((2 * count, LANES), F32)],
        (poles, poles_far),
        flops=10**5,
        moved=10**5,
    )
    return grad_q, grad_k, grad_v, grad_short.T, grad_residues.T


def solution(mesh):
    streams = P("chan", "seq")
    return jax.shard_map(
        per_device,
        mesh=mesh,
        in_specs=(streams,) * 4 + (P("chan", None), P(), P()),
        out_specs=(streams,) * 3 + (P("chan", None), P()),
        check_vma=False,
    )
```

```python
import functools

import jax
import jax.numpy as jnp
from jax import lax
from jax.experimental import pallas as pl
from jax.experimental.pallas import tpu as pltpu
from jax.sharding import PartitionSpec as P

F32 = jnp.float32
BF16 = jnp.bfloat16
LANES = 128
SUB = 8
LEN = 128
POLES = 16
TAPS = 7
HALO = TAPS - 1
EDGE = 8
MODE = 4 + TAPS
ROWS_OUT = 24
ROW_SHORT, ROW_V, ROW_MOMENT, ROW_K, ROW_Z = 6, 7, 8, 22, 23
ROWS_BACK = 8
VMEM = 48 * 1024 * 1024
VMEM_FIRST = 62 * 1024 * 1024


def one_minus_exp(x):
    series = 1.0 - x * (1.0 / 7.0)
    for order in (6.0, 5.0, 4.0, 3.0, 2.0):
        series = 1.0 - x * (1.0 / order) * series
    return x * series


def tile(index):
    if isinstance(index, int):
        return pl.ds(SUB * index, SUB)
    return pl.ds(pl.multiple_of(SUB * index, SUB), SUB)


def across(block):
    return pl.ds(block, LEN, stride=SUB)


def lane_group():
    return lax.broadcasted_iota(jnp.int32, (SUB, LANES), 1) // 16


def to_owner(x):
    y = pltpu.roll(x, 0, 1, stride=16, stride_axis=0)
    group = lane_group()
    for bit in (1, 2, 4):
        y = jnp.where((group & bit) != 0, pltpu.roll(y, SUB - bit, 0), y)
    return pltpu.roll(y, 0, 1, stride=16, stride_axis=0)


def skew_left(x):
    row = lax.broadcasted_iota(jnp.int32, (SUB, LANES), 0)
    for bit in (1, 2, 4):
        x = jnp.where((row & bit) != 0, pltpu.roll(x, LANES - 16 * bit, 1), x)
    return x


def from_owner(x):
    y = skew_left(x)
    group = lane_group()
    for bit in (1, 2, 4):
        y = jnp.where((group & bit) != 0, pltpu.roll(y, bit, 0), y)
    return skew_left(y)


def decay_of(par, r):
    return par[tile(r), :]


def coef_of(par, r):
    return par[tile(POLES + r), :]


def add_in_order(terms):
    return functools.reduce(lambda a, b: a + b, terms)


def tap_of(par, j):
    return par[tile(2 * POLES + j), :]


def scan_down(par, z, gated, w, local, gather):
    zero = jnp.zeros((SUB, LANES), F32)
    for pair in range(POLES // 2):
        modes = (2 * pair, 2 * pair + 1)
        decay = [decay_of(par, r) for r in modes]
        coef = [coef_of(par, r) for r in modes]
        final = pair == POLES // 2 - 1
        state = tuple(
            tuple(decay[n] if m == 3 else zero for m in range(MODE)) for n in range(2)
        )
        sums = (zero,) * TAPS if final else ()

        def step(i, carry, pair=pair, decay=decay, coef=coef, final=final):
            state, sums = carry
            t = LEN - 1 - i
            z_now = z[tile(t), :]
            g_now = gated[tile(t), :]
            w_now = [w[j, tile(t), :] for j in range(TAPS)]
            total = None if pair == 0 else local[tile(t), :]
            after = []
            for n in range(2):
                back, pole, ahead, power, *moments = state[n]
                back = back * decay[n] + z_now
                pole = pole + g_now * back
                ahead = ahead + power * g_now
                moments = [m + power * x for m, x in zip(moments, w_now)]
                power = power * decay[n]
                term = coef[n] * back
                total = term if total is None else total + term
                after.append((back, pole, ahead, power, *moments))
            local[tile(t), :] = total
            if final:
                sums = tuple(a + total * x for a, x in zip(sums, w_now))
            return tuple(after), sums

        state, sums = lax.fori_loop(0, LEN, step, (state, sums), unroll=4)
        for n, r in enumerate(modes):
            half, slot = divmod(r, SUB)
            back, pole, ahead, _, *moments = state[n]
            gather[tile(half * SUB + slot), :] = ahead
            gather[tile((2 + half) * SUB + slot), :] = back
            gather[tile((4 + half) * SUB + slot), :] = pole
            for j, value in enumerate(moments):
                gather[tile((ROW_MOMENT + 2 * j + half) * SUB + slot), :] = value
        for j, value in enumerate(sums):
            gather[tile(ROW_SHORT * SUB + j), :] = value


def first_kernel(*refs):
    sources, targets, refs = refs[:7], refs[7:15], refs[15:]
    (k, v, q, cot, rates, residues, amounts), refs = refs[:7], refs[7:]
    (vt, gate, gated, local, par, tail, head, message), refs = refs[:8], refs[8:]
    kt, zt, w, gather, spread, came, went = refs
    copies = [
        pltpu.make_async_copy(a, b, came.at[n])
        for n, (a, b) in enumerate(zip(sources, (k, v, q, cot, rates, residues, amounts)))
    ]
    leaving = [
        pltpu.make_async_copy(a, b, went.at[n])
        for n, (a, b) in enumerate(zip((vt, gate, gated, local, par, tail, head, message), targets))
    ]
    for copy in copies:
        copy.start()
    copies[0].wait()
    for s in range(SUB):
        kt[across(s), :] = k[s * LANES : (s + 1) * LANES, :].astype(F32).T
    copies[1].wait()
    for s in range(SUB):
        vt[across(s), :] = v[s * LANES : (s + 1) * LANES, :].astype(F32).T
    leaving[0].start()
    for copy in copies[2:]:
        copy.wait()
    for s in range(SUB):
        rows = slice(s * LANES, (s + 1) * LANES)
        zt[across(s), :] = (q[rows, :].astype(F32) * cot[rows, :].astype(F32)).T
        rate = rates[:, rows]
        par[pl.ds(s, POLES, stride=SUB), :] = jnp.exp(-rate)
        par[pl.ds(SUB * POLES + s, POLES, stride=SUB), :] = residues[:, rows] * jnp.sqrt(
            one_minus_exp(2.0 * rate)
        )
        par[pl.ds(2 * SUB * POLES + s, TAPS, stride=SUB), :] = amounts[:, rows]
    edge = SUB * EDGE
    last = slice(SUB * (LEN - HALO), SUB * LEN)
    tail[...] = kt[last, :]
    head[0:edge, :] = zt[0:edge, :]
    head[edge:, :] = vt[0:edge, :]
    for n in (4, 5, 6):
        leaving[n].start()
    for row, block in (
        (ROW_V, vt[0:edge, :]),
        (ROW_K, kt[SUB * (LEN - EDGE) : SUB * LEN, :]),
        (ROW_Z, zt[0:edge, :]),
    ):
        gather[row * edge : (row + 1) * edge, :] = block

    taps = [tap_of(par, j) for j in range(TAPS)]

    def prepare(t, before):
        keys = (kt[tile(t), :], *before)
        now = taps[0] * keys[0]
        for j in range(1, TAPS):
            now = now + taps[j] * keys[j]
        value = vt[tile(t), :]
        gate[tile(t), :] = now
        gated[tile(t), :] = now * value
        for j in range(TAPS):
            w[j, tile(t), :] = value * keys[j]
        return keys[:HALO]

    gather[tile(ROW_SHORT * SUB + TAPS), :] = jnp.zeros((SUB, LANES), F32)
    zero = gather[tile(ROW_SHORT * SUB + TAPS), :]
    lax.fori_loop(0, LEN, prepare, (zero,) * HALO, unroll=4)
    leaving[1].start()
    leaving[2].start()
    scan_down(par, zt, gated, w, local, gather)
    leaving[3].start()
    for row in range(ROWS_OUT):
        for s in range(SUB):
            block = to_owner(gather[pl.ds(row * SUB * SUB + s, SUB, stride=SUB), :])
            spread[pl.ds(s * SUB * ROWS_OUT + row, SUB, stride=ROWS_OUT), :] = block
    message[...] = spread[...].astype(BF16)
    leaving[7].start()
    for copy in leaving:
        copy.wait()


def owner_kernel(count, scale, arrived, mine, out, x, y, kept, fix):
    x[0:ROWS_OUT, :] = jnp.zeros((ROWS_OUT, LANES), F32)
    x[ROWS_OUT:, :] = arrived[...].astype(F32)
    even = lax.broadcasted_iota(jnp.int32, (SUB, LANES), 0) % 2 == 0
    group = lane_group()
    zero = jnp.zeros((SUB, LANES), F32)

    def pattern(ref, row):
        return jnp.where(even, ref[pl.ds(row, 1), :], ref[pl.ds(row + 1, 1), :])

    rate = pattern(mine, 0)
    weight = jnp.sqrt(one_minus_exp(2.0 * rate))
    coef = pattern(mine, 2) * weight
    leap = jnp.exp(-float(LEN) * rate)
    taps = [mine[pl.ds(4 + j, 1), :] for j in range(TAPS)]
    rates = [mine[pl.ds(half, 1), :] for half in range(2)]
    growth = [jnp.broadcast_to(jnp.exp(r), (SUB, LANES)) for r in rates]
    powers = [
        [jnp.broadcast_to(jnp.exp(-float(LEN - t) * r), (SUB, LANES)) for t in range(HALO)]
        for r in rates
    ]
    taps = [jnp.broadcast_to(tap, (SUB, LANES)) for tap in taps]

    source = lax.broadcasted_iota(jnp.int32, (LANES, SUB * LANES), 0)
    target = lax.broadcasted_iota(jnp.int32, (LANES, SUB * LANES), 1)
    same = (source // 16 == target // LANES) & (source % 16 == target % 16)
    everywhere = jnp.where(same, 1.0, 0.0).astype(BF16)
    for n, (row, first) in enumerate(((ROW_V, 1), (ROW_Z, 1), (ROW_K, 0))):
        rows = x[pl.ds(first * ROWS_OUT + row, count, stride=ROWS_OUT), :].astype(BF16)
        kept[n] = jnp.dot(rows, everywhere, preferred_element_type=F32)

    def edge_of(b):
        at = pl.ds(b * SUB, SUB)
        value, slope = (
            [kept[n, at, t * LANES : (t + 1) * LANES] for t in range(HALO)] for n in range(2)
        )
        key = [kept[2, at, (EDGE - m) * LANES : (EDGE - m + 1) * LANES] for m in range(1, TAPS)]
        return value, slope, [None, *key]

    def shards(row, b):
        return pl.ds((b * SUB + 1) * ROWS_OUT + row, SUB, stride=ROWS_OUT)

    fix[...] = jnp.zeros(fix.shape, F32)
    batches = count // SUB
    poles = [zero, zero]
    for b in range(batches):
        value, slope, key = edge_of(b)
        extra = [
            value[t] * add_in_order(taps[j] * key[j - t] for j in range(t + 1, TAPS))
            for t in range(HALO)
        ]
        for half in range(2):
            back = x[shards(2 + half, b), :]
            fix[pl.ds(b * SUB * SUB + half, SUB, stride=SUB), :] = add_in_order(
                extra[t] * powers[half][t] for t in range(HALO)
            )
            for t in range(HALO):
                poles[half] = poles[half] + extra[t] * back
                if t < HALO - 1:
                    back = (back - slope[t]) * growth[half]

    ahead, pole, total = zero, zero, zero
    for d in range(count):
        base = (d + 1) * ROWS_OUT
        y[pl.ds(d * ROWS_BACK, 2), :] = ahead[0:2, :]
        now = x[pl.ds(base, SUB), :]
        pole = pole + ahead * pattern(x, base + 2)
        total = total + now
        ahead = ahead * leap + (now + fix[tile(d), :])
    back, low, high = zero, zero, zero
    for d in reversed(range(count)):
        base = (d + 1) * ROWS_OUT
        y[pl.ds(d * ROWS_BACK + 2, 2), :] = back[0:2, :]
        low = low + back * x[pl.ds(base + SUB, SUB), :]
        high = high + back * x[pl.ds(base + 2 * SUB, SUB), :]
        back = back * leap + pattern(x, base + 2)

    edges = [[zero] * TAPS for _ in range(2)]
    for b in range(batches):
        value, slope, key = edge_of(b)
        start = b * SUB
        states = []
        for half in range(2):
            own = x[shards(2 + half, b), :]
            later = y[pl.ds(start * ROWS_BACK + 2 + half, SUB, stride=ROWS_BACK), :]
            states.append(own + later * powers[half][0])
        for t in range(HALO):
            for j in range(t + 1, TAPS):
                product = value[t] * key[j - t]
                for half in range(2):
                    edges[half][j] = edges[half][j] + states[half] * product
            states = [(a - slope[t]) * g for a, g in zip(states, growth)]

    def down(rows):
        return jnp.sum(rows, axis=0, keepdims=True)

    owned = jnp.concatenate([down(p) for p in poles])
    owned = (owned + pole[0:2, :] + total[4:6, :]) * weight[0:2, :] * scale
    short = total[ROW_SHORT : ROW_SHORT + 1, :]
    group = group[0:1, :]
    for part, first in ((low * coef, 0), (high * coef, 4)):
        part = part + pltpu.roll(part, SUB - 1, 0)
        for shift in (16, 32, 64):
            part = part + pltpu.roll(part, shift, 1)
        for n in range(min(4, TAPS - first)):
            short = short + jnp.where(group == first + n, part[2 * n : 2 * n + 1, :], 0.0)
    for j in range(1, TAPS):
        part = down(edges[0][j]) * coef[0:1, :] + down(edges[1][j]) * coef[1:2, :]
        for shift in (16, 32, 64):
            part = part + pltpu.roll(part, shift, 1)
        short = short + jnp.where(group == j, part, 0.0)
    short = short * scale
    coarse = short.astype(BF16).astype(F32)
    fine = short - coarse
    for d in range(count):
        y[pl.ds(d * ROWS_BACK + 4, 2), :] = owned
        y[pl.ds(d * ROWS_BACK + 6, 1), :] = coarse
        y[pl.ds(d * ROWS_BACK + 7, 1), :] = fine
    out[...] = y[...].astype(BF16)


def forward_kernel(gated, par, own_out):
    half = POLES // 2
    for part in range(2):
        modes = range(part * half, (part + 1) * half)
        decay = [decay_of(par, r) for r in modes]
        coef = [coef_of(par, r) for r in modes]
        ahead = (jnp.zeros((SUB, LANES), F32),) * half

        def forward(i, ahead, part=part, decay=decay, coef=coef):
            now = gated[tile(i), :]
            total = None if part == 0 else own_out[tile(i), :]
            after = []
            for h, d, c in zip(ahead, decay, coef):
                h = h + now
                term = c * h
                total = term if total is None else total + term
                after.append(h * d)
            own_out[tile(i), :] = total
            return tuple(after)

        lax.fori_loop(0, LEN, forward, ahead, unroll=4)


def halo_gates(tail, par):
    return [
        add_in_order(tap_of(par, j) * tail[tile(HALO + t - j), :] for j in range(t + 1, TAPS))
        for t in range(HALO)
    ]


def add_up(terms):
    terms = list(terms)
    while len(terms) > 1:
        terms = [a + b for a, b in zip(terms[0::2], terms[1::2])]
    return terms[0]


def unpack(arrived, x, state, first):
    x[...] = arrived[...].astype(F32)
    for s in range(SUB):
        for row in range(2):
            block = x[pl.ds(s * SUB * ROWS_BACK + first + row, SUB, stride=ROWS_BACK), :]
            state[pl.ds(row * SUB * SUB + s, SUB, stride=SUB), :] = from_owner(block)


def query_kernel(arrived, own_out, tail, vt, par, cot, grad_q, grad_short, x, state, long_out):
    unpack(arrived, x, state, 0)
    for s in range(SUB):
        coarse = x[pl.ds(s * SUB * ROWS_BACK + 6, SUB, stride=ROWS_BACK), :]
        fine = x[pl.ds(s * SUB * ROWS_BACK + 7, SUB, stride=ROWS_BACK), :]
        grad_short[:, s * LANES : (s + 1) * LANES] = from_owner(coarse + fine)[0:TAPS, :]
    decay = [decay_of(par, r) for r in range(POLES)]

    def forward(t, terms):
        long_out[tile(t), :] = own_out[tile(t), :] + add_up(terms)
        return tuple(q * d for q, d in zip(terms, decay))

    terms = tuple(coef_of(par, r) * state[tile(r), :] for r in range(POLES))
    gates = halo_gates(tail, par)
    for t in range(EDGE):
        if t < HALO:
            extra = gates[t] * vt[tile(t), :]
            terms = tuple(q + coef_of(par, r) * extra for r, q in enumerate(terms))
        terms = forward(t, terms)
    lax.fori_loop(EDGE, LEN, forward, terms, unroll=4)
    for s in range(SUB):
        rows = slice(s * LANES, (s + 1) * LANES)
        grad_q[rows, :] = (cot[rows, :].astype(F32) * long_out[across(s), :].T).astype(BF16)


def key_kernel(
    arrived, gate, local, vt, tail, head, par, query,
    grad_k, grad_v, grad_q, x, state, slope, vals, gone,
):
    leaving = pltpu.make_async_copy(query, grad_q, gone)
    leaving.start()
    unpack(arrived, x, state, 2)
    decay = [decay_of(par, r) for r in range(POLES)]
    back = [state[tile(r), :] for r in range(POLES)]
    growth = [1.0 / d for d in decay]
    ahead = []
    for n in range(HALO):
        ahead.append(
            add_up(coef_of(par, r) * back[r] for r in range(POLES)) * head[tile(EDGE + n), :]
        )
        if n < HALO - 1:
            z_now = head[tile(n), :]
            back = [(b - z_now) * g for b, g in zip(back, growth)]
    taps = [tap_of(par, j) for j in range(TAPS)]

    def backward(i, carry, extra=None):
        terms, ahead = carry
        t = LEN - 1 - i
        terms = tuple(q * d for q, d in zip(terms, decay))
        total = local[tile(t), :] + add_up(terms)
        now = gate[tile(t), :]
        vals[tile(t), :] = total * (now if extra is None else now + extra)
        slopes = (total * vt[tile(t), :], *ahead)
        slope[tile(t), :] = add_in_order(taps[j] * slopes[j] for j in range(TAPS))
        return terms, slopes[:HALO]

    terms = tuple(coef_of(par, r) * state[tile(r), :] for r in range(POLES))
    carry = (terms, tuple(ahead))
    carry = lax.fori_loop(0, LEN - EDGE, backward, carry, unroll=4)
    gates = halo_gates(tail, par)
    for t in reversed(range(EDGE)):
        carry = backward(LEN - 1 - t, carry, gates[t] if t < HALO else None)
    for s in range(SUB):
        rows = slice(s * LANES, (s + 1) * LANES)
        grad_k[rows, :] = slope[across(s), :].T.astype(BF16)
        grad_v[rows, :] = vals[across(s), :].T.astype(BF16)
    leaving.wait()


def pole_kernel(near, far, out, x):
    x[...] = near[...].astype(F32) + far[...].astype(F32)
    for s in range(SUB):
        for half in range(2):
            block = x[pl.ds(s * SUB * 2 + half, SUB, stride=2), :]
            out[half * SUB : (half + 1) * SUB, s * LANES : (s + 1) * LANES] = from_owner(block)


def call(
    kernel, name, outs, scratch, operands, flops=0, moved=0, space=pltpu.VMEM, vmem=VMEM, last=None
):
    spaces = [space] * (len(outs) - 1) + [last or space]
    return pl.pallas_call(
        kernel,
        out_shape=outs,
        in_specs=[pl.BlockSpec(memory_space=space)] * len(operands),
        out_specs=[pl.BlockSpec(memory_space=s) for s in spaces],
        scratch_shapes=scratch,
        compiler_params=pltpu.CompilerParams(vmem_limit_bytes=vmem),
        cost_estimate=pl.CostEstimate(flops=flops, bytes_accessed=moved, transcendentals=0),
        name=name,
    )(*operands)


def shape(rows, dtype=F32, lanes=LANES):
    return jax.ShapeDtypeStruct((rows, lanes), dtype)


def per_device(q_in, k_in, v_in, cotangent, taps_short, residues, rates):
    channels, length = q_in.shape
    count = lax.axis_size("seq")
    index = lax.axis_index("seq")
    chans = lax.axis_size("chan")
    assert (channels, length, count) == (SUB * LANES, LEN, SUB * SUB)
    scale = (length * count) ** (-0.5)
    full, edge, halo = SUB * LEN, SUB * EDGE, SUB * HALO

    operands = (k_in, v_in, q_in, cotangent, rates.T, residues.T, taps_short.T)
    outs = [shape(full)] * 4 + [shape(SUB * 40), shape(halo), shape(2 * edge)]
    outs.append(shape(count * ROWS_OUT, BF16))
    vt, gate, gated, local, par, tail, head, message = call(
        first_kernel,
        "first",
        outs,
        [
            *(pltpu.VMEM(a.shape, a.dtype) for a in (*operands, *outs)),
            pltpu.VMEM((full, LANES), F32),
            pltpu.VMEM((full, LANES), F32),
            pltpu.VMEM((TAPS, full, LANES), F32),
            pltpu.VMEM((SUB * SUB * ROWS_OUT, LANES), F32),
            pltpu.VMEM((count * ROWS_OUT, LANES), F32),
            pltpu.SemaphoreType.DMA((len(operands),)),
            pltpu.SemaphoreType.DMA((len(outs),)),
        ],
        operands,
        flops=48 * 10**6,
        moved=4 * 10**6,
        space=pltpu.HBM,
        vmem=VMEM_FIRST,
    )

    def exchange(x, rows):
        x = x.reshape(count, rows // 2, 2, LANES)
        return lax.all_to_all(x, "seq", split_axis=0, concat_axis=0, tiled=True)

    arrived = exchange(message, ROWS_OUT).reshape(count * ROWS_OUT, LANES)
    start = (index // SUB) * LANES + ((SUB - index % SUB) % SUB) * 16
    mine = [
        lax.dynamic_slice(a.T, (0, start), (POLES, 16)).reshape(2, LANES) for a in (rates, residues)
    ]
    own_taps = lax.dynamic_slice(taps_short.T, (0, start), (TAPS, 16))
    mine = jnp.concatenate([*mine, jnp.tile(own_taps, (1, LANES // 16))])
    tail = lax.ppermute(tail, "seq", [(i, i + 1) for i in range(count - 1)])
    head = lax.ppermute(head, "seq", [(i + 1, i) for i in range(count - 1)])
    (own_out,) = call(
        forward_kernel,
        "forward",
        [shape(full)],
        [],
        (gated, par),
        flops=10 * 10**6,
        moved=10**6,
    )
    arrived, own_out, tail, head, mine = lax.optimization_barrier(
        (arrived, own_out, tail, head, mine)
    )
    (back,) = call(
        functools.partial(owner_kernel, count, scale),
        "owner",
        [shape(count * ROWS_BACK, BF16)],
        [
            pltpu.VMEM(((count + 1) * ROWS_OUT, LANES), F32),
            pltpu.VMEM((count * ROWS_BACK, LANES), F32),
            pltpu.VMEM((3, count, SUB * LANES), F32),
            pltpu.VMEM((count * SUB, LANES), F32),
        ],
        (arrived, mine),
        flops=2 * 10**6,
        moved=10**6,
    )
    returned = exchange(back, ROWS_BACK)
    poles = returned[:, 2].reshape(2 * count, LANES)
    returned = returned.reshape(count * ROWS_BACK, LANES)

    def other(x, bit):
        return lax.ppermute(x, "chan", [(i, i ^ bit) for i in range(chans)])

    swap = [
        pltpu.VMEM((count * ROWS_BACK, LANES), F32),
        pltpu.VMEM((SUB * POLES, LANES), F32),
    ]
    near = other(poles, 1)
    query, grad_short = call(
        query_kernel,
        "query",
        [shape(channels, BF16), shape(TAPS, F32, channels)],
        [*swap, pltpu.VMEM((full, LANES), F32)],
        (returned, own_out, tail, vt, par, cotangent),
        flops=5 * 10**6,
        moved=10**6,
    )
    near, query = lax.optimization_barrier((near, query))
    near = (poles.astype(F32) + near.astype(F32)).astype(BF16)
    far = other(near, 3)
    grad_k, grad_v, grad_q = call(
        key_kernel,
        "key",
        [shape(channels, BF16)] * 3,
        [
            *swap,
            pltpu.VMEM((full, LANES), F32),
            pltpu.VMEM((full, LANES), F32),
            pltpu.SemaphoreType.DMA,
        ],
        (returned, gate, local, vt, tail, head, par, query),
        flops=8 * 10**6,
        moved=2 * 10**6,
        last=pltpu.HBM,
    )
    (grad_residues,) = call(
        pole_kernel,
        "poles",
        [shape(POLES, F32, channels)],
        [pltpu.VMEM((2 * count, LANES), F32)],
        (near, far),
        flops=10**5,
        moved=10**5,
    )
    return grad_q, grad_k, grad_v, grad_short.T, grad_residues.T


def solution(mesh):
    streams = P("chan", "seq")
    return jax.shard_map(
        per_device,
        mesh=mesh,
        in_specs=(streams,) * 4 + (P("chan", None), P(), P()),
        out_specs=(streams,) * 3 + (P("chan", None), P()),
        check_vma=False,
    )
```

```python
import functools

import jax
import jax.numpy as jnp
from jax import lax
from jax.experimental import pallas as pl
from jax.experimental.pallas import tpu as pltpu
from jax.sharding import PartitionSpec as P

F32 = jnp.float32
BF16 = jnp.bfloat16
LANES = 128
SUB = 8
LEN = 128
POLES = 16
TAPS = 7
HALO = TAPS - 1
EDGE = 8
ROWS_OUT = 24
FIR_TERMS = tuple((n, q) for n in range(9) for q in range(2) if (n, q) != (8, 1))
BACK_MODES, BACK_UNROLL, AHEAD_MODES, AHEAD_UNROLL = 8, 16, 2, 16
ROW_SHORT, ROW_V, ROW_MOMENT, ROW_K, ROW_Z = 6, 7, 8, 22, 23
ROWS_BACK = 8
VMEM = 48 * 1024 * 1024
VMEM_FIRST = 62 * 1024 * 1024


def one_minus_exp(x):
    series = 1.0 - x * (1.0 / 7.0)
    for order in (6.0, 5.0, 4.0, 3.0, 2.0):
        series = 1.0 - x * (1.0 / order) * series
    return x * series


def tile(index):
    if isinstance(index, int):
        return pl.ds(SUB * index, SUB)
    return pl.ds(pl.multiple_of(SUB * index, SUB), SUB)


def across(block):
    return pl.ds(block, LEN, stride=SUB)


def lane_group():
    return lax.broadcasted_iota(jnp.int32, (SUB, LANES), 1) // 16


def to_owner(x):
    y = pltpu.roll(x, 0, 1, stride=16, stride_axis=0)
    group = lane_group()
    for bit in (1, 2, 4):
        y = jnp.where((group & bit) != 0, pltpu.roll(y, SUB - bit, 0), y)
    return pltpu.roll(y, 0, 1, stride=16, stride_axis=0)


def skew_left(x):
    row = lax.broadcasted_iota(jnp.int32, (SUB, LANES), 0)
    for bit in (1, 2, 4):
        x = jnp.where((row & bit) != 0, pltpu.roll(x, LANES - 16 * bit, 1), x)
    return x


def from_owner(x):
    y = skew_left(x)
    group = lane_group()
    for bit in (1, 2, 4):
        y = jnp.where((group & bit) != 0, pltpu.roll(y, bit, 0), y)
    return skew_left(y)


def decay_of(par, r):
    return par[tile(r), :]


def coef_of(par, r):
    return par[tile(POLES + r), :]


def add_in_order(terms):
    return functools.reduce(lambda a, b: a + b, terms)


def tap_of(par, j):
    return par[tile(2 * POLES + j), :]


def add_up(terms):
    terms = list(terms)
    while len(terms) > 1:
        terms = [a + b for a, b in zip(terms[0::2], terms[1::2])]
    return terms[0]


def key_sums(now, before):
    even = (now[0], now[1] - now[0], before[0] - now[0])
    odd = (now[2], now[3] - now[2], now[1] - now[2])
    earlier = (before[1], before[0] - before[1], before[2] - before[1])
    return [x for e, o, p in zip(even, odd, earlier) for x in (e, o - e, p - e)]


def correlate(sums, u, keys):
    lines = (
        (u[0] + u[1], u[2] + u[3]),
        (u[1], u[3]),
        (u[0], u[2]),
    )
    factors = []
    for even, odd in lines:
        factors += [even + odd, odd, even]
    return [
        total + factors[line] * keys[q][line]
        for total, (line, q) in zip(sums, FIR_TERMS)
    ]


def moments(sums):
    part = dict(zip(FIR_TERMS, sums))
    lines = []
    for n in range(3):
        line = []
        for q in range(2):
            line.append(part[3 * n, q] + part[3 * n + 1, q])
            if (3 * n + 2, q) in part:
                line.append(part[3 * n + 2, q] + part[3 * n, q])
        lines.append(line)
    both, odd, even = lines
    out = []
    for j in range(TAPS):
        n = j // 2
        out.append(both[n] + (even[n] if j % 2 else odd[n]))
    return out


def scan_down(par, z, v, gate, gated, keys, local, gather):
    zero = jnp.zeros((SUB, LANES), F32)
    terms = len(FIR_TERMS)

    def keys_of(m):
        return tuple(keys[n, tile(m + 1), :] for n in range(9))

    for first in range(0, POLES, BACK_MODES):
        modes = range(first, first + BACK_MODES)
        decay = [decay_of(par, r) for r in modes]
        coef = [coef_of(par, r) for r in modes]

        def back_step(i, state, first=first, decay=decay, coef=coef):
            at = tile(LEN - 1 - i)
            z_now, g_now = z[at, :], gated[at, :]
            after, parts = [], []
            for (back, pole), d, c in zip(state, decay, coef):
                back = back * d + z_now
                after.append((back, pole + g_now * back))
                parts.append(c * back)
            total = add_up(parts)
            local[at, :] = total if first == 0 else local[at, :] + total
            return tuple(after)

        state = lax.fori_loop(
            0, LEN, back_step, ((zero, zero),) * BACK_MODES, unroll=BACK_UNROLL
        )
        for (back, pole), r in zip(state, modes):
            half, slot = divmod(r, SUB)
            gather[tile((2 + half) * SUB + slot), :] = back
            gather[tile((4 + half) * SUB + slot), :] = pole

    for first in range(0, POLES, AHEAD_MODES):
        modes = range(first, first + AHEAD_MODES)
        decay = [decay_of(par, r) for r in modes]

        def ahead_step(i, carry, decay=decay):
            state, now = carry
            m = LEN // 4 - 1 - i
            at = [tile(4 * m + n) for n in range(4)]
            before = keys_of(m - 1)
            keyed = (now, before)
            after = []
            for (ahead, power, sums), d in zip(state, decay):
                u = [None] * 4
                for p in reversed(range(4)):
                    u[p] = power * v[at[p], :]
                    ahead = ahead + u[p] * gate[at[p], :]
                    power = power * d
                after.append((ahead, power, tuple(correlate(sums, u, keyed))))
            return tuple(after), before

        state = tuple((zero, d, (zero,) * terms) for d in decay)
        carry = (state, keys_of(LEN // 4 - 1))
        state, _ = lax.fori_loop(0, LEN // 4, ahead_step, carry, unroll=AHEAD_UNROLL)
        for (ahead, _, sums), r in zip(state, modes):
            half, slot = divmod(r, SUB)
            gather[tile(half * SUB + slot), :] = ahead
            for j, value in enumerate(moments(sums)):
                gather[tile((ROW_MOMENT + 2 * j + half) * SUB + slot), :] = value

    def step(m, carry):
        sums, before = carry
        at = [tile(4 * m + n) for n in range(4)]
        now = keys_of(m)
        u = [local[p, :] * v[p, :] for p in at]
        return tuple(correlate(sums, u, (now, before))), now

    sums, _ = lax.fori_loop(0, LEN // 4, step, ((zero,) * terms, keys_of(-1)), unroll=8)
    for j, value in enumerate(moments(sums)):
        gather[tile(ROW_SHORT * SUB + j), :] = value


def first_kernel(*refs):
    sources, targets, refs = refs[:7], refs[7:15], refs[15:]
    (k, v, q, cot, rates, residues, amounts), refs = refs[:7], refs[7:]
    (vt, gate, gated, local, par, tail, head, message), refs = refs[:8], refs[8:]
    kt, zt, keys, gather, spread, came, went = refs
    copies = [
        pltpu.make_async_copy(a, b, came.at[n])
        for n, (a, b) in enumerate(zip(sources, (k, v, q, cot, rates, residues, amounts)))
    ]
    leaving = [
        pltpu.make_async_copy(a, b, went.at[n])
        for n, (a, b) in enumerate(zip((vt, gate, gated, local, par, tail, head, message), targets))
    ]
    for copy in copies:
        copy.start()
    copies[0].wait()
    for s in range(SUB):
        kt[across(s), :] = k[s * LANES : (s + 1) * LANES, :].astype(F32).T
    copies[1].wait()
    for s in range(SUB):
        vt[across(s), :] = v[s * LANES : (s + 1) * LANES, :].astype(F32).T
    leaving[0].start()
    for copy in copies[2:]:
        copy.wait()
    for s in range(SUB):
        rows = slice(s * LANES, (s + 1) * LANES)
        zt[across(s), :] = (q[rows, :].astype(F32) * cot[rows, :].astype(F32)).T
        rate = rates[:, rows]
        par[pl.ds(s, POLES, stride=SUB), :] = jnp.exp(-rate)
        par[pl.ds(SUB * POLES + s, POLES, stride=SUB), :] = residues[:, rows] * jnp.sqrt(
            one_minus_exp(2.0 * rate)
        )
        par[pl.ds(2 * SUB * POLES + s, TAPS, stride=SUB), :] = amounts[:, rows]
    edge = SUB * EDGE
    last = slice(SUB * (LEN - HALO), SUB * LEN)
    tail[...] = kt[last, :]
    head[0:edge, :] = zt[0:edge, :]
    head[edge:, :] = vt[0:edge, :]
    for n in (4, 5, 6):
        leaving[n].start()
    for row, block in (
        (ROW_V, vt[0:edge, :]),
        (ROW_K, kt[SUB * (LEN - EDGE) : SUB * LEN, :]),
        (ROW_Z, zt[0:edge, :]),
    ):
        gather[row * edge : (row + 1) * edge, :] = block

    taps = [tap_of(par, j) for j in range(TAPS)]

    def prepare(m, before):
        at = [tile(4 * m + n) for n in range(4)]
        now = [kt[p, :] for p in at]
        line = [*reversed(now), *before]
        for n in range(4):
            total = add_in_order(taps[j] * line[3 - n + j] for j in range(TAPS))
            gate[at[n], :] = total
            gated[at[n], :] = total * vt[at[n], :]
        for n, value in enumerate(key_sums(now, before)):
            keys[n, tile(m + 1), :] = value
        return tuple(line[:HALO])

    gather[tile(ROW_SHORT * SUB + TAPS), :] = jnp.zeros((SUB, LANES), F32)
    zero = gather[tile(ROW_SHORT * SUB + TAPS), :]
    for n in range(9):
        keys[n, tile(0), :] = zero
    lax.fori_loop(0, LEN // 4, prepare, (zero,) * HALO, unroll=2)
    leaving[1].start()
    leaving[2].start()
    scan_down(par, zt, vt, gate, gated, keys, local, gather)
    leaving[3].start()
    for row in range(ROWS_OUT):
        for s in range(SUB):
            block = to_owner(gather[pl.ds(row * SUB * SUB + s, SUB, stride=SUB), :])
            spread[pl.ds(s * SUB * ROWS_OUT + row, SUB, stride=ROWS_OUT), :] = block
    message[...] = spread[...].astype(BF16)
    leaving[7].start()
    for copy in leaving:
        copy.wait()


def owner_kernel(count, scale, arrived, mine, out, x, y, kept, fix):
    x[0:ROWS_OUT, :] = jnp.zeros((ROWS_OUT, LANES), F32)
    x[ROWS_OUT:, :] = arrived[...].astype(F32)
    even = lax.broadcasted_iota(jnp.int32, (SUB, LANES), 0) % 2 == 0
    group = lane_group()
    zero = jnp.zeros((SUB, LANES), F32)

    def pattern(ref, row):
        return jnp.where(even, ref[pl.ds(row, 1), :], ref[pl.ds(row + 1, 1), :])

    rate = pattern(mine, 0)
    weight = jnp.sqrt(one_minus_exp(2.0 * rate))
    coef = pattern(mine, 2) * weight
    leap = jnp.exp(-float(LEN) * rate)
    taps = [mine[pl.ds(4 + j, 1), :] for j in range(TAPS)]
    rates = [mine[pl.ds(half, 1), :] for half in range(2)]
    growth = [jnp.broadcast_to(jnp.exp(r), (SUB, LANES)) for r in rates]
    powers = [
        [jnp.broadcast_to(jnp.exp(-float(LEN - t) * r), (SUB, LANES)) for t in range(HALO)]
        for r in rates
    ]
    taps = [jnp.broadcast_to(tap, (SUB, LANES)) for tap in taps]

    source = lax.broadcasted_iota(jnp.int32, (LANES, SUB * LANES), 0)
    target = lax.broadcasted_iota(jnp.int32, (LANES, SUB * LANES), 1)
    same = (source // 16 == target // LANES) & (source % 16 == target % 16)
    everywhere = jnp.where(same, 1.0, 0.0).astype(BF16)
    for n, (row, first) in enumerate(((ROW_V, 1), (ROW_Z, 1), (ROW_K, 0))):
        rows = x[pl.ds(first * ROWS_OUT + row, count, stride=ROWS_OUT), :].astype(BF16)
        kept[n] = jnp.dot(rows, everywhere, preferred_element_type=F32)

    def edge_of(b):
        at = pl.ds(b * SUB, SUB)
        value, slope = (
            [kept[n, at, t * LANES : (t + 1) * LANES] for t in range(HALO)] for n in range(2)
        )
        key = [kept[2, at, (EDGE - m) * LANES : (EDGE - m + 1) * LANES] for m in range(1, TAPS)]
        return value, slope, [None, *key]

    def shards(row, b):
        return pl.ds((b * SUB + 1) * ROWS_OUT + row, SUB, stride=ROWS_OUT)

    fix[...] = jnp.zeros(fix.shape, F32)
    batches = count // SUB
    poles = [zero, zero]
    for b in range(batches):
        value, slope, key = edge_of(b)
        extra = [
            value[t] * add_in_order(taps[j] * key[j - t] for j in range(t + 1, TAPS))
            for t in range(HALO)
        ]
        for half in range(2):
            back = x[shards(2 + half, b), :]
            fix[pl.ds(b * SUB * SUB + half, SUB, stride=SUB), :] = add_in_order(
                extra[t] * powers[half][t] for t in range(HALO)
            )
            for t in range(HALO):
                poles[half] = poles[half] + extra[t] * back
                if t < HALO - 1:
                    back = (back - slope[t]) * growth[half]

    ahead, pole, total = zero, zero, zero
    for d in range(count):
        base = (d + 1) * ROWS_OUT
        y[pl.ds(d * ROWS_BACK, 2), :] = ahead[0:2, :]
        now = x[pl.ds(base, SUB), :]
        pole = pole + ahead * pattern(x, base + 2)
        total = total + now
        ahead = ahead * leap + (now + fix[tile(d), :])
    back, low, high = zero, zero, zero
    for d in reversed(range(count)):
        base = (d + 1) * ROWS_OUT
        y[pl.ds(d * ROWS_BACK + 2, 2), :] = back[0:2, :]
        low = low + back * x[pl.ds(base + SUB, SUB), :]
        high = high + back * x[pl.ds(base + 2 * SUB, SUB), :]
        back = back * leap + pattern(x, base + 2)

    edges = [[zero] * TAPS for _ in range(2)]
    for b in range(batches):
        value, slope, key = edge_of(b)
        start = b * SUB
        states = []
        for half in range(2):
            own = x[shards(2 + half, b), :]
            later = y[pl.ds(start * ROWS_BACK + 2 + half, SUB, stride=ROWS_BACK), :]
            states.append(own + later * powers[half][0])
        for t in range(HALO):
            for j in range(t + 1, TAPS):
                product = value[t] * key[j - t]
                for half in range(2):
                    edges[half][j] = edges[half][j] + states[half] * product
            states = [(a - slope[t]) * g for a, g in zip(states, growth)]

    def down(rows):
        return jnp.sum(rows, axis=0, keepdims=True)

    owned = jnp.concatenate([down(p) for p in poles])
    owned = (owned + pole[0:2, :] + total[4:6, :]) * weight[0:2, :] * scale
    short = total[ROW_SHORT : ROW_SHORT + 1, :]
    group = group[0:1, :]
    for part, first in ((low * coef, 0), (high * coef, 4)):
        part = part + pltpu.roll(part, SUB - 1, 0)
        for shift in (16, 32, 64):
            part = part + pltpu.roll(part, shift, 1)
        for n in range(min(4, TAPS - first)):
            short = short + jnp.where(group == first + n, part[2 * n : 2 * n + 1, :], 0.0)
    for j in range(1, TAPS):
        part = down(edges[0][j]) * coef[0:1, :] + down(edges[1][j]) * coef[1:2, :]
        for shift in (16, 32, 64):
            part = part + pltpu.roll(part, shift, 1)
        short = short + jnp.where(group == j, part, 0.0)
    short = short * scale
    coarse = short.astype(BF16).astype(F32)
    fine = short - coarse
    for d in range(count):
        y[pl.ds(d * ROWS_BACK + 4, 2), :] = owned
        y[pl.ds(d * ROWS_BACK + 6, 1), :] = coarse
        y[pl.ds(d * ROWS_BACK + 7, 1), :] = fine
    out[...] = y[...].astype(BF16)


def forward_kernel(gated, par, own_out):
    half = POLES // 2
    for part in range(2):
        modes = range(part * half, (part + 1) * half)
        decay = [decay_of(par, r) for r in modes]
        coef = [coef_of(par, r) for r in modes]
        ahead = (jnp.zeros((SUB, LANES), F32),) * half

        def forward(i, ahead, part=part, decay=decay, coef=coef):
            now = gated[tile(i), :]
            total = None if part == 0 else own_out[tile(i), :]
            after = []
            for h, d, c in zip(ahead, decay, coef):
                h = h + now
                term = c * h
                total = term if total is None else total + term
                after.append(h * d)
            own_out[tile(i), :] = total
            return tuple(after)

        lax.fori_loop(0, LEN, forward, ahead, unroll=16)


def halo_gates(tail, par):
    return [
        add_in_order(tap_of(par, j) * tail[tile(HALO + t - j), :] for j in range(t + 1, TAPS))
        for t in range(HALO)
    ]


def unpack(arrived, x, state, first):
    x[...] = arrived[...].astype(F32)
    for s in range(SUB):
        for row in range(2):
            block = x[pl.ds(s * SUB * ROWS_BACK + first + row, SUB, stride=ROWS_BACK), :]
            state[pl.ds(row * SUB * SUB + s, SUB, stride=SUB), :] = from_owner(block)


def query_kernel(arrived, own_out, tail, vt, par, cot, grad_q, grad_short, x, state, long_out):
    unpack(arrived, x, state, 0)
    for s in range(SUB):
        coarse = x[pl.ds(s * SUB * ROWS_BACK + 6, SUB, stride=ROWS_BACK), :]
        fine = x[pl.ds(s * SUB * ROWS_BACK + 7, SUB, stride=ROWS_BACK), :]
        grad_short[:, s * LANES : (s + 1) * LANES] = from_owner(coarse + fine)[0:TAPS, :]
    decay = [decay_of(par, r) for r in range(POLES)]

    def forward(t, terms):
        long_out[tile(t), :] = own_out[tile(t), :] + add_up(terms)
        return tuple(q * d for q, d in zip(terms, decay))

    terms = tuple(coef_of(par, r) * state[tile(r), :] for r in range(POLES))
    gates = halo_gates(tail, par)
    for t in range(EDGE):
        if t < HALO:
            extra = gates[t] * vt[tile(t), :]
            terms = tuple(q + coef_of(par, r) * extra for r, q in enumerate(terms))
        terms = forward(t, terms)
    lax.fori_loop(EDGE, LEN, forward, terms, unroll=24)
    for s in range(SUB):
        rows = slice(s * LANES, (s + 1) * LANES)
        grad_q[rows, :] = (cot[rows, :].astype(F32) * long_out[across(s), :].T).astype(BF16)


def key_kernel(
    arrived, gate, local, vt, tail, head, par, query,
    grad_k, grad_v, grad_q, x, state, slope, vals, gone,
):
    leaving = pltpu.make_async_copy(query, grad_q, gone)
    leaving.start()
    unpack(arrived, x, state, 2)
    decay = [decay_of(par, r) for r in range(POLES)]
    back = [state[tile(r), :] for r in range(POLES)]
    growth = [1.0 / d for d in decay]
    ahead = []
    for n in range(HALO):
        ahead.append(
            add_up(coef_of(par, r) * back[r] for r in range(POLES)) * head[tile(EDGE + n), :]
        )
        if n < HALO - 1:
            z_now = head[tile(n), :]
            back = [(b - z_now) * g for b, g in zip(back, growth)]
    taps = [tap_of(par, j) for j in range(TAPS)]

    def backward(i, carry, extra=None):
        terms, ahead = carry
        t = LEN - 1 - i
        terms = tuple(q * d for q, d in zip(terms, decay))
        total = local[tile(t), :] + add_up(terms)
        now = gate[tile(t), :]
        vals[tile(t), :] = total * (now if extra is None else now + extra)
        slopes = (total * vt[tile(t), :], *ahead)
        slope[tile(t), :] = add_in_order(taps[j] * slopes[j] for j in range(TAPS))
        return terms, slopes[:HALO]

    terms = tuple(coef_of(par, r) * state[tile(r), :] for r in range(POLES))
    carry = (terms, tuple(ahead))
    carry = lax.fori_loop(0, LEN - EDGE, backward, carry, unroll=24)
    gates = halo_gates(tail, par)
    for t in reversed(range(EDGE)):
        carry = backward(LEN - 1 - t, carry, gates[t] if t < HALO else None)
    for s in range(SUB):
        rows = slice(s * LANES, (s + 1) * LANES)
        grad_k[rows, :] = slope[across(s), :].T.astype(BF16)
        grad_v[rows, :] = vals[across(s), :].T.astype(BF16)
    leaving.wait()


def pole_kernel(near, far, out, x):
    x[...] = near[...].astype(F32) + far[...].astype(F32)
    for s in range(SUB):
        for half in range(2):
            block = x[pl.ds(s * SUB * 2 + half, SUB, stride=2), :]
            out[half * SUB : (half + 1) * SUB, s * LANES : (s + 1) * LANES] = from_owner(block)


def call(
    kernel, name, outs, scratch, operands, flops=0, moved=0, space=pltpu.VMEM, vmem=VMEM, last=None
):
    spaces = [space] * (len(outs) - 1) + [last or space]
    return pl.pallas_call(
        kernel,
        out_shape=outs,
        in_specs=[pl.BlockSpec(memory_space=space)] * len(operands),
        out_specs=[pl.BlockSpec(memory_space=s) for s in spaces],
        scratch_shapes=scratch,
        compiler_params=pltpu.CompilerParams(vmem_limit_bytes=vmem),
        cost_estimate=pl.CostEstimate(flops=flops, bytes_accessed=moved, transcendentals=0),
        name=name,
    )(*operands)


def shape(rows, dtype=F32, lanes=LANES):
    return jax.ShapeDtypeStruct((rows, lanes), dtype)


def per_device(q_in, k_in, v_in, cotangent, taps_short, residues, rates):
    channels, length = q_in.shape
    count = lax.axis_size("seq")
    index = lax.axis_index("seq")
    chans = lax.axis_size("chan")
    assert (channels, length, count) == (SUB * LANES, LEN, SUB * SUB)
    scale = (length * count) ** (-0.5)
    full, edge, halo = SUB * LEN, SUB * EDGE, SUB * HALO

    operands = (k_in, v_in, q_in, cotangent, rates.T, residues.T, taps_short.T)
    outs = [shape(full)] * 4 + [shape(SUB * 40), shape(halo), shape(2 * edge)]
    outs.append(shape(count * ROWS_OUT, BF16))
    vt, gate, gated, local, par, tail, head, message = call(
        first_kernel,
        "first",
        outs,
        [
            *(pltpu.VMEM(a.shape, a.dtype) for a in (*operands, *outs)),
            pltpu.VMEM((full, LANES), F32),
            pltpu.VMEM((full, LANES), F32),
            pltpu.VMEM((9, full // 4 + SUB, LANES), F32),
            pltpu.VMEM((SUB * SUB * ROWS_OUT, LANES), F32),
            pltpu.VMEM((count * ROWS_OUT, LANES), F32),
            pltpu.SemaphoreType.DMA((len(operands),)),
            pltpu.SemaphoreType.DMA((len(outs),)),
        ],
        operands,
        flops=48 * 10**6,
        moved=4 * 10**6,
        space=pltpu.HBM,
        vmem=VMEM_FIRST,
    )

    def exchange(x, rows):
        x = x.reshape(count, rows // 2, 2, LANES)
        return lax.all_to_all(x, "seq", split_axis=0, concat_axis=0, tiled=True)

    arrived = exchange(message, ROWS_OUT).reshape(count * ROWS_OUT, LANES)
    start = (index // SUB) * LANES + ((SUB - index % SUB) % SUB) * 16
    mine = [
        lax.dynamic_slice(a.T, (0, start), (POLES, 16)).reshape(2, LANES) for a in (rates, residues)
    ]
    own_taps = lax.dynamic_slice(taps_short.T, (0, start), (TAPS, 16))
    mine = jnp.concatenate([*mine, jnp.tile(own_taps, (1, LANES // 16))])
    tail = lax.ppermute(tail, "seq", [(i, i + 1) for i in range(count - 1)])
    head = lax.ppermute(head, "seq", [(i + 1, i) for i in range(count - 1)])
    (own_out,) = call(
        forward_kernel,
        "forward",
        [shape(full)],
        [],
        (gated, par),
        flops=10 * 10**6,
        moved=10**6,
    )
    arrived, own_out, tail, head, mine = lax.optimization_barrier(
        (arrived, own_out, tail, head, mine)
    )
    (back,) = call(
        functools.partial(owner_kernel, count, scale),
        "owner",
        [shape(count * ROWS_BACK, BF16)],
        [
            pltpu.VMEM(((count + 1) * ROWS_OUT, LANES), F32),
            pltpu.VMEM((count * ROWS_BACK, LANES), F32),
            pltpu.VMEM((3, count, SUB * LANES), F32),
            pltpu.VMEM((count * SUB, LANES), F32),
        ],
        (arrived, mine),
        flops=2 * 10**6,
        moved=10**6,
    )
    returned = exchange(back, ROWS_BACK)
    poles = returned[:, 2].reshape(2 * count, LANES)
    returned = returned.reshape(count * ROWS_BACK, LANES)

    def other(x, bit):
        return lax.ppermute(x, "chan", [(i, i ^ bit) for i in range(chans)])

    swap = [
        pltpu.VMEM((count * ROWS_BACK, LANES), F32),
        pltpu.VMEM((SUB * POLES, LANES), F32),
    ]
    near = other(poles, 1)
    query, grad_short = call(
        query_kernel,
        "query",
        [shape(channels, BF16), shape(TAPS, F32, channels)],
        [*swap, pltpu.VMEM((full, LANES), F32)],
        (returned, own_out, tail, vt, par, cotangent),
        flops=5 * 10**6,
        moved=10**6,
    )
    near, query = lax.optimization_barrier((near, query))
    near = (poles.astype(F32) + near.astype(F32)).astype(BF16)
    far = other(near, 3)
    grad_k, grad_v, grad_q = call(
        key_kernel,
        "key",
        [shape(channels, BF16)] * 3,
        [
            *swap,
            pltpu.VMEM((full, LANES), F32),
            pltpu.VMEM((full, LANES), F32),
            pltpu.SemaphoreType.DMA,
        ],
        (returned, gate, local, vt, tail, head, par, query),
        flops=8 * 10**6,
        moved=2 * 10**6,
        last=pltpu.HBM,
    )
    (grad_residues,) = call(
        pole_kernel,
        "poles",
        [shape(POLES, F32, channels)],
        [pltpu.VMEM((2 * count, LANES), F32)],
        (near, far),
        flops=10**5,
        moved=10**5,
    )
    return grad_q, grad_k, grad_v, grad_short.T, grad_residues.T


def solution(mesh):
    streams = P("chan", "seq")
    return jax.shard_map(
        per_device,
        mesh=mesh,
        in_specs=(streams,) * 4 + (P("chan", None), P(), P()),
        out_specs=(streams,) * 3 + (P("chan", None), P()),
        check_vma=False,
    )
```

```python
import functools

import jax
import jax.numpy as jnp
from jax import lax
from jax.experimental import pallas as pl
from jax.experimental.pallas import tpu as pltpu
from jax.sharding import PartitionSpec as P

F32 = jnp.float32
BF16 = jnp.bfloat16
LANES = 128
SUB = 8
LEN = 128
POLES = 16
TAPS = 7
HALO = TAPS - 1
EDGE = 8
ROWS_OUT = 24
FIR_TERMS = tuple((n, q) for n in range(9) for q in range(2) if (n, q) != (8, 1))
BACK_MODES, BACK_UNROLL, AHEAD_MODES, AHEAD_UNROLL = 8, 16, 2, 16
ROW_SHORT, ROW_V, ROW_MOMENT, ROW_K, ROW_Z = 6, 7, 8, 22, 23
ROWS_BACK = 8
VMEM = 48 * 1024 * 1024
VMEM_FIRST = 62 * 1024 * 1024


def one_minus_exp(x):
    series = 1.0 - x * (1.0 / 7.0)
    for order in (6.0, 5.0, 4.0, 3.0, 2.0):
        series = 1.0 - x * (1.0 / order) * series
    return x * series


def tile(index):
    if isinstance(index, int):
        return pl.ds(SUB * index, SUB)
    return pl.ds(pl.multiple_of(SUB * index, SUB), SUB)


def across(block):
    return pl.ds(block, LEN, stride=SUB)


def lane_group():
    return lax.broadcasted_iota(jnp.int32, (SUB, LANES), 1) // 16


def skewed(x, way):
    row = lax.broadcasted_iota(jnp.int32, (SUB, LANES), 0)
    lane = lax.broadcasted_iota(jnp.int32, (SUB, LANES), 1)
    return jnp.take_along_axis(x, (lane + way * 16 * row) % LANES, axis=1)


def turned(x, way):
    row = lax.broadcasted_iota(jnp.int32, (SUB, LANES), 0)
    return jnp.take_along_axis(x, (row + way * lane_group()) % SUB, axis=0)


def to_owner(x):
    return skewed(turned(skewed(x, -1), 1), -1)


def from_owner(x):
    return skewed(turned(skewed(x, 1), -1), 1)


def decay_of(par, r):
    return par[tile(r), :]


def coef_of(par, r):
    return par[tile(POLES + r), :]


def add_in_order(terms):
    return functools.reduce(lambda a, b: a + b, terms)


def tap_of(par, j):
    return par[tile(2 * POLES + j), :]


def add_up(terms):
    terms = list(terms)
    while len(terms) > 1:
        terms = [a + b for a, b in zip(terms[0::2], terms[1::2])]
    return terms[0]


def key_sums(now, before):
    even = (now[0], now[1] - now[0], before[0] - now[0])
    odd = (now[2], now[3] - now[2], now[1] - now[2])
    earlier = (before[1], before[0] - before[1], before[2] - before[1])
    return [x for e, o, p in zip(even, odd, earlier) for x in (e, o - e, p - e)]


def correlate(sums, u, keys):
    lines = (
        (u[0] + u[1], u[2] + u[3]),
        (u[1], u[3]),
        (u[0], u[2]),
    )
    factors = []
    for even, odd in lines:
        factors += [even + odd, odd, even]
    return [
        total + factors[line] * keys[q][line]
        for total, (line, q) in zip(sums, FIR_TERMS)
    ]


def moments(sums):
    part = dict(zip(FIR_TERMS, sums))
    lines = []
    for n in range(3):
        line = []
        for q in range(2):
            line.append(part[3 * n, q] + part[3 * n + 1, q])
            if (3 * n + 2, q) in part:
                line.append(part[3 * n + 2, q] + part[3 * n, q])
        lines.append(line)
    both, odd, even = lines
    out = []
    for j in range(TAPS):
        n = j // 2
        out.append(both[n] + (even[n] if j % 2 else odd[n]))
    return out


def scan_down(par, z, v, gate, gated, keys, local, gather):
    zero = jnp.zeros((SUB, LANES), F32)
    terms = len(FIR_TERMS)

    def keys_of(m):
        return tuple(keys[n, tile(m + 1), :] for n in range(9))

    for first in range(0, POLES, BACK_MODES):
        modes = range(first, first + BACK_MODES)
        decay = [decay_of(par, r) for r in modes]
        coef = [coef_of(par, r) for r in modes]

        def back_step(i, state, first=first, decay=decay, coef=coef):
            at = tile(LEN - 1 - i)
            z_now, g_now = z[at, :], gated[at, :]
            after, parts = [], []
            for (back, pole), d, c in zip(state, decay, coef):
                back = back * d + z_now
                after.append((back, pole + g_now * back))
                parts.append(c * back)
            total = add_up(parts)
            local[at, :] = total if first == 0 else local[at, :] + total
            return tuple(after)

        state = lax.fori_loop(
            0, LEN, back_step, ((zero, zero),) * BACK_MODES, unroll=BACK_UNROLL
        )
        for (back, pole), r in zip(state, modes):
            half, slot = divmod(r, SUB)
            gather[tile((2 + half) * SUB + slot), :] = back
            gather[tile((4 + half) * SUB + slot), :] = pole

    for first in range(0, POLES, AHEAD_MODES):
        modes = range(first, first + AHEAD_MODES)
        decay = [decay_of(par, r) for r in modes]

        def ahead_step(i, carry, decay=decay):
            state, now = carry
            m = LEN // 4 - 1 - i
            at = [tile(4 * m + n) for n in range(4)]
            before = keys_of(m - 1)
            keyed = (now, before)
            after = []
            for (ahead, power, sums), d in zip(state, decay):
                u = [None] * 4
                for p in reversed(range(4)):
                    u[p] = power * v[at[p], :]
                    ahead = ahead + u[p] * gate[at[p], :]
                    power = power * d
                after.append((ahead, power, tuple(correlate(sums, u, keyed))))
            return tuple(after), before

        state = tuple((zero, d, (zero,) * terms) for d in decay)
        carry = (state, keys_of(LEN // 4 - 1))
        state, _ = lax.fori_loop(0, LEN // 4, ahead_step, carry, unroll=AHEAD_UNROLL)
        for (ahead, _, sums), r in zip(state, modes):
            half, slot = divmod(r, SUB)
            gather[tile(half * SUB + slot), :] = ahead
            for j, value in enumerate(moments(sums)):
                gather[tile((ROW_MOMENT + 2 * j + half) * SUB + slot), :] = value

    def step(m, carry):
        sums, before = carry
        at = [tile(4 * m + n) for n in range(4)]
        now = keys_of(m)
        u = [local[p, :] * v[p, :] for p in at]
        return tuple(correlate(sums, u, (now, before))), now

    sums, _ = lax.fori_loop(0, LEN // 4, step, ((zero,) * terms, keys_of(-1)), unroll=8)
    for j, value in enumerate(moments(sums)):
        gather[tile(ROW_SHORT * SUB + j), :] = value


def first_kernel(*refs):
    sources, targets, refs = refs[:7], refs[7:14], refs[14:]
    (k, v, q, cot, rates, residues, amounts), refs = refs[:7], refs[7:]
    (vt, gate, gated, local, par, head, message), refs = refs[:7], refs[7:]
    kt, zt, keys, gather, spread, came, went = refs
    copies = [
        pltpu.make_async_copy(a, b, came.at[n])
        for n, (a, b) in enumerate(zip(sources, (k, v, q, cot, rates, residues, amounts)))
    ]
    leaving = [
        pltpu.make_async_copy(a, b, went.at[n])
        for n, (a, b) in enumerate(zip((vt, gate, gated, local, par, head, message), targets))
    ]
    for copy in copies:
        copy.start()
    copies[0].wait()
    for s in range(SUB):
        kt[across(s), :] = k[s * LANES : (s + 1) * LANES, :].astype(F32).T
    copies[1].wait()
    for s in range(SUB):
        vt[across(s), :] = v[s * LANES : (s + 1) * LANES, :].astype(F32).T
    leaving[0].start()
    for copy in copies[2:]:
        copy.wait()
    for s in range(SUB):
        rows = slice(s * LANES, (s + 1) * LANES)
        zt[across(s), :] = (q[rows, :].astype(F32) * cot[rows, :].astype(F32)).T
        rate = rates[:, rows]
        par[pl.ds(s, POLES, stride=SUB), :] = jnp.exp(-rate)
        par[pl.ds(SUB * POLES + s, POLES, stride=SUB), :] = residues[:, rows] * jnp.sqrt(
            one_minus_exp(2.0 * rate)
        )
        par[pl.ds(2 * SUB * POLES + s, TAPS, stride=SUB), :] = amounts[:, rows]
    edge = SUB * EDGE
    head[0:edge, :] = zt[0:edge, :]
    head[edge:, :] = vt[0:edge, :]
    for n in (4, 5):
        leaving[n].start()
    for row, block in (
        (ROW_V, vt[0:edge, :]),
        (ROW_K, kt[SUB * (LEN - EDGE) : SUB * LEN, :]),
        (ROW_Z, zt[0:edge, :]),
    ):
        gather[row * edge : (row + 1) * edge, :] = block

    taps = [tap_of(par, j) for j in range(TAPS)]

    def prepare(m, before):
        at = [tile(4 * m + n) for n in range(4)]
        now = [kt[p, :] for p in at]
        line = [*reversed(now), *before]
        for n in range(4):
            total = add_in_order(taps[j] * line[3 - n + j] for j in range(TAPS))
            gate[at[n], :] = total
            gated[at[n], :] = total * vt[at[n], :]
        for n, value in enumerate(key_sums(now, before)):
            keys[n, tile(m + 1), :] = value
        return tuple(line[:HALO])

    gather[tile(ROW_SHORT * SUB + TAPS), :] = jnp.zeros((SUB, LANES), F32)
    zero = gather[tile(ROW_SHORT * SUB + TAPS), :]
    for n in range(9):
        keys[n, tile(0), :] = zero
    lax.fori_loop(0, LEN // 4, prepare, (zero,) * HALO, unroll=2)
    leaving[1].start()
    leaving[2].start()
    scan_down(par, zt, vt, gate, gated, keys, local, gather)
    leaving[3].start()
    for row in range(ROWS_OUT):
        for s in range(SUB):
            block = to_owner(gather[pl.ds(row * SUB * SUB + s, SUB, stride=SUB), :])
            spread[pl.ds(s * SUB * ROWS_OUT + row, SUB, stride=ROWS_OUT), :] = block
    message[...] = spread[...].astype(BF16)
    leaving[6].start()
    for copy in leaving:
        copy.wait()


def owner_kernel(
    count, scale, index, arrived, rate_rows, residue_rows, tap_rows, out, x, y, kept, fix, mine
):
    x[0:ROWS_OUT, :] = jnp.zeros((ROWS_OUT, LANES), F32)
    x[ROWS_OUT:, :] = arrived[...].astype(F32)
    even = lax.broadcasted_iota(jnp.int32, (SUB, LANES), 0) % 2 == 0
    group = lane_group()
    zero = jnp.zeros((SUB, LANES), F32)

    block = pl.ds(pl.multiple_of((index[0] // SUB) * LANES, LANES), LANES)
    place = index[0] % SUB
    for n, ref in enumerate((rate_rows, residue_rows)):
        for half in range(2):
            mine[...] = to_owner(ref[half * SUB : (half + 1) * SUB, block])
            fix[2 * n + half : 2 * n + half + 1, :] = mine[pl.ds(place, 1), :]
    held = jnp.where(group[0:TAPS, :] == (SUB - place) % SUB, tap_rows[:, block], 0.0)
    for shift in (16, 32, 64):
        held = held + pltpu.roll(held, shift, 1)
    taps = [jnp.broadcast_to(held[j : j + 1, :], (SUB, LANES)) for j in range(TAPS)]

    def pattern(ref, row):
        return jnp.where(even, ref[pl.ds(row, 1), :], ref[pl.ds(row + 1, 1), :])

    rate = pattern(fix, 0)
    weight = jnp.sqrt(one_minus_exp(2.0 * rate))
    coef = pattern(fix, 2) * weight
    leap = jnp.exp(-float(LEN) * rate)
    rates = [fix[pl.ds(half, 1), :] for half in range(2)]
    growth = [jnp.broadcast_to(jnp.exp(r), (SUB, LANES)) for r in rates]
    powers = [
        [jnp.broadcast_to(jnp.exp(-float(LEN - t) * r), (SUB, LANES)) for t in range(HALO)]
        for r in rates
    ]

    source = lax.broadcasted_iota(jnp.int32, (LANES, SUB * LANES), 0)
    target = lax.broadcasted_iota(jnp.int32, (LANES, SUB * LANES), 1)
    same = (source // 16 == target // LANES) & (source % 16 == target % 16)
    everywhere = jnp.where(same, 1.0, 0.0).astype(BF16)
    for n, (row, first) in enumerate(((ROW_V, 1), (ROW_Z, 1), (ROW_K, 0))):
        rows = x[pl.ds(first * ROWS_OUT + row, count, stride=ROWS_OUT), :].astype(BF16)
        kept[n] = jnp.dot(rows, everywhere, preferred_element_type=F32)

    def edge_of(b):
        at = pl.ds(b * SUB, SUB)
        value, slope = (
            [kept[n, at, t * LANES : (t + 1) * LANES] for t in range(HALO)] for n in range(2)
        )
        key = [kept[2, at, (EDGE - m) * LANES : (EDGE - m + 1) * LANES] for m in range(1, TAPS)]
        return value, slope, [None, *key]

    def shards(row, b):
        return pl.ds((b * SUB + 1) * ROWS_OUT + row, SUB, stride=ROWS_OUT)

    fix[...] = jnp.zeros(fix.shape, F32)
    batches = count // SUB
    poles = [zero, zero]
    for b in range(batches):
        value, slope, key = edge_of(b)
        extra = [
            value[t] * add_in_order(taps[j] * key[j - t] for j in range(t + 1, TAPS))
            for t in range(HALO)
        ]
        for half in range(2):
            back = x[shards(2 + half, b), :]
            fix[pl.ds(b * SUB * SUB + half, SUB, stride=SUB), :] = add_in_order(
                extra[t] * powers[half][t] for t in range(HALO)
            )
            for t in range(HALO):
                poles[half] = poles[half] + extra[t] * back
                if t < HALO - 1:
                    back = (back - slope[t]) * growth[half]

    ahead, pole, total = zero, zero, zero
    for d in range(count):
        base = (d + 1) * ROWS_OUT
        y[pl.ds(d * ROWS_BACK, 2), :] = ahead[0:2, :]
        now = x[pl.ds(base, SUB), :]
        pole = pole + ahead * pattern(x, base + 2)
        total = total + now
        ahead = ahead * leap + (now + fix[tile(d), :])
    back, low, high = zero, zero, zero
    for d in reversed(range(count)):
        base = (d + 1) * ROWS_OUT
        y[pl.ds(d * ROWS_BACK + 2, 2), :] = back[0:2, :]
        low = low + back * x[pl.ds(base + SUB, SUB), :]
        high = high + back * x[pl.ds(base + 2 * SUB, SUB), :]
        back = back * leap + pattern(x, base + 2)

    edges = [[zero] * TAPS for _ in range(2)]
    for b in range(batches):
        value, slope, key = edge_of(b)
        start = b * SUB
        states = []
        for half in range(2):
            own = x[shards(2 + half, b), :]
            later = y[pl.ds(start * ROWS_BACK + 2 + half, SUB, stride=ROWS_BACK), :]
            states.append(own + later * powers[half][0])
        for t in range(HALO):
            for j in range(t + 1, TAPS):
                product = value[t] * key[j - t]
                for half in range(2):
                    edges[half][j] = edges[half][j] + states[half] * product
            states = [(a - slope[t]) * g for a, g in zip(states, growth)]

    def down(rows):
        return jnp.sum(rows, axis=0, keepdims=True)

    owned = jnp.concatenate([down(p) for p in poles])
    owned = (owned + pole[0:2, :] + total[4:6, :]) * weight[0:2, :] * scale
    short = total[ROW_SHORT : ROW_SHORT + 1, :]
    group = group[0:1, :]
    for part, first in ((low * coef, 0), (high * coef, 4)):
        part = part + pltpu.roll(part, SUB - 1, 0)
        for shift in (16, 32, 64):
            part = part + pltpu.roll(part, shift, 1)
        for n in range(min(4, TAPS - first)):
            short = short + jnp.where(group == first + n, part[2 * n : 2 * n + 1, :], 0.0)
    for j in range(1, TAPS):
        part = down(edges[0][j]) * coef[0:1, :] + down(edges[1][j]) * coef[1:2, :]
        for shift in (16, 32, 64):
            part = part + pltpu.roll(part, shift, 1)
        short = short + jnp.where(group == j, part, 0.0)
    short = short * scale
    for d in range(count):
        y[pl.ds(d * ROWS_BACK + 4, 2), :] = owned
        y[pl.ds(d * ROWS_BACK + 6, 1), :] = short
        y[pl.ds(d * ROWS_BACK + 7, 1), :] = x[pl.ds(d * ROWS_OUT + ROW_K, 1), :]
    out[...] = y[...].astype(BF16)


def forward_kernel(gated, par, own_out):
    half = POLES // 2
    for part in range(2):
        modes = range(part * half, (part + 1) * half)
        decay = [decay_of(par, r) for r in modes]
        coef = [coef_of(par, r) for r in modes]
        ahead = (jnp.zeros((SUB, LANES), F32),) * half

        def forward(i, ahead, part=part, decay=decay, coef=coef):
            now = gated[tile(i), :]
            total = None if part == 0 else own_out[tile(i), :]
            after = []
            for h, d, c in zip(ahead, decay, coef):
                h = h + now
                term = c * h
                total = term if total is None else total + term
                after.append(h * d)
            own_out[tile(i), :] = total
            return tuple(after)

        lax.fori_loop(0, LEN, forward, ahead, unroll=16)


def halo_gates(last, par):
    return [
        add_in_order(tap_of(par, j) * last[tile(EDGE + t - j), :] for j in range(t + 1, TAPS))
        for t in range(HALO)
    ]


def unpack(arrived, x, state, first):
    x[...] = arrived[...].astype(F32)
    for s in range(SUB):
        for row in range(2):
            block = x[pl.ds(s * SUB * ROWS_BACK + first + row, SUB, stride=ROWS_BACK), :]
            state[pl.ds(row * SUB * SUB + s, SUB, stride=SUB), :] = from_owner(block)


def query_kernel(
    arrived, own_out, vt, par, cot, grad_q, extra_gate, grad_short, x, state, long_out, last
):
    unpack(arrived, x, state, 0)
    for s in range(SUB):
        short = x[pl.ds(s * SUB * ROWS_BACK + 6, SUB, stride=ROWS_BACK), :]
        grad_short[:, s * LANES : (s + 1) * LANES] = from_owner(short)[0:TAPS, :]
        keys = x[pl.ds(s * SUB * ROWS_BACK + 7, SUB, stride=ROWS_BACK), :]
        last[pl.ds(s, SUB, stride=SUB), :] = from_owner(keys)
    decay = [decay_of(par, r) for r in range(POLES)]

    def forward(t, terms):
        long_out[tile(t), :] = own_out[tile(t), :] + add_up(terms)
        return tuple(q * d for q, d in zip(terms, decay))

    terms = tuple(coef_of(par, r) * state[tile(r), :] for r in range(POLES))
    gates = halo_gates(last, par)
    for t in range(EDGE):
        if t < HALO:
            extra_gate[tile(t), :] = gates[t]
            extra = gates[t] * vt[tile(t), :]
            terms = tuple(q + coef_of(par, r) * extra for r, q in enumerate(terms))
        terms = forward(t, terms)
    lax.fori_loop(EDGE, LEN, forward, terms, unroll=24)
    for s in range(SUB):
        rows = slice(s * LANES, (s + 1) * LANES)
        grad_q[rows, :] = (cot[rows, :].astype(F32) * long_out[across(s), :].T).astype(BF16)


def key_kernel(
    arrived, gate, local, vt, extra_gate, head, par, query,
    grad_k, grad_v, grad_q, x, state, slope, vals, gone,
):
    leaving = pltpu.make_async_copy(query, grad_q, gone)
    leaving.start()
    unpack(arrived, x, state, 2)
    decay = [decay_of(par, r) for r in range(POLES)]
    back = [state[tile(r), :] for r in range(POLES)]
    growth = [1.0 / d for d in decay]
    ahead = []
    for n in range(HALO):
        ahead.append(
            add_up(coef_of(par, r) * back[r] for r in range(POLES)) * head[tile(EDGE + n), :]
        )
        if n < HALO - 1:
            z_now = head[tile(n), :]
            back = [(b - z_now) * g for b, g in zip(back, growth)]
    taps = [tap_of(par, j) for j in range(TAPS)]

    def backward(i, carry, extra=None):
        terms, ahead = carry
        t = LEN - 1 - i
        terms = tuple(q * d for q, d in zip(terms, decay))
        total = local[tile(t), :] + add_up(terms)
        now = gate[tile(t), :]
        vals[tile(t), :] = total * (now if extra is None else now + extra)
        slopes = (total * vt[tile(t), :], *ahead)
        slope[tile(t), :] = add_in_order(taps[j] * slopes[j] for j in range(TAPS))
        return terms, slopes[:HALO]

    terms = tuple(coef_of(par, r) * state[tile(r), :] for r in range(POLES))
    carry = (terms, tuple(ahead))
    carry = lax.fori_loop(0, LEN - EDGE, backward, carry, unroll=24)
    for t in reversed(range(EDGE)):
        extra = extra_gate[tile(t), :] if t < HALO else None
        carry = backward(LEN - 1 - t, carry, extra)
    for s in range(SUB):
        rows = slice(s * LANES, (s + 1) * LANES)
        grad_k[rows, :] = slope[across(s), :].T.astype(BF16)
        grad_v[rows, :] = vals[across(s), :].T.astype(BF16)
    leaving.wait()


def pole_kernel(near, far, out, x):
    x[...] = near[...].astype(F32) + far[...].astype(F32)
    for s in range(SUB):
        for half in range(2):
            block = x[pl.ds(s * SUB * 2 + half, SUB, stride=2), :]
            out[half * SUB : (half + 1) * SUB, s * LANES : (s + 1) * LANES] = from_owner(block)


def call(
    kernel, name, outs, scratch, operands, flops=0, moved=0, space=pltpu.VMEM, vmem=VMEM, last=None
):
    spaces = [space] * (len(outs) - 1) + [last or space]
    return pl.pallas_call(
        kernel,
        out_shape=outs,
        in_specs=[
            pl.BlockSpec(memory_space=pltpu.SMEM if a.dtype == jnp.int32 else space)
            for a in operands
        ],
        out_specs=[pl.BlockSpec(memory_space=s) for s in spaces],
        scratch_shapes=scratch,
        compiler_params=pltpu.CompilerParams(vmem_limit_bytes=vmem),
        cost_estimate=pl.CostEstimate(flops=flops, bytes_accessed=moved, transcendentals=0),
        name=name,
    )(*operands)


def shape(rows, dtype=F32, lanes=LANES):
    return jax.ShapeDtypeStruct((rows, lanes), dtype)


def per_device(q_in, k_in, v_in, cotangent, taps_short, residues, rates):
    channels, length = q_in.shape
    count = lax.axis_size("seq")
    index = lax.axis_index("seq")
    chans = lax.axis_size("chan")
    assert (channels, length, count) == (SUB * LANES, LEN, SUB * SUB)
    scale = (length * count) ** (-0.5)
    full, edge, halo = SUB * LEN, SUB * EDGE, SUB * HALO

    operands = (k_in, v_in, q_in, cotangent, rates.T, residues.T, taps_short.T)
    outs = [shape(full)] * 4 + [shape(SUB * 40), shape(2 * edge)]
    outs.append(shape(count * ROWS_OUT, BF16))
    vt, gate, gated, local, par, head, message = call(
        first_kernel,
        "first",
        outs,
        [
            *(pltpu.VMEM(a.shape, a.dtype) for a in (*operands, *outs)),
            pltpu.VMEM((full, LANES), F32),
            pltpu.VMEM((full, LANES), F32),
            pltpu.VMEM((9, full // 4 + SUB, LANES), F32),
            pltpu.VMEM((SUB * SUB * ROWS_OUT, LANES), F32),
            pltpu.VMEM((count * ROWS_OUT, LANES), F32),
            pltpu.SemaphoreType.DMA((len(operands),)),
            pltpu.SemaphoreType.DMA((len(outs),)),
        ],
        operands,
        flops=48 * 10**6,
        moved=4 * 10**6,
        space=pltpu.HBM,
        vmem=VMEM_FIRST,
    )

    def exchange(x, rows):
        x = x.reshape(count, rows // 2, 2, LANES)
        return lax.all_to_all(x, "seq", split_axis=0, concat_axis=0, tiled=True)

    arrived = exchange(message, ROWS_OUT).reshape(count * ROWS_OUT, LANES)
    head = lax.ppermute(head, "seq", [(i + 1, i) for i in range(count - 1)])
    (own_out,) = call(
        forward_kernel,
        "forward",
        [shape(full)],
        [],
        (gated, par),
        flops=10 * 10**6,
        moved=10**6,
    )
    arrived, own_out, head = lax.optimization_barrier((arrived, own_out, head))
    (back,) = call(
        functools.partial(owner_kernel, count, scale),
        "owner",
        [shape(count * ROWS_BACK, BF16)],
        [
            pltpu.VMEM(((count + 1) * ROWS_OUT, LANES), F32),
            pltpu.VMEM((count * ROWS_BACK, LANES), F32),
            pltpu.VMEM((3, count, SUB * LANES), F32),
            pltpu.VMEM((count * SUB, LANES), F32),
            pltpu.VMEM((SUB, LANES), F32),
        ],
        (index.reshape(1), arrived, rates.T, residues.T, taps_short.T),
        flops=2 * 10**6,
        moved=10**6,
    )
    returned = exchange(back, ROWS_BACK)
    poles = returned[:, 2].reshape(2 * count, LANES)
    returned = returned.reshape(count * ROWS_BACK, LANES)

    def other(x, bit):
        return lax.ppermute(x, "chan", [(i, i ^ bit) for i in range(chans)])

    swap = [
        pltpu.VMEM((count * ROWS_BACK, LANES), F32),
        pltpu.VMEM((SUB * POLES, LANES), F32),
    ]
    near = other(poles, 1)
    query, extra_gate, grad_short = call(
        query_kernel,
        "query",
        [shape(channels, BF16), shape(halo), shape(TAPS, F32, channels)],
        [*swap, pltpu.VMEM((full, LANES), F32), pltpu.VMEM((edge, LANES), F32)],
        (returned, own_out, vt, par, cotangent),
        flops=5 * 10**6,
        moved=10**6,
    )
    near, query = lax.optimization_barrier((near, query))
    near = (poles.astype(F32) + near.astype(F32)).astype(BF16)
    far = other(near, 3)
    grad_k, grad_v, grad_q = call(
        key_kernel,
        "key",
        [shape(channels, BF16)] * 3,
        [
            *swap,
            pltpu.VMEM((full, LANES), F32),
            pltpu.VMEM((full, LANES), F32),
            pltpu.SemaphoreType.DMA,
        ],
        (returned, gate, local, vt, extra_gate, head, par, query),
        flops=8 * 10**6,
        moved=2 * 10**6,
        last=pltpu.HBM,
    )
    (grad_residues,) = call(
        pole_kernel,
        "poles",
        [shape(POLES, F32, channels)],
        [pltpu.VMEM((2 * count, LANES), F32)],
        (near, far),
        flops=10**5,
        moved=10**5,
    )
    return grad_q, grad_k, grad_v, grad_short.T, grad_residues.T


def solution(mesh):
    streams = P("chan", "seq")
    return jax.shard_map(
        per_device,
        mesh=mesh,
        in_specs=(streams,) * 4 + (P("chan", None), P(), P()),
        out_specs=(streams,) * 3 + (P("chan", None), P()),
        check_vma=False,
    )
```

```python
import functools

import jax
import jax.numpy as jnp
from jax import lax
from jax.experimental import pallas as pl
from jax.experimental.pallas import tpu as pltpu
from jax.sharding import PartitionSpec as P

F32 = jnp.float32
BF16 = jnp.bfloat16
LANES = 128
SUB = 8
LEN = 128
POLES = 16
TAPS = 7
HALO = TAPS - 1
EDGE = 8
ROWS_OUT = 24
FIR_TERMS = tuple((n, q) for n in range(9) for q in range(2) if (n, q) != (8, 1))
BACK_MODES, BACK_UNROLL, AHEAD_MODES, AHEAD_UNROLL = 8, 16, 2, 32
ROW_SHORT, ROW_V, ROW_MOMENT, ROW_K, ROW_Z = 6, 7, 8, 22, 23
ROWS_BACK = 8
VMEM = 48 * 1024 * 1024
VMEM_FIRST = 62 * 1024 * 1024


def one_minus_exp(x):
    series = 1.0 - x * (1.0 / 7.0)
    for order in (6.0, 5.0, 4.0, 3.0, 2.0):
        series = 1.0 - x * (1.0 / order) * series
    return x * series


def tile(index):
    if isinstance(index, int):
        return pl.ds(SUB * index, SUB)
    return pl.ds(pl.multiple_of(SUB * index, SUB), SUB)


def across(block):
    return pl.ds(block, LEN, stride=SUB)


def lane_group():
    return lax.broadcasted_iota(jnp.int32, (SUB, LANES), 1) // 16


def skewed(x, way):
    row = lax.broadcasted_iota(jnp.int32, (SUB, LANES), 0)
    lane = lax.broadcasted_iota(jnp.int32, (SUB, LANES), 1)
    return jnp.take_along_axis(x, (lane + way * 16 * row) % LANES, axis=1)


def turned(x, way):
    row = lax.broadcasted_iota(jnp.int32, (SUB, LANES), 0)
    return jnp.take_along_axis(x, (row + way * lane_group()) % SUB, axis=0)


def to_owner(x):
    return skewed(turned(skewed(x, -1), 1), -1)


def from_owner(x):
    return skewed(turned(skewed(x, 1), -1), 1)


def decay_of(par, r):
    return par[tile(r), :]


def coef_of(par, r):
    return par[tile(POLES + r), :]


def add_in_order(terms):
    return functools.reduce(lambda a, b: a + b, terms)


def tap_of(par, j):
    return par[tile(2 * POLES + j), :]


def add_up(terms):
    terms = list(terms)
    while len(terms) > 1:
        terms = [a + b for a, b in zip(terms[0::2], terms[1::2])]
    return terms[0]


def key_sums(now, before):
    even = (now[0], now[1] - now[0], before[0] - now[0])
    odd = (now[2], now[3] - now[2], now[1] - now[2])
    earlier = (before[1], before[0] - before[1], before[2] - before[1])
    return [x for e, o, p in zip(even, odd, earlier) for x in (e, o - e, p - e)]


def correlate(sums, u, keys):
    lines = (
        (u[0] + u[1], u[2] + u[3]),
        (u[1], u[3]),
        (u[0], u[2]),
    )
    factors = []
    for even, odd in lines:
        factors += [even + odd, odd, even]
    return [
        total + factors[line] * keys[q][line]
        for total, (line, q) in zip(sums, FIR_TERMS)
    ]


def moments(sums):
    part = dict(zip(FIR_TERMS, sums))
    lines = []
    for n in range(3):
        line = []
        for q in range(2):
            line.append(part[3 * n, q] + part[3 * n + 1, q])
            if (3 * n + 2, q) in part:
                line.append(part[3 * n + 2, q] + part[3 * n, q])
        lines.append(line)
    both, odd, even = lines
    out = []
    for j in range(TAPS):
        n = j // 2
        out.append(both[n] + (even[n] if j % 2 else odd[n]))
    return out


def scan_down(par, z, v, gated, keys, local, gather):
    zero = jnp.zeros((SUB, LANES), F32)
    terms = len(FIR_TERMS)

    def keys_of(m):
        return tuple(keys[n, tile(m + 1), :] for n in range(9))

    for first in range(0, POLES, BACK_MODES):
        modes = range(first, first + BACK_MODES)
        decay = [decay_of(par, r) for r in modes]
        coef = [coef_of(par, r) for r in modes]

        def back_step(i, state, first=first, decay=decay, coef=coef):
            at = tile(LEN - 1 - i)
            z_now, g_now = z[at, :], gated[at, :]
            after, parts = [], []
            for (back, pole), d, c in zip(state, decay, coef):
                back = back * d + z_now
                after.append((back, pole + g_now * back))
                parts.append(c * back)
            total = add_up(parts)
            local[at, :] = total if first == 0 else local[at, :] + total
            return tuple(after)

        state = lax.fori_loop(
            0, LEN, back_step, ((zero, zero),) * BACK_MODES, unroll=BACK_UNROLL
        )
        for (back, pole), r in zip(state, modes):
            half, slot = divmod(r, SUB)
            gather[tile((2 + half) * SUB + slot), :] = back
            gather[tile((4 + half) * SUB + slot), :] = pole

    for first in range(0, POLES, AHEAD_MODES):
        modes = range(first, first + AHEAD_MODES)
        decay = [decay_of(par, r) for r in modes]

        def ahead_step(i, carry, decay=decay):
            state, now = carry
            m = LEN // 4 - 1 - i
            at = [tile(4 * m + n) for n in range(4)]
            before = keys_of(m - 1)
            keyed = (now, before)
            after = []
            for (power, sums), d in zip(state, decay):
                u = [None] * 4
                for p in reversed(range(4)):
                    u[p] = power * v[at[p], :]
                    power = power * d
                after.append((power, tuple(correlate(sums, u, keyed))))
            return tuple(after), before

        state = tuple((d, (zero,) * terms) for d in decay)
        carry = (state, keys_of(LEN // 4 - 1))
        state, _ = lax.fori_loop(0, LEN // 4, ahead_step, carry, unroll=AHEAD_UNROLL)
        for (_, sums), r in zip(state, modes):
            half, slot = divmod(r, SUB)
            taken = moments(sums)
            ahead = add_in_order(tap_of(par, j) * value for j, value in enumerate(taken))
            gather[tile(half * SUB + slot), :] = ahead
            for j, value in enumerate(taken):
                gather[tile((ROW_MOMENT + 2 * j + half) * SUB + slot), :] = value

    def step(m, carry):
        sums, before = carry
        at = [tile(4 * m + n) for n in range(4)]
        now = keys_of(m)
        u = [local[p, :] * v[p, :] for p in at]
        return tuple(correlate(sums, u, (now, before))), now

    sums, _ = lax.fori_loop(0, LEN // 4, step, ((zero,) * terms, keys_of(-1)), unroll=8)
    for j, value in enumerate(moments(sums)):
        gather[tile(ROW_SHORT * SUB + j), :] = value


def first_kernel(*refs):
    sources, targets, refs = refs[:7], refs[7:14], refs[14:]
    (k, v, q, cot, rates, residues, amounts), refs = refs[:7], refs[7:]
    (vt, gate, gated, local, par, head, message), refs = refs[:7], refs[7:]
    kt, zt, keys, gather, spread, came, went = refs
    copies = [
        pltpu.make_async_copy(a, b, came.at[n])
        for n, (a, b) in enumerate(zip(sources, (k, v, q, cot, rates, residues, amounts)))
    ]
    leaving = [
        pltpu.make_async_copy(a, b, went.at[n])
        for n, (a, b) in enumerate(zip((vt, gate, gated, local, par, head, message), targets))
    ]
    for copy in copies:
        copy.start()
    copies[0].wait()
    for s in range(SUB):
        kt[across(s), :] = k[s * LANES : (s + 1) * LANES, :].astype(F32).T
    copies[1].wait()
    for s in range(SUB):
        vt[across(s), :] = v[s * LANES : (s + 1) * LANES, :].astype(F32).T
    leaving[0].start()
    for copy in copies[2:]:
        copy.wait()
    for s in range(SUB):
        rows = slice(s * LANES, (s + 1) * LANES)
        zt[across(s), :] = (q[rows, :].astype(F32) * cot[rows, :].astype(F32)).T
        rate = rates[:, rows]
        par[pl.ds(s, POLES, stride=SUB), :] = jnp.exp(-rate)
        par[pl.ds(SUB * POLES + s, POLES, stride=SUB), :] = residues[:, rows] * jnp.sqrt(
            one_minus_exp(2.0 * rate)
        )
        par[pl.ds(2 * SUB * POLES + s, TAPS, stride=SUB), :] = amounts[:, rows]
    edge = SUB * EDGE
    head[0:edge, :] = zt[0:edge, :]
    head[edge:, :] = vt[0:edge, :]
    for n in (4, 5):
        leaving[n].start()
    for row, block in (
        (ROW_V, vt[0:edge, :]),
        (ROW_K, kt[SUB * (LEN - EDGE) : SUB * LEN, :]),
        (ROW_Z, zt[0:edge, :]),
    ):
        gather[row * edge : (row + 1) * edge, :] = block

    taps = [tap_of(par, j) for j in range(TAPS)]

    def prepare(m, before):
        at = [tile(4 * m + n) for n in range(4)]
        now = [kt[p, :] for p in at]
        line = [*reversed(now), *before]
        for n in range(4):
            total = add_in_order(taps[j] * line[3 - n + j] for j in range(TAPS))
            gate[at[n], :] = total
            gated[at[n], :] = total * vt[at[n], :]
        for n, value in enumerate(key_sums(now, before)):
            keys[n, tile(m + 1), :] = value
        return tuple(line[:HALO])

    gather[tile(ROW_SHORT * SUB + TAPS), :] = jnp.zeros((SUB, LANES), F32)
    zero = gather[tile(ROW_SHORT * SUB + TAPS), :]
    for n in range(9):
        keys[n, tile(0), :] = zero
    lax.fori_loop(0, LEN // 4, prepare, (zero,) * HALO, unroll=2)
    leaving[1].start()
    leaving[2].start()
    scan_down(par, zt, vt, gated, keys, local, gather)
    leaving[3].start()
    for row in range(ROWS_OUT):
        for s in range(SUB):
            block = to_owner(gather[pl.ds(row * SUB * SUB + s, SUB, stride=SUB), :])
            spread[pl.ds(s * SUB * ROWS_OUT + row, SUB, stride=ROWS_OUT), :] = block
    message[...] = spread[...].astype(BF16)
    leaving[6].start()
    for copy in leaving:
        copy.wait()


def owner_kernel(
    count, scale, index, arrived, rate_rows, residue_rows, tap_rows, out, x, y, kept, fix, mine
):
    x[0:ROWS_OUT, :] = jnp.zeros((ROWS_OUT, LANES), F32)
    x[ROWS_OUT:, :] = arrived[...].astype(F32)
    even = lax.broadcasted_iota(jnp.int32, (SUB, LANES), 0) % 2 == 0
    group = lane_group()
    zero = jnp.zeros((SUB, LANES), F32)

    block = pl.ds(pl.multiple_of((index[0] // SUB) * LANES, LANES), LANES)
    place = index[0] % SUB
    for n, ref in enumerate((rate_rows, residue_rows)):
        for half in range(2):
            mine[...] = to_owner(ref[half * SUB : (half + 1) * SUB, block])
            fix[2 * n + half : 2 * n + half + 1, :] = mine[pl.ds(place, 1), :]
    held = jnp.where(group[0:TAPS, :] == (SUB - place) % SUB, tap_rows[:, block], 0.0)
    for shift in (16, 32, 64):
        held = held + pltpu.roll(held, shift, 1)
    taps = [jnp.broadcast_to(held[j : j + 1, :], (SUB, LANES)) for j in range(TAPS)]

    def pattern(ref, row):
        return jnp.where(even, ref[pl.ds(row, 1), :], ref[pl.ds(row + 1, 1), :])

    rate = pattern(fix, 0)
    weight = jnp.sqrt(one_minus_exp(2.0 * rate))
    coef = pattern(fix, 2) * weight
    leap = jnp.exp(-float(LEN) * rate)
    rates = [fix[pl.ds(half, 1), :] for half in range(2)]
    growth = [jnp.broadcast_to(jnp.exp(r), (SUB, LANES)) for r in rates]
    powers = [
        [jnp.broadcast_to(jnp.exp(-float(LEN - t) * r), (SUB, LANES)) for t in range(HALO)]
        for r in rates
    ]

    source = lax.broadcasted_iota(jnp.int32, (LANES, SUB * LANES), 0)
    target = lax.broadcasted_iota(jnp.int32, (LANES, SUB * LANES), 1)
    same = (source // 16 == target // LANES) & (source % 16 == target % 16)
    everywhere = jnp.where(same, 1.0, 0.0).astype(BF16)
    for n, (row, first) in enumerate(((ROW_V, 1), (ROW_Z, 1), (ROW_K, 0))):
        rows = x[pl.ds(first * ROWS_OUT + row, count, stride=ROWS_OUT), :].astype(BF16)
        kept[n] = jnp.dot(rows, everywhere, preferred_element_type=F32)

    def edge_of(b):
        at = pl.ds(b * SUB, SUB)
        value, slope = (
            [kept[n, at, t * LANES : (t + 1) * LANES] for t in range(HALO)] for n in range(2)
        )
        key = [kept[2, at, (EDGE - m) * LANES : (EDGE - m + 1) * LANES] for m in range(1, TAPS)]
        return value, slope, [None, *key]

    def shards(row, b):
        return pl.ds((b * SUB + 1) * ROWS_OUT + row, SUB, stride=ROWS_OUT)

    fix[...] = jnp.zeros(fix.shape, F32)
    batches = count // SUB
    poles = [zero, zero]
    for b in range(batches):
        value, slope, key = edge_of(b)
        extra = [
            value[t] * add_in_order(taps[j] * key[j - t] for j in range(t + 1, TAPS))
            for t in range(HALO)
        ]
        for half in range(2):
            back = x[shards(2 + half, b), :]
            fix[pl.ds(b * SUB * SUB + half, SUB, stride=SUB), :] = add_in_order(
                extra[t] * powers[half][t] for t in range(HALO)
            )
            for t in range(HALO):
                poles[half] = poles[half] + extra[t] * back
                if t < HALO - 1:
                    back = (back - slope[t]) * growth[half]

    ahead, pole, total = zero, zero, zero
    for d in range(count):
        base = (d + 1) * ROWS_OUT
        y[pl.ds(d * ROWS_BACK, 2), :] = ahead[0:2, :]
        now = x[pl.ds(base, SUB), :]
        pole = pole + ahead * pattern(x, base + 2)
        total = total + now
        ahead = ahead * leap + (now + fix[tile(d), :])
    back, low, high = zero, zero, zero
    for d in reversed(range(count)):
        base = (d + 1) * ROWS_OUT
        y[pl.ds(d * ROWS_BACK + 2, 2), :] = back[0:2, :]
        low = low + back * x[pl.ds(base + SUB, SUB), :]
        high = high + back * x[pl.ds(base + 2 * SUB, SUB), :]
        back = back * leap + pattern(x, base + 2)

    edges = [[zero] * TAPS for _ in range(2)]
    for b in range(batches):
        value, slope, key = edge_of(b)
        start = b * SUB
        states = []
        for half in range(2):
            own = x[shards(2 + half, b), :]
            later = y[pl.ds(start * ROWS_BACK + 2 + half, SUB, stride=ROWS_BACK), :]
            states.append(own + later * powers[half][0])
        for t in range(HALO):
            for j in range(t + 1, TAPS):
                product = value[t] * key[j - t]
                for half in range(2):
                    edges[half][j] = edges[half][j] + states[half] * product
            states = [(a - slope[t]) * g for a, g in zip(states, growth)]

    def down(rows):
        return jnp.sum(rows, axis=0, keepdims=True)

    owned = jnp.concatenate([down(p) for p in poles])
    owned = (owned + pole[0:2, :] + total[4:6, :]) * weight[0:2, :] * scale
    short = total[ROW_SHORT : ROW_SHORT + 1, :]
    group = group[0:1, :]
    for part, first in ((low * coef, 0), (high * coef, 4)):
        part = part + pltpu.roll(part, SUB - 1, 0)
        for shift in (16, 32, 64):
            part = part + pltpu.roll(part, shift, 1)
        for n in range(min(4, TAPS - first)):
            short = short + jnp.where(group == first + n, part[2 * n : 2 * n + 1, :], 0.0)
    for j in range(1, TAPS):
        part = down(edges[0][j]) * coef[0:1, :] + down(edges[1][j]) * coef[1:2, :]
        for shift in (16, 32, 64):
            part = part + pltpu.roll(part, shift, 1)
        short = short + jnp.where(group == j, part, 0.0)
    short = short * scale
    for d in range(count):
        y[pl.ds(d * ROWS_BACK + 4, 2), :] = owned
        y[pl.ds(d * ROWS_BACK + 6, 1), :] = short
        y[pl.ds(d * ROWS_BACK + 7, 1), :] = x[pl.ds(d * ROWS_OUT + ROW_K, 1), :]
    out[...] = y[...].astype(BF16)


def forward_kernel(gated, par, own_out):
    half = POLES // 2
    for part in range(2):
        modes = range(part * half, (part + 1) * half)
        decay = [decay_of(par, r) for r in modes]
        coef = [coef_of(par, r) for r in modes]
        ahead = (jnp.zeros((SUB, LANES), F32),) * half

        def forward(i, ahead, part=part, decay=decay, coef=coef):
            now = gated[tile(i), :]
            total = None if part == 0 else own_out[tile(i), :]
            after = []
            for h, d, c in zip(ahead, decay, coef):
                h = h + now
                term = c * h
                total = term if total is None else total + term
                after.append(h * d)
            own_out[tile(i), :] = total
            return tuple(after)

        lax.fori_loop(0, LEN, forward, ahead, unroll=16)


def halo_gates(last, par):
    return [
        add_in_order(tap_of(par, j) * last[tile(EDGE + t - j), :] for j in range(t + 1, TAPS))
        for t in range(HALO)
    ]


def unpack(arrived, x, state, first):
    x[...] = arrived[...].astype(F32)
    for s in range(SUB):
        for row in range(2):
            block = x[pl.ds(s * SUB * ROWS_BACK + first + row, SUB, stride=ROWS_BACK), :]
            state[pl.ds(row * SUB * SUB + s, SUB, stride=SUB), :] = from_owner(block)


def query_kernel(
    arrived, own_out, vt, par, cot, grad_q, extra_gate, grad_short, x, state, long_out, last
):
    unpack(arrived, x, state, 0)
    for s in range(SUB):
        short = x[pl.ds(s * SUB * ROWS_BACK + 6, SUB, stride=ROWS_BACK), :]
        grad_short[:, s * LANES : (s + 1) * LANES] = from_owner(short)[0:TAPS, :]
        keys = x[pl.ds(s * SUB * ROWS_BACK + 7, SUB, stride=ROWS_BACK), :]
        last[pl.ds(s, SUB, stride=SUB), :] = from_owner(keys)
    decay = [decay_of(par, r) for r in range(POLES)]

    def forward(t, terms):
        long_out[tile(t), :] = own_out[tile(t), :] + add_up(terms)
        return tuple(q * d for q, d in zip(terms, decay))

    terms = tuple(coef_of(par, r) * state[tile(r), :] for r in range(POLES))
    gates = halo_gates(last, par)
    for t in range(EDGE):
        if t < HALO:
            extra_gate[tile(t), :] = gates[t]
            extra = gates[t] * vt[tile(t), :]
            terms = tuple(q + coef_of(par, r) * extra for r, q in enumerate(terms))
        terms = forward(t, terms)
    lax.fori_loop(EDGE, LEN, forward, terms, unroll=24)
    for s in range(SUB):
        rows = slice(s * LANES, (s + 1) * LANES)
        grad_q[rows, :] = (cot[rows, :].astype(F32) * long_out[across(s), :].T).astype(BF16)


def key_kernel(
    arrived, gate, local, vt, extra_gate, head, par, query,
    grad_k, grad_v, grad_q, x, state, slope, vals, gone,
):
    leaving = pltpu.make_async_copy(query, grad_q, gone)
    leaving.start()
    unpack(arrived, x, state, 2)
    decay = [decay_of(par, r) for r in range(POLES)]
    back = [state[tile(r), :] for r in range(POLES)]
    growth = [1.0 / d for d in decay]
    ahead = []
    for n in range(HALO):
        ahead.append(
            add_up(coef_of(par, r) * back[r] for r in range(POLES)) * head[tile(EDGE + n), :]
        )
        if n < HALO - 1:
            z_now = head[tile(n), :]
            back = [(b - z_now) * g for b, g in zip(back, growth)]
    taps = [tap_of(par, j) for j in range(TAPS)]

    def backward(i, carry, extra=None):
        terms, ahead = carry
        t = LEN - 1 - i
        terms = tuple(q * d for q, d in zip(terms, decay))
        total = local[tile(t), :] + add_up(terms)
        now = gate[tile(t), :]
        vals[tile(t), :] = total * (now if extra is None else now + extra)
        slopes = (total * vt[tile(t), :], *ahead)
        slope[tile(t), :] = add_in_order(taps[j] * slopes[j] for j in range(TAPS))
        return terms, slopes[:HALO]

    terms = tuple(coef_of(par, r) * state[tile(r), :] for r in range(POLES))
    carry = (terms, tuple(ahead))
    carry = lax.fori_loop(0, LEN - EDGE, backward, carry, unroll=24)
    for t in reversed(range(EDGE)):
        extra = extra_gate[tile(t), :] if t < HALO else None
        carry = backward(LEN - 1 - t, carry, extra)
    for s in range(SUB):
        rows = slice(s * LANES, (s + 1) * LANES)
        grad_k[rows, :] = slope[across(s), :].T.astype(BF16)
        grad_v[rows, :] = vals[across(s), :].T.astype(BF16)
    leaving.wait()


def pole_kernel(*refs):
    *parts, out, x = refs
    x[...] = add_up([part[...].astype(F32) for part in parts])
    for s in range(SUB):
        for half in range(2):
            block = x[pl.ds(s * SUB * 2 + half, SUB, stride=2), :]
            out[half * SUB : (half + 1) * SUB, s * LANES : (s + 1) * LANES] = from_owner(block)


def call(
    kernel, name, outs, scratch, operands, flops=0, moved=0, space=pltpu.VMEM, vmem=VMEM, last=None
):
    spaces = [space] * (len(outs) - 1) + [last or space]
    return pl.pallas_call(
        kernel,
        out_shape=outs,
        in_specs=[
            pl.BlockSpec(memory_space=pltpu.SMEM if a.dtype == jnp.int32 else space)
            for a in operands
        ],
        out_specs=[pl.BlockSpec(memory_space=s) for s in spaces],
        scratch_shapes=scratch,
        compiler_params=pltpu.CompilerParams(vmem_limit_bytes=vmem),
        cost_estimate=pl.CostEstimate(flops=flops, bytes_accessed=moved, transcendentals=0),
        name=name,
    )(*operands)


def shape(rows, dtype=F32, lanes=LANES):
    return jax.ShapeDtypeStruct((rows, lanes), dtype)


def per_device(q_in, k_in, v_in, cotangent, taps_short, residues, rates):
    channels, length = q_in.shape
    count = lax.axis_size("seq")
    index = lax.axis_index("seq")
    chans = lax.axis_size("chan")
    assert (channels, length, count) == (SUB * LANES, LEN, SUB * SUB)
    scale = (length * count) ** (-0.5)
    full, edge, halo = SUB * LEN, SUB * EDGE, SUB * HALO

    operands = (k_in, v_in, q_in, cotangent, rates.T, residues.T, taps_short.T)
    outs = [shape(full)] * 4 + [shape(SUB * 40), shape(2 * edge)]
    outs.append(shape(count * ROWS_OUT, BF16))
    vt, gate, gated, local, par, head, message = call(
        first_kernel,
        "first",
        outs,
        [
            *(pltpu.VMEM(a.shape, a.dtype) for a in (*operands, *outs)),
            pltpu.VMEM((full, LANES), F32),
            pltpu.VMEM((full, LANES), F32),
            pltpu.VMEM((9, full // 4 + SUB, LANES), F32),
            pltpu.VMEM((SUB * SUB * ROWS_OUT, LANES), F32),
            pltpu.VMEM((count * ROWS_OUT, LANES), F32),
            pltpu.SemaphoreType.DMA((len(operands),)),
            pltpu.SemaphoreType.DMA((len(outs),)),
        ],
        operands,
        flops=48 * 10**6,
        moved=4 * 10**6,
        space=pltpu.HBM,
        vmem=VMEM_FIRST,
    )

    def exchange(x, rows):
        x = x.reshape(count, rows // 2, 2, LANES)
        return lax.all_to_all(x, "seq", split_axis=0, concat_axis=0, tiled=True)

    arrived = exchange(message, ROWS_OUT).reshape(count * ROWS_OUT, LANES)
    head = lax.ppermute(head, "seq", [(i + 1, i) for i in range(count - 1)])
    (own_out,) = call(
        forward_kernel,
        "forward",
        [shape(full)],
        [],
        (gated, par),
        flops=10 * 10**6,
        moved=10**6,
    )
    arrived, own_out, head = lax.optimization_barrier((arrived, own_out, head))
    (back,) = call(
        functools.partial(owner_kernel, count, scale),
        "owner",
        [shape(count * ROWS_BACK, BF16)],
        [
            pltpu.VMEM(((count + 1) * ROWS_OUT, LANES), F32),
            pltpu.VMEM((count * ROWS_BACK, LANES), F32),
            pltpu.VMEM((3, count, SUB * LANES), F32),
            pltpu.VMEM((count * SUB, LANES), F32),
            pltpu.VMEM((SUB, LANES), F32),
        ],
        (index.reshape(1), arrived, rates.T, residues.T, taps_short.T),
        flops=2 * 10**6,
        moved=10**6,
    )
    returned = exchange(back, ROWS_BACK)
    poles = returned[:, 2].reshape(2 * count, LANES)
    returned = returned.reshape(count * ROWS_BACK, LANES)

    others = [
        lax.ppermute(poles, "chan", [(i, i ^ bits) for i in range(chans)]) for bits in (2, 1, 3)
    ]

    swap = [
        pltpu.VMEM((count * ROWS_BACK, LANES), F32),
        pltpu.VMEM((SUB * POLES, LANES), F32),
    ]
    query, extra_gate, grad_short = call(
        query_kernel,
        "query",
        [shape(channels, BF16), shape(halo), shape(TAPS, F32, channels)],
        [*swap, pltpu.VMEM((full, LANES), F32), pltpu.VMEM((edge, LANES), F32)],
        (returned, own_out, vt, par, cotangent),
        flops=5 * 10**6,
        moved=10**6,
    )
    grad_k, grad_v, grad_q = call(
        key_kernel,
        "key",
        [shape(channels, BF16)] * 3,
        [
            *swap,
            pltpu.VMEM((full, LANES), F32),
            pltpu.VMEM((full, LANES), F32),
            pltpu.SemaphoreType.DMA,
        ],
        (returned, gate, local, vt, extra_gate, head, par, query),
        flops=8 * 10**6,
        moved=2 * 10**6,
        last=pltpu.HBM,
    )
    grad_k, *others = lax.optimization_barrier((grad_k, *others))
    (grad_residues,) = call(
        pole_kernel,
        "poles",
        [shape(POLES, F32, channels)],
        [pltpu.VMEM((2 * count, LANES), F32)],
        (poles, *others),
        flops=10**5,
        moved=10**5,
    )
    return grad_q, grad_k, grad_v, grad_short.T, grad_residues.T


def solution(mesh):
    streams = P("chan", "seq")
    return jax.shard_map(
        per_device,
        mesh=mesh,
        in_specs=(streams,) * 4 + (P("chan", None), P(), P()),
        out_specs=(streams,) * 3 + (P("chan", None), P()),
        check_vma=False,
    )
```

```python
import functools

import jax
import jax.numpy as jnp
from jax import lax
from jax.experimental import pallas as pl
from jax.experimental.pallas import tpu as pltpu
from jax.sharding import PartitionSpec as P

F32 = jnp.float32
BF16 = jnp.bfloat16
LANES = 128
SUB = 8
LEN = 128
POLES = 16
TAPS = 7
HALO = TAPS - 1
EDGE = 8
ROWS_OUT = 24
FIR_TERMS = tuple((n, q) for n in range(9) for q in range(2) if (n, q) != (8, 1))
BACK_MODES, BACK_UNROLL, AHEAD_MODES, AHEAD_UNROLL = 8, 16, 2, 32
ROW_SHORT, ROW_V, ROW_MOMENT, ROW_K, ROW_Z = 6, 7, 8, 22, 23
ROWS_BACK = 8
VMEM = 48 * 1024 * 1024
VMEM_FIRST = 62 * 1024 * 1024


def one_minus_exp(x):
    series = 1.0 - x * (1.0 / 7.0)
    for order in (6.0, 5.0, 4.0, 3.0, 2.0):
        series = 1.0 - x * (1.0 / order) * series
    return x * series


def tile(index):
    if isinstance(index, int):
        return pl.ds(SUB * index, SUB)
    return pl.ds(pl.multiple_of(SUB * index, SUB), SUB)


def across(block):
    return pl.ds(block, LEN, stride=SUB)


def lane_group():
    return lax.broadcasted_iota(jnp.int32, (SUB, LANES), 1) // 16


def skewed(x, way):
    row = lax.broadcasted_iota(jnp.int32, (SUB, LANES), 0)
    lane = lax.broadcasted_iota(jnp.int32, (SUB, LANES), 1)
    return jnp.take_along_axis(x, (lane + way * 16 * row) % LANES, axis=1)


def turned(x, way):
    row = lax.broadcasted_iota(jnp.int32, (SUB, LANES), 0)
    return jnp.take_along_axis(x, (row + way * lane_group()) % SUB, axis=0)


def to_owner(x):
    return skewed(turned(skewed(x, -1), 1), -1)


def from_owner(x):
    return skewed(turned(skewed(x, 1), -1), 1)


def decay_of(par, r):
    return par[tile(r), :]


def coef_of(par, r):
    return par[tile(POLES + r), :]


def add_in_order(terms):
    return functools.reduce(lambda a, b: a + b, terms)


def tap_of(par, j):
    return par[tile(2 * POLES + j), :]


def add_up(terms):
    terms = list(terms)
    while len(terms) > 1:
        terms = [a + b for a, b in zip(terms[0::2], terms[1::2])]
    return terms[0]


def key_sums(now, before):
    even = (now[0], now[1] - now[0], before[0] - now[0])
    odd = (now[2], now[3] - now[2], now[1] - now[2])
    earlier = (before[1], before[0] - before[1], before[2] - before[1])
    return [x for e, o, p in zip(even, odd, earlier) for x in (e, o - e, p - e)]


def correlate(sums, u, keys):
    lines = (
        (u[0] + u[1], u[2] + u[3]),
        (u[1], u[3]),
        (u[0], u[2]),
    )
    factors = []
    for even, odd in lines:
        factors += [even + odd, odd, even]
    return [
        total + factors[line] * keys[q][line]
        for total, (line, q) in zip(sums, FIR_TERMS)
    ]


def moments(sums):
    part = dict(zip(FIR_TERMS, sums))
    lines = []
    for n in range(3):
        line = []
        for q in range(2):
            line.append(part[3 * n, q] + part[3 * n + 1, q])
            if (3 * n + 2, q) in part:
                line.append(part[3 * n + 2, q] + part[3 * n, q])
        lines.append(line)
    both, odd, even = lines
    out = []
    for j in range(TAPS):
        n = j // 2
        out.append(both[n] + (even[n] if j % 2 else odd[n]))
    return out


def scan_down(par, z, v, gated, keys, local, gather):
    zero = jnp.zeros((SUB, LANES), F32)
    terms = len(FIR_TERMS)

    def keys_of(m):
        return tuple(keys[n, tile(m + 1), :] for n in range(9))

    for first in range(0, POLES, BACK_MODES):
        modes = range(first, first + BACK_MODES)
        decay = [decay_of(par, r) for r in modes]
        coef = [coef_of(par, r) for r in modes]

        def back_step(i, state, first=first, decay=decay, coef=coef):
            at = tile(LEN - 1 - i)
            z_now, g_now = z[at, :], gated[at, :]
            after, parts = [], []
            for (back, pole), d, c in zip(state, decay, coef):
                back = back * d + z_now
                after.append((back, pole + g_now * back))
                parts.append(c * back)
            total = add_up(parts)
            local[at, :] = total if first == 0 else local[at, :] + total
            return tuple(after)

        state = lax.fori_loop(
            0, LEN, back_step, ((zero, zero),) * BACK_MODES, unroll=BACK_UNROLL
        )
        for (back, pole), r in zip(state, modes):
            half, slot = divmod(r, SUB)
            gather[tile((2 + half) * SUB + slot), :] = back
            gather[tile((4 + half) * SUB + slot), :] = pole

    for first in range(0, POLES, AHEAD_MODES):
        modes = range(first, first + AHEAD_MODES)
        decay = [decay_of(par, r) for r in modes]

        def ahead_step(i, carry, decay=decay):
            state, now = carry
            m = LEN // 4 - 1 - i
            at = [tile(4 * m + n) for n in range(4)]
            before = keys_of(m - 1)
            keyed = (now, before)
            after = []
            for (power, sums), d in zip(state, decay):
                u = [None] * 4
                for p in reversed(range(4)):
                    u[p] = power * v[at[p], :]
                    power = power * d
                after.append((power, tuple(correlate(sums, u, keyed))))
            return tuple(after), before

        state = tuple((d, (zero,) * terms) for d in decay)
        carry = (state, keys_of(LEN // 4 - 1))
        state, _ = lax.fori_loop(0, LEN // 4, ahead_step, carry, unroll=AHEAD_UNROLL)
        for (_, sums), r in zip(state, modes):
            half, slot = divmod(r, SUB)
            taken = moments(sums)
            ahead = add_in_order(tap_of(par, j) * value for j, value in enumerate(taken))
            gather[tile(half * SUB + slot), :] = ahead
            for j, value in enumerate(taken):
                gather[tile((ROW_MOMENT + 2 * j + half) * SUB + slot), :] = value

    def step(m, carry):
        sums, before = carry
        at = [tile(4 * m + n) for n in range(4)]
        now = keys_of(m)
        u = [local[p, :] * v[p, :] for p in at]
        return tuple(correlate(sums, u, (now, before))), now

    sums, _ = lax.fori_loop(0, LEN // 4, step, ((zero,) * terms, keys_of(-1)), unroll=8)
    for j, value in enumerate(moments(sums)):
        gather[tile(ROW_SHORT * SUB + j), :] = value


def first_kernel(*refs):
    sources, targets, refs = refs[:7], refs[7:14], refs[14:]
    (k, v, q, cot, rates, residues, amounts), refs = refs[:7], refs[7:]
    (vt, gate, gated, local, par, head, message), refs = refs[:7], refs[7:]
    kt, zt, keys, gather, spread, came, went = refs
    copies = [
        pltpu.make_async_copy(a, b, came.at[n])
        for n, (a, b) in enumerate(zip(sources, (k, v, q, cot, rates, residues, amounts)))
    ]
    leaving = [
        pltpu.make_async_copy(a, b, went.at[n])
        for n, (a, b) in enumerate(zip((vt, gate, gated, local, par, head, message), targets))
    ]
    for copy in copies:
        copy.start()
    copies[0].wait()
    for s in range(SUB):
        kt[across(s), :] = k[s * LANES : (s + 1) * LANES, :].astype(F32).T
    copies[1].wait()
    for s in range(SUB):
        vt[across(s), :] = v[s * LANES : (s + 1) * LANES, :].astype(F32).T
    leaving[0].start()
    for copy in copies[2:]:
        copy.wait()
    for s in range(SUB):
        rows = slice(s * LANES, (s + 1) * LANES)
        zt[across(s), :] = (q[rows, :].astype(F32) * cot[rows, :].astype(F32)).T
        rate = rates[:, rows]
        par[pl.ds(s, POLES, stride=SUB), :] = jnp.exp(-rate)
        par[pl.ds(SUB * POLES + s, POLES, stride=SUB), :] = residues[:, rows] * jnp.sqrt(
            one_minus_exp(2.0 * rate)
        )
        par[pl.ds(2 * SUB * POLES + s, TAPS, stride=SUB), :] = amounts[:, rows]
    edge = SUB * EDGE
    head[0:edge, :] = zt[0:edge, :]
    head[edge:, :] = vt[0:edge, :]
    for n in (4, 5):
        leaving[n].start()
    for row, block in (
        (ROW_V, vt[0:edge, :]),
        (ROW_K, kt[SUB * (LEN - EDGE) : SUB * LEN, :]),
        (ROW_Z, zt[0:edge, :]),
    ):
        gather[row * edge : (row + 1) * edge, :] = block

    taps = [tap_of(par, j) for j in range(TAPS)]

    def prepare(m, before):
        at = [tile(4 * m + n) for n in range(4)]
        now = [kt[p, :] for p in at]
        line = [*reversed(now), *before]
        for n in range(4):
            total = add_in_order(taps[j] * line[3 - n + j] for j in range(TAPS))
            gate[at[n], :] = total
            gated[at[n], :] = total * vt[at[n], :]
        for n, value in enumerate(key_sums(now, before)):
            keys[n, tile(m + 1), :] = value
        return tuple(line[:HALO])

    gather[tile(ROW_SHORT * SUB + TAPS), :] = jnp.zeros((SUB, LANES), F32)
    zero = gather[tile(ROW_SHORT * SUB + TAPS), :]
    for n in range(9):
        keys[n, tile(0), :] = zero
    lax.fori_loop(0, LEN // 4, prepare, (zero,) * HALO, unroll=2)
    leaving[1].start()
    leaving[2].start()
    scan_down(par, zt, vt, gated, keys, local, gather)
    leaving[3].start()
    for row in range(ROWS_OUT):
        for s in range(SUB):
            block = to_owner(gather[pl.ds(row * SUB * SUB + s, SUB, stride=SUB), :])
            spread[pl.ds(s * SUB * ROWS_OUT + row, SUB, stride=ROWS_OUT), :] = block
    message[...] = spread[...].astype(BF16)
    leaving[6].start()
    for copy in leaving:
        copy.wait()


def owner_kernel(
    count, scale, index, arrived, rate_rows, residue_rows, tap_rows, out, x, y, kept, fix, mine
):
    x[0:ROWS_OUT, :] = jnp.zeros((ROWS_OUT, LANES), F32)
    x[ROWS_OUT:, :] = arrived[...].astype(F32)
    even = lax.broadcasted_iota(jnp.int32, (SUB, LANES), 0) % 2 == 0
    group = lane_group()
    zero = jnp.zeros((SUB, LANES), F32)

    block = pl.ds(pl.multiple_of((index[0] // SUB) * LANES, LANES), LANES)
    place = index[0] % SUB
    for n, ref in enumerate((rate_rows, residue_rows)):
        for half in range(2):
            mine[...] = to_owner(ref[half * SUB : (half + 1) * SUB, block])
            fix[2 * n + half : 2 * n + half + 1, :] = mine[pl.ds(place, 1), :]
    held = jnp.where(group[0:TAPS, :] == (SUB - place) % SUB, tap_rows[:, block], 0.0)
    for shift in (16, 32, 64):
        held = held + pltpu.roll(held, shift, 1)
    taps = [jnp.broadcast_to(held[j : j + 1, :], (SUB, LANES)) for j in range(TAPS)]

    def pattern(ref, row):
        return jnp.where(even, ref[pl.ds(row, 1), :], ref[pl.ds(row + 1, 1), :])

    rate = pattern(fix, 0)
    weight = jnp.sqrt(one_minus_exp(2.0 * rate))
    coef = pattern(fix, 2) * weight
    leap = jnp.exp(-float(LEN) * rate)
    rates = [fix[pl.ds(half, 1), :] for half in range(2)]
    growth = [jnp.broadcast_to(jnp.exp(r), (SUB, LANES)) for r in rates]
    powers = [
        [jnp.broadcast_to(jnp.exp(-float(LEN - t) * r), (SUB, LANES)) for t in range(HALO)]
        for r in rates
    ]

    source = lax.broadcasted_iota(jnp.int32, (LANES, SUB * LANES), 0)
    target = lax.broadcasted_iota(jnp.int32, (LANES, SUB * LANES), 1)
    same = (source // 16 == target // LANES) & (source % 16 == target % 16)
    everywhere = jnp.where(same, 1.0, 0.0).astype(BF16)
    for n, (row, first) in enumerate(((ROW_V, 1), (ROW_Z, 1), (ROW_K, 0))):
        rows = x[pl.ds(first * ROWS_OUT + row, count, stride=ROWS_OUT), :].astype(BF16)
        kept[n] = jnp.dot(rows, everywhere, preferred_element_type=F32)

    def edge_of(b):
        at = pl.ds(b * SUB, SUB)
        value, slope = (
            [kept[n, at, t * LANES : (t + 1) * LANES] for t in range(HALO)] for n in range(2)
        )
        key = [kept[2, at, (EDGE - m) * LANES : (EDGE - m + 1) * LANES] for m in range(1, TAPS)]
        return value, slope, [None, *key]

    def shards(row, b):
        return pl.ds((b * SUB + 1) * ROWS_OUT + row, SUB, stride=ROWS_OUT)

    fix[...] = jnp.zeros(fix.shape, F32)
    batches = count // SUB
    poles = [zero, zero]
    for b in range(batches):
        value, slope, key = edge_of(b)
        extra = [
            value[t] * add_in_order(taps[j] * key[j - t] for j in range(t + 1, TAPS))
            for t in range(HALO)
        ]
        for half in range(2):
            back = x[shards(2 + half, b), :]
            fix[pl.ds(b * SUB * SUB + half, SUB, stride=SUB), :] = add_in_order(
                extra[t] * powers[half][t] for t in range(HALO)
            )
            for t in range(HALO):
                poles[half] = poles[half] + extra[t] * back
                if t < HALO - 1:
                    back = (back - slope[t]) * growth[half]

    ahead, pole, total = zero, zero, zero
    for d in range(count):
        base = (d + 1) * ROWS_OUT
        y[pl.ds(d * ROWS_BACK, 2), :] = ahead[0:2, :]
        now = x[pl.ds(base, SUB), :]
        pole = pole + ahead * pattern(x, base + 2)
        total = total + now
        ahead = ahead * leap + (now + fix[tile(d), :])
    back, low, high = zero, zero, zero
    for d in reversed(range(count)):
        base = (d + 1) * ROWS_OUT
        y[pl.ds(d * ROWS_BACK + 2, 2), :] = back[0:2, :]
        low = low + back * x[pl.ds(base + SUB, SUB), :]
        high = high + back * x[pl.ds(base + 2 * SUB, SUB), :]
        back = back * leap + pattern(x, base + 2)

    edges = [[zero] * TAPS for _ in range(2)]
    for b in range(batches):
        value, slope, key = edge_of(b)
        start = b * SUB
        states = []
        for half in range(2):
            own = x[shards(2 + half, b), :]
            later = y[pl.ds(start * ROWS_BACK + 2 + half, SUB, stride=ROWS_BACK), :]
            states.append(own + later * powers[half][0])
        for t in range(HALO):
            for j in range(t + 1, TAPS):
                product = value[t] * key[j - t]
                for half in range(2):
                    edges[half][j] = edges[half][j] + states[half] * product
            states = [(a - slope[t]) * g for a, g in zip(states, growth)]

    def down(rows):
        return jnp.sum(rows, axis=0, keepdims=True)

    owned = jnp.concatenate([down(p) for p in poles])
    owned = (owned + pole[0:2, :] + total[4:6, :]) * weight[0:2, :] * scale
    short = total[ROW_SHORT : ROW_SHORT + 1, :]
    group = group[0:1, :]
    for part, first in ((low * coef, 0), (high * coef, 4)):
        part = part + pltpu.roll(part, SUB - 1, 0)
        for shift in (16, 32, 64):
            part = part + pltpu.roll(part, shift, 1)
        for n in range(min(4, TAPS - first)):
            short = short + jnp.where(group == first + n, part[2 * n : 2 * n + 1, :], 0.0)
    for j in range(1, TAPS):
        part = down(edges[0][j]) * coef[0:1, :] + down(edges[1][j]) * coef[1:2, :]
        for shift in (16, 32, 64):
            part = part + pltpu.roll(part, shift, 1)
        short = short + jnp.where(group == j, part, 0.0)
    short = short * scale
    for d in range(count):
        y[pl.ds(d * ROWS_BACK + 4, 2), :] = owned
        y[pl.ds(d * ROWS_BACK + 6, 1), :] = short
        y[pl.ds(d * ROWS_BACK + 7, 1), :] = x[pl.ds(d * ROWS_OUT + ROW_K, 1), :]
    out[...] = y[...].astype(BF16)


def forward_kernel(gated, par, own_out):
    half = POLES // 2
    for part in range(2):
        modes = range(part * half, (part + 1) * half)
        decay = [decay_of(par, r) for r in modes]
        coef = [coef_of(par, r) for r in modes]
        ahead = (jnp.zeros((SUB, LANES), F32),) * half

        def forward(i, ahead, part=part, decay=decay, coef=coef):
            now = gated[tile(i), :]
            total = None if part == 0 else own_out[tile(i), :]
            after = []
            for h, d, c in zip(ahead, decay, coef):
                h = h + now
                term = c * h
                total = term if total is None else total + term
                after.append(h * d)
            own_out[tile(i), :] = total
            return tuple(after)

        lax.fori_loop(0, LEN, forward, ahead, unroll=16)


def halo_gates(last, par):
    return [
        add_in_order(tap_of(par, j) * last[tile(EDGE + t - j), :] for j in range(t + 1, TAPS))
        for t in range(HALO)
    ]


def unpack(x, state, first):
    for s in range(SUB):
        for row in range(2):
            block = x[pl.ds(s * SUB * ROWS_BACK + first + row, SUB, stride=ROWS_BACK), :]
            state[pl.ds(row * SUB * SUB + s, SUB, stride=SUB), :] = from_owner(block)


def query_part(own_out, vt, par, cot, grad_q, extra_gate, grad_short, x, state, long_out, last):
    unpack(x, state, 0)
    for s in range(SUB):
        short = x[pl.ds(s * SUB * ROWS_BACK + 6, SUB, stride=ROWS_BACK), :]
        grad_short[:, s * LANES : (s + 1) * LANES] = from_owner(short)[0:TAPS, :]
        keys = x[pl.ds(s * SUB * ROWS_BACK + 7, SUB, stride=ROWS_BACK), :]
        last[pl.ds(s, SUB, stride=SUB), :] = from_owner(keys)
    decay = [decay_of(par, r) for r in range(POLES)]

    def forward(t, terms):
        long_out[tile(t), :] = own_out[tile(t), :] + add_up(terms)
        return tuple(q * d for q, d in zip(terms, decay))

    terms = tuple(coef_of(par, r) * state[tile(r), :] for r in range(POLES))
    gates = halo_gates(last, par)
    for t in range(EDGE):
        if t < HALO:
            extra_gate[tile(t), :] = gates[t]
            extra = gates[t] * vt[tile(t), :]
            terms = tuple(q + coef_of(par, r) * extra for r, q in enumerate(terms))
        terms = forward(t, terms)
    lax.fori_loop(EDGE, LEN, forward, terms, unroll=24)
    for s in range(SUB):
        rows = slice(s * LANES, (s + 1) * LANES)
        grad_q[rows, :] = (cot[rows, :].astype(F32) * long_out[across(s), :].T).astype(BF16)


def key_part(gate, local, vt, extra_gate, head, par, grad_k, grad_v, x, state, slope, vals):
    unpack(x, state, 2)
    decay = [decay_of(par, r) for r in range(POLES)]
    back = [state[tile(r), :] for r in range(POLES)]
    growth = [1.0 / d for d in decay]
    ahead = []
    for n in range(HALO):
        ahead.append(
            add_up(coef_of(par, r) * back[r] for r in range(POLES)) * head[tile(EDGE + n), :]
        )
        if n < HALO - 1:
            z_now = head[tile(n), :]
            back = [(b - z_now) * g for b, g in zip(back, growth)]
    taps = [tap_of(par, j) for j in range(TAPS)]

    def backward(i, carry, extra=None):
        terms, ahead = carry
        t = LEN - 1 - i
        terms = tuple(q * d for q, d in zip(terms, decay))
        total = local[tile(t), :] + add_up(terms)
        now = gate[tile(t), :]
        vals[tile(t), :] = total * (now if extra is None else now + extra)
        slopes = (total * vt[tile(t), :], *ahead)
        slope[tile(t), :] = add_in_order(taps[j] * slopes[j] for j in range(TAPS))
        return terms, slopes[:HALO]

    terms = tuple(coef_of(par, r) * state[tile(r), :] for r in range(POLES))
    carry = (terms, tuple(ahead))
    carry = lax.fori_loop(0, LEN - EDGE, backward, carry, unroll=24)
    for t in reversed(range(EDGE)):
        extra = extra_gate[tile(t), :] if t < HALO else None
        carry = backward(LEN - 1 - t, carry, extra)
    for s in range(SUB):
        rows = slice(s * LANES, (s + 1) * LANES)
        grad_k[rows, :] = slope[across(s), :].T.astype(BF16)
        grad_v[rows, :] = vals[across(s), :].T.astype(BF16)


def leave_kernel(
    arrived, own_out, gate, local, vt, head, par, cot, grad_k, grad_v, grad_short, grad_q,
    x, state, long_out, last, extra_gate, slope, vals, query, gone,
):
    x[...] = arrived[...].astype(F32)
    query_part(own_out, vt, par, cot, query, extra_gate, grad_short, x, state, long_out, last)
    leaving = pltpu.make_async_copy(query, grad_q, gone)
    leaving.start()
    key_part(gate, local, vt, extra_gate, head, par, grad_k, grad_v, x, state, slope, vals)
    leaving.wait()


def pole_kernel(*refs):
    *parts, out, x = refs
    x[...] = add_up([part[...].astype(F32) for part in parts])
    for s in range(SUB):
        for half in range(2):
            block = x[pl.ds(s * SUB * 2 + half, SUB, stride=2), :]
            out[half * SUB : (half + 1) * SUB, s * LANES : (s + 1) * LANES] = from_owner(block)


def call(
    kernel, name, outs, scratch, operands, flops=0, moved=0, space=pltpu.VMEM, vmem=VMEM, last=None
):
    spaces = [space] * (len(outs) - 1) + [last or space]
    return pl.pallas_call(
        kernel,
        out_shape=outs,
        in_specs=[
            pl.BlockSpec(memory_space=pltpu.SMEM if a.dtype == jnp.int32 else space)
            for a in operands
        ],
        out_specs=[pl.BlockSpec(memory_space=s) for s in spaces],
        scratch_shapes=scratch,
        compiler_params=pltpu.CompilerParams(vmem_limit_bytes=vmem),
        cost_estimate=pl.CostEstimate(flops=flops, bytes_accessed=moved, transcendentals=0),
        name=name,
    )(*operands)


def shape(rows, dtype=F32, lanes=LANES):
    return jax.ShapeDtypeStruct((rows, lanes), dtype)


def per_device(q_in, k_in, v_in, cotangent, taps_short, residues, rates):
    channels, length = q_in.shape
    count = lax.axis_size("seq")
    index = lax.axis_index("seq")
    chans = lax.axis_size("chan")
    assert (channels, length, count) == (SUB * LANES, LEN, SUB * SUB)
    scale = (length * count) ** (-0.5)
    full, edge, halo = SUB * LEN, SUB * EDGE, SUB * HALO

    operands = (k_in, v_in, q_in, cotangent, rates.T, residues.T, taps_short.T)
    outs = [shape(full)] * 4 + [shape(SUB * 40), shape(2 * edge)]
    outs.append(shape(count * ROWS_OUT, BF16))
    vt, gate, gated, local, par, head, message = call(
        first_kernel,
        "first",
        outs,
        [
            *(pltpu.VMEM(a.shape, a.dtype) for a in (*operands, *outs)),
            pltpu.VMEM((full, LANES), F32),
            pltpu.VMEM((full, LANES), F32),
            pltpu.VMEM((9, full // 4 + SUB, LANES), F32),
            pltpu.VMEM((SUB * SUB * ROWS_OUT, LANES), F32),
            pltpu.VMEM((count * ROWS_OUT, LANES), F32),
            pltpu.SemaphoreType.DMA((len(operands),)),
            pltpu.SemaphoreType.DMA((len(outs),)),
        ],
        operands,
        flops=48 * 10**6,
        moved=4 * 10**6,
        space=pltpu.HBM,
        vmem=VMEM_FIRST,
    )

    def exchange(x, rows):
        x = x.reshape(count, rows // 2, 2, LANES)
        return lax.all_to_all(x, "seq", split_axis=0, concat_axis=0, tiled=True)

    arrived = exchange(message, ROWS_OUT).reshape(count * ROWS_OUT, LANES)
    head = lax.ppermute(head, "seq", [(i + 1, i) for i in range(count - 1)])
    (own_out,) = call(
        forward_kernel,
        "forward",
        [shape(full)],
        [],
        (gated, par),
        flops=10 * 10**6,
        moved=10**6,
    )
    arrived, own_out, head = lax.optimization_barrier((arrived, own_out, head))
    (back,) = call(
        functools.partial(owner_kernel, count, scale),
        "owner",
        [shape(count * ROWS_BACK, BF16)],
        [
            pltpu.VMEM(((count + 1) * ROWS_OUT, LANES), F32),
            pltpu.VMEM((count * ROWS_BACK, LANES), F32),
            pltpu.VMEM((3, count, SUB * LANES), F32),
            pltpu.VMEM((count * SUB, LANES), F32),
            pltpu.VMEM((SUB, LANES), F32),
        ],
        (index.reshape(1), arrived, rates.T, residues.T, taps_short.T),
        flops=2 * 10**6,
        moved=10**6,
    )
    returned = exchange(back, ROWS_BACK)
    poles = returned[:, 2].reshape(2 * count, LANES)
    returned = returned.reshape(count * ROWS_BACK, LANES)

    others = [
        lax.ppermute(poles, "chan", [(i, i ^ bits) for i in range(chans)]) for bits in (3, 1, 2)
    ]

    grad_k, grad_v, grad_short, grad_q = call(
        leave_kernel,
        "leave",
        [shape(channels, BF16)] * 2 + [shape(TAPS, F32, channels), shape(channels, BF16)],
        [
            pltpu.VMEM((count * ROWS_BACK, LANES), F32),
            pltpu.VMEM((SUB * POLES, LANES), F32),
            pltpu.VMEM((full, LANES), F32),
            pltpu.VMEM((edge, LANES), F32),
            pltpu.VMEM((halo, LANES), F32),
            pltpu.VMEM((full, LANES), F32),
            pltpu.VMEM((full, LANES), F32),
            pltpu.VMEM((channels, LANES), BF16),
            pltpu.SemaphoreType.DMA,
        ],
        (returned, own_out, gate, local, vt, head, par, cotangent),
        flops=13 * 10**6,
        moved=3 * 10**6,
        last=pltpu.HBM,
    )
    grad_k, *others = lax.optimization_barrier((grad_k, *others))
    (grad_residues,) = call(
        pole_kernel,
        "poles",
        [shape(POLES, F32, channels)],
        [pltpu.VMEM((2 * count, LANES), F32)],
        (poles, *others),
        flops=10**5,
        moved=10**5,
    )
    return grad_q, grad_k, grad_v, grad_short.T, grad_residues.T


def solution(mesh):
    streams = P("chan", "seq")
    return jax.shard_map(
        per_device,
        mesh=mesh,
        in_specs=(streams,) * 4 + (P("chan", None), P(), P()),
        out_specs=(streams,) * 3 + (P("chan", None), P()),
        check_vma=False,
    )
```

```python
import functools

import jax
import jax.numpy as jnp
from jax import lax
from jax.experimental import pallas as pl
from jax.experimental.pallas import tpu as pltpu
from jax.sharding import PartitionSpec as P

F32 = jnp.float32
BF16 = jnp.bfloat16
LANES = 128
SUB = 8
LEN = 128
POLES = 16
TAPS = 7
HALO = TAPS - 1
EDGE = 8
ROWS_OUT = 24
FIR_TERMS = tuple((n, q) for n in range(9) for q in range(2) if (n, q) != (8, 1))
BACK_MODES, BACK_UNROLL, AHEAD_MODES, AHEAD_UNROLL = 8, 16, 2, 32
ROW_SHORT, ROW_V, ROW_MOMENT, ROW_K, ROW_Z = 6, 7, 8, 22, 23
ROWS_BACK = 8
VMEM = 48 * 1024 * 1024
VMEM_FIRST = 62 * 1024 * 1024


def one_minus_exp(x):
    series = 1.0 - x * (1.0 / 7.0)
    for order in (6.0, 5.0, 4.0, 3.0, 2.0):
        series = 1.0 - x * (1.0 / order) * series
    return x * series


def tile(index):
    if isinstance(index, int):
        return pl.ds(SUB * index, SUB)
    return pl.ds(pl.multiple_of(SUB * index, SUB), SUB)


def across(block):
    return pl.ds(block, LEN, stride=SUB)


def lane_group():
    return lax.broadcasted_iota(jnp.int32, (SUB, LANES), 1) // 16


def skewed(x, way):
    row = lax.broadcasted_iota(jnp.int32, (SUB, LANES), 0)
    lane = lax.broadcasted_iota(jnp.int32, (SUB, LANES), 1)
    return jnp.take_along_axis(x, (lane + way * 16 * row) % LANES, axis=1)


def turned(x, way):
    row = lax.broadcasted_iota(jnp.int32, (SUB, LANES), 0)
    return jnp.take_along_axis(x, (row + way * lane_group()) % SUB, axis=0)


def to_owner(x):
    return skewed(turned(skewed(x, -1), 1), -1)


def from_owner(x):
    return skewed(turned(skewed(x, 1), -1), 1)


def decay_of(par, r):
    return par[tile(r), :]


def coef_of(par, r):
    return par[tile(POLES + r), :]


def add_in_order(terms):
    return functools.reduce(lambda a, b: a + b, terms)


def tap_of(par, j):
    return par[tile(2 * POLES + j), :]


def add_up(terms):
    terms = list(terms)
    while len(terms) > 1:
        terms = [a + b for a, b in zip(terms[0::2], terms[1::2])]
    return terms[0]


def key_sums(now, before):
    even = (now[0], now[1] - now[0], before[0] - now[0])
    odd = (now[2], now[3] - now[2], now[1] - now[2])
    earlier = (before[1], before[0] - before[1], before[2] - before[1])
    return [x for e, o, p in zip(even, odd, earlier) for x in (e, o - e, p - e)]


def correlate(sums, u, keys):
    lines = (
        (u[0] + u[1], u[2] + u[3]),
        (u[1], u[3]),
        (u[0], u[2]),
    )
    factors = []
    for even, odd in lines:
        factors += [even + odd, odd, even]
    return [
        total + factors[line] * keys[q][line]
        for total, (line, q) in zip(sums, FIR_TERMS)
    ]


def moments(sums):
    part = dict(zip(FIR_TERMS, sums))
    lines = []
    for n in range(3):
        line = []
        for q in range(2):
            line.append(part[3 * n, q] + part[3 * n + 1, q])
            if (3 * n + 2, q) in part:
                line.append(part[3 * n + 2, q] + part[3 * n, q])
        lines.append(line)
    both, odd, even = lines
    out = []
    for j in range(TAPS):
        n = j // 2
        out.append(both[n] + (even[n] if j % 2 else odd[n]))
    return out


def scan_down(par, z, v, gated, keys, local, gather):
    zero = jnp.zeros((SUB, LANES), F32)
    terms = len(FIR_TERMS)

    def keys_of(m):
        return tuple(keys[n, tile(m + 1), :] for n in range(9))

    for first in range(0, POLES, BACK_MODES):
        modes = range(first, first + BACK_MODES)
        decay = [decay_of(par, r) for r in modes]
        coef = [coef_of(par, r) for r in modes]

        def back_step(i, state, first=first, decay=decay, coef=coef):
            at = tile(LEN - 1 - i)
            z_now, g_now = z[at, :], gated[at, :]
            after, parts = [], []
            for (back, pole), d, c in zip(state, decay, coef):
                back = back * d + z_now
                after.append((back, pole + g_now * back))
                parts.append(c * back)
            total = add_up(parts)
            local[at, :] = total if first == 0 else local[at, :] + total
            return tuple(after)

        state = lax.fori_loop(
            0, LEN, back_step, ((zero, zero),) * BACK_MODES, unroll=BACK_UNROLL
        )
        for (back, pole), r in zip(state, modes):
            half, slot = divmod(r, SUB)
            gather[tile((2 + half) * SUB + slot), :] = back
            gather[tile((4 + half) * SUB + slot), :] = pole

    for first in range(0, POLES, AHEAD_MODES):
        modes = range(first, first + AHEAD_MODES)
        decay = [decay_of(par, r) for r in modes]

        def ahead_step(i, carry, decay=decay):
            state, now = carry
            m = LEN // 4 - 1 - i
            at = [tile(4 * m + n) for n in range(4)]
            before = keys_of(m - 1)
            keyed = (now, before)
            after = []
            for (power, sums), d in zip(state, decay):
                u = [None] * 4
                for p in reversed(range(4)):
                    u[p] = power * v[at[p], :]
                    power = power * d
                after.append((power, tuple(correlate(sums, u, keyed))))
            return tuple(after), before

        state = tuple((d, (zero,) * terms) for d in decay)
        carry = (state, keys_of(LEN // 4 - 1))
        state, _ = lax.fori_loop(0, LEN // 4, ahead_step, carry, unroll=AHEAD_UNROLL)
        for (_, sums), r in zip(state, modes):
            half, slot = divmod(r, SUB)
            taken = moments(sums)
            ahead = add_in_order(tap_of(par, j) * value for j, value in enumerate(taken))
            gather[tile(half * SUB + slot), :] = ahead
            for j, value in enumerate(taken):
                gather[tile((ROW_MOMENT + 2 * j + half) * SUB + slot), :] = value

    def step(m, carry):
        sums, before = carry
        at = [tile(4 * m + n) for n in range(4)]
        now = keys_of(m)
        u = [local[p, :] * v[p, :] for p in at]
        return tuple(correlate(sums, u, (now, before))), now

    sums, _ = lax.fori_loop(0, LEN // 4, step, ((zero,) * terms, keys_of(-1)), unroll=8)
    for j, value in enumerate(moments(sums)):
        gather[tile(ROW_SHORT * SUB + j), :] = value


def first_kernel(*refs):
    sources, targets, refs = refs[:7], refs[7:14], refs[14:]
    (k, v, q, cot, rates, residues, amounts), refs = refs[:7], refs[7:]
    (vt, gate, gated, local, par, head, message), refs = refs[:7], refs[7:]
    kt, zt, keys, gather, spread, came, went = refs
    copies = [
        pltpu.make_async_copy(a, b, came.at[n])
        for n, (a, b) in enumerate(zip(sources, (k, v, q, cot, rates, residues, amounts)))
    ]
    leaving = [
        pltpu.make_async_copy(a, b, went.at[n])
        for n, (a, b) in enumerate(zip((vt, gate, gated, local, par, head, message), targets))
    ]
    for copy in copies:
        copy.start()
    copies[0].wait()
    for s in range(SUB):
        kt[across(s), :] = k[s * LANES : (s + 1) * LANES, :].astype(F32).T
    copies[1].wait()
    for s in range(SUB):
        vt[across(s), :] = v[s * LANES : (s + 1) * LANES, :].astype(F32).T
    leaving[0].start()
    for copy in copies[2:]:
        copy.wait()
    for s in range(SUB):
        rows = slice(s * LANES, (s + 1) * LANES)
        zt[across(s), :] = (q[rows, :].astype(F32) * cot[rows, :].astype(F32)).T
        rate = rates[:, rows]
        par[pl.ds(s, POLES, stride=SUB), :] = jnp.exp(-rate)
        par[pl.ds(SUB * POLES + s, POLES, stride=SUB), :] = residues[:, rows] * jnp.sqrt(
            one_minus_exp(2.0 * rate)
        )
        par[pl.ds(2 * SUB * POLES + s, TAPS, stride=SUB), :] = amounts[:, rows]
    edge = SUB * EDGE
    head[0:edge, :] = zt[0:edge, :]
    head[edge:, :] = vt[0:edge, :]
    for n in (4, 5):
        leaving[n].start()
    for row, block in (
        (ROW_V, vt[0:edge, :]),
        (ROW_K, kt[SUB * (LEN - EDGE) : SUB * LEN, :]),
        (ROW_Z, zt[0:edge, :]),
    ):
        gather[row * edge : (row + 1) * edge, :] = block

    taps = [tap_of(par, j) for j in range(TAPS)]

    def prepare(m, before):
        at = [tile(4 * m + n) for n in range(4)]
        now = [kt[p, :] for p in at]
        line = [*reversed(now), *before]
        for n in range(4):
            total = add_in_order(taps[j] * line[3 - n + j] for j in range(TAPS))
            gate[at[n], :] = total
            gated[at[n], :] = total * vt[at[n], :]
        for n, value in enumerate(key_sums(now, before)):
            keys[n, tile(m + 1), :] = value
        return tuple(line[:HALO])

    gather[tile(ROW_SHORT * SUB + TAPS), :] = jnp.zeros((SUB, LANES), F32)
    zero = gather[tile(ROW_SHORT * SUB + TAPS), :]
    for n in range(9):
        keys[n, tile(0), :] = zero
    lax.fori_loop(0, LEN // 4, prepare, (zero,) * HALO, unroll=2)
    leaving[1].start()
    leaving[2].start()
    scan_down(par, zt, vt, gated, keys, local, gather)
    leaving[3].start()
    size = message.shape[0] // 2
    halves = []
    for n in range(2):
        for s in range(n * SUB // 2, (n + 1) * SUB // 2):
            for row in range(ROWS_OUT):
                block = to_owner(gather[pl.ds(row * SUB * SUB + s, SUB, stride=SUB), :])
                spread[pl.ds(s * SUB * ROWS_OUT + row, SUB, stride=ROWS_OUT), :] = block
        part = pl.ds(n * size, size)
        message[part, :] = spread[part, :].astype(BF16)
        halves.append(
            pltpu.make_async_copy(message.at[part, :], targets[-1].at[part, :], went.at[6 + n])
        )
        halves[-1].start()
    leaving = [*leaving[:-1], *halves]
    for copy in leaving:
        copy.wait()


def owner_kernel(
    count, scale, index, arrived, rate_rows, residue_rows, tap_rows, out, x, y, kept, fix, mine
):
    x[0:ROWS_OUT, :] = jnp.zeros((ROWS_OUT, LANES), F32)
    x[ROWS_OUT:, :] = arrived[...].astype(F32)
    even = lax.broadcasted_iota(jnp.int32, (SUB, LANES), 0) % 2 == 0
    group = lane_group()
    zero = jnp.zeros((SUB, LANES), F32)

    block = pl.ds(pl.multiple_of((index[0] // SUB) * LANES, LANES), LANES)
    place = index[0] % SUB
    for n, ref in enumerate((rate_rows, residue_rows)):
        for half in range(2):
            mine[...] = to_owner(ref[half * SUB : (half + 1) * SUB, block])
            fix[2 * n + half : 2 * n + half + 1, :] = mine[pl.ds(place, 1), :]
    held = jnp.where(group[0:TAPS, :] == (SUB - place) % SUB, tap_rows[:, block], 0.0)
    for shift in (16, 32, 64):
        held = held + pltpu.roll(held, shift, 1)
    taps = [jnp.broadcast_to(held[j : j + 1, :], (SUB, LANES)) for j in range(TAPS)]

    def pattern(ref, row):
        return jnp.where(even, ref[pl.ds(row, 1), :], ref[pl.ds(row + 1, 1), :])

    rate = pattern(fix, 0)
    weight = jnp.sqrt(one_minus_exp(2.0 * rate))
    coef = pattern(fix, 2) * weight
    leap = jnp.exp(-float(LEN) * rate)
    rates = [fix[pl.ds(half, 1), :] for half in range(2)]
    growth = [jnp.broadcast_to(jnp.exp(r), (SUB, LANES)) for r in rates]
    powers = [
        [jnp.broadcast_to(jnp.exp(-float(LEN - t) * r), (SUB, LANES)) for t in range(HALO)]
        for r in rates
    ]

    source = lax.broadcasted_iota(jnp.int32, (LANES, SUB * LANES), 0)
    target = lax.broadcasted_iota(jnp.int32, (LANES, SUB * LANES), 1)
    same = (source // 16 == target // LANES) & (source % 16 == target % 16)
    everywhere = jnp.where(same, 1.0, 0.0).astype(BF16)
    for n, (row, first) in enumerate(((ROW_V, 1), (ROW_Z, 1), (ROW_K, 0))):
        rows = x[pl.ds(first * ROWS_OUT + row, count, stride=ROWS_OUT), :].astype(BF16)
        kept[n] = jnp.dot(rows, everywhere, preferred_element_type=F32)

    def edge_of(b):
        at = pl.ds(b * SUB, SUB)
        value, slope = (
            [kept[n, at, t * LANES : (t + 1) * LANES] for t in range(HALO)] for n in range(2)
        )
        key = [kept[2, at, (EDGE - m) * LANES : (EDGE - m + 1) * LANES] for m in range(1, TAPS)]
        return value, slope, [None, *key]

    def shards(row, b):
        return pl.ds((b * SUB + 1) * ROWS_OUT + row, SUB, stride=ROWS_OUT)

    fix[...] = jnp.zeros(fix.shape, F32)
    batches = count // SUB
    poles = [zero, zero]
    for b in range(batches):
        value, slope, key = edge_of(b)
        extra = [
            value[t] * add_in_order(taps[j] * key[j - t] for j in range(t + 1, TAPS))
            for t in range(HALO)
        ]
        for half in range(2):
            back = x[shards(2 + half, b), :]
            fix[pl.ds(b * SUB * SUB + half, SUB, stride=SUB), :] = add_in_order(
                extra[t] * powers[half][t] for t in range(HALO)
            )
            for t in range(HALO):
                poles[half] = poles[half] + extra[t] * back
                if t < HALO - 1:
                    back = (back - slope[t]) * growth[half]

    ahead, pole, total = zero, zero, zero
    for d in range(count):
        base = (d + 1) * ROWS_OUT
        y[pl.ds(d * ROWS_BACK, 2), :] = ahead[0:2, :]
        now = x[pl.ds(base, SUB), :]
        pole = pole + ahead * pattern(x, base + 2)
        total = total + now
        ahead = ahead * leap + (now + fix[tile(d), :])
    back, low, high = zero, zero, zero
    for d in reversed(range(count)):
        base = (d + 1) * ROWS_OUT
        y[pl.ds(d * ROWS_BACK + 2, 2), :] = back[0:2, :]
        low = low + back * x[pl.ds(base + SUB, SUB), :]
        high = high + back * x[pl.ds(base + 2 * SUB, SUB), :]
        back = back * leap + pattern(x, base + 2)

    edges = [[zero] * TAPS for _ in range(2)]
    for b in range(batches):
        value, slope, key = edge_of(b)
        start = b * SUB
        states = []
        for half in range(2):
            own = x[shards(2 + half, b), :]
            later = y[pl.ds(start * ROWS_BACK + 2 + half, SUB, stride=ROWS_BACK), :]
            states.append(own + later * powers[half][0])
        for t in range(HALO):
            for j in range(t + 1, TAPS):
                product = value[t] * key[j - t]
                for half in range(2):
                    edges[half][j] = edges[half][j] + states[half] * product
            states = [(a - slope[t]) * g for a, g in zip(states, growth)]

    def down(rows):
        return jnp.sum(rows, axis=0, keepdims=True)

    owned = jnp.concatenate([down(p) for p in poles])
    owned = (owned + pole[0:2, :] + total[4:6, :]) * weight[0:2, :] * scale
    short = total[ROW_SHORT : ROW_SHORT + 1, :]
    group = group[0:1, :]
    for part, first in ((low * coef, 0), (high * coef, 4)):
        part = part + pltpu.roll(part, SUB - 1, 0)
        for shift in (16, 32, 64):
            part = part + pltpu.roll(part, shift, 1)
        for n in range(min(4, TAPS - first)):
            short = short + jnp.where(group == first + n, part[2 * n : 2 * n + 1, :], 0.0)
    for j in range(1, TAPS):
        part = down(edges[0][j]) * coef[0:1, :] + down(edges[1][j]) * coef[1:2, :]
        for shift in (16, 32, 64):
            part = part + pltpu.roll(part, shift, 1)
        short = short + jnp.where(group == j, part, 0.0)
    short = short * scale
    for d in range(count):
        y[pl.ds(d * ROWS_BACK + 4, 2), :] = owned
        y[pl.ds(d * ROWS_BACK + 6, 1), :] = short
        y[pl.ds(d * ROWS_BACK + 7, 1), :] = x[pl.ds(d * ROWS_OUT + ROW_K, 1), :]
    out[...] = y[...].astype(BF16)


def forward_kernel(gated, par, own_out):
    half = POLES // 2
    for part in range(2):
        modes = range(part * half, (part + 1) * half)
        decay = [decay_of(par, r) for r in modes]
        coef = [coef_of(par, r) for r in modes]
        ahead = (jnp.zeros((SUB, LANES), F32),) * half

        def forward(i, ahead, part=part, decay=decay, coef=coef):
            now = gated[tile(i), :]
            total = None if part == 0 else own_out[tile(i), :]
            after = []
            for h, d, c in zip(ahead, decay, coef):
                h = h + now
                term = c * h
                total = term if total is None else total + term
                after.append(h * d)
            own_out[tile(i), :] = total
            return tuple(after)

        lax.fori_loop(0, LEN, forward, ahead, unroll=16)


def halo_gates(last, par):
    return [
        add_in_order(tap_of(par, j) * last[tile(EDGE + t - j), :] for j in range(t + 1, TAPS))
        for t in range(HALO)
    ]


def unpack(x, state, first):
    for s in range(SUB):
        for row in range(2):
            block = x[pl.ds(s * SUB * ROWS_BACK + first + row, SUB, stride=ROWS_BACK), :]
            state[pl.ds(row * SUB * SUB + s, SUB, stride=SUB), :] = from_owner(block)


def query_part(own_out, vt, par, cot, grad_q, extra_gate, grad_short, x, state, long_out, last):
    unpack(x, state, 0)
    for s in range(SUB):
        short = x[pl.ds(s * SUB * ROWS_BACK + 6, SUB, stride=ROWS_BACK), :]
        grad_short[:, s * LANES : (s + 1) * LANES] = from_owner(short)[0:TAPS, :]
        keys = x[pl.ds(s * SUB * ROWS_BACK + 7, SUB, stride=ROWS_BACK), :]
        last[pl.ds(s, SUB, stride=SUB), :] = from_owner(keys)
    decay = [decay_of(par, r) for r in range(POLES)]

    def forward(t, terms):
        long_out[tile(t), :] = own_out[tile(t), :] + add_up(terms)
        return tuple(q * d for q, d in zip(terms, decay))

    terms = tuple(coef_of(par, r) * state[tile(r), :] for r in range(POLES))
    gates = halo_gates(last, par)
    for t in range(EDGE):
        if t < HALO:
            extra_gate[tile(t), :] = gates[t]
            extra = gates[t] * vt[tile(t), :]
            terms = tuple(q + coef_of(par, r) * extra for r, q in enumerate(terms))
        terms = forward(t, terms)
    lax.fori_loop(EDGE, LEN, forward, terms, unroll=24)
    for s in range(SUB):
        rows = slice(s * LANES, (s + 1) * LANES)
        grad_q[rows, :] = (cot[rows, :].astype(F32) * long_out[across(s), :].T).astype(BF16)


def key_part(gate, local, vt, extra_gate, head, par, grad_k, grad_v, x, state, slope, vals):
    unpack(x, state, 2)
    decay = [decay_of(par, r) for r in range(POLES)]
    back = [state[tile(r), :] for r in range(POLES)]
    growth = [1.0 / d for d in decay]
    ahead = []
    for n in range(HALO):
        ahead.append(
            add_up(coef_of(par, r) * back[r] for r in range(POLES)) * head[tile(EDGE + n), :]
        )
        if n < HALO - 1:
            z_now = head[tile(n), :]
            back = [(b - z_now) * g for b, g in zip(back, growth)]
    taps = [tap_of(par, j) for j in range(TAPS)]

    def backward(i, carry, extra=None):
        terms, ahead = carry
        t = LEN - 1 - i
        terms = tuple(q * d for q, d in zip(terms, decay))
        total = local[tile(t), :] + add_up(terms)
        now = gate[tile(t), :]
        vals[tile(t), :] = total * (now if extra is None else now + extra)
        slopes = (total * vt[tile(t), :], *ahead)
        slope[tile(t), :] = add_in_order(taps[j] * slopes[j] for j in range(TAPS))
        return terms, slopes[:HALO]

    terms = tuple(coef_of(par, r) * state[tile(r), :] for r in range(POLES))
    carry = (terms, tuple(ahead))
    carry = lax.fori_loop(0, LEN - EDGE, backward, carry, unroll=24)
    for t in reversed(range(EDGE)):
        extra = extra_gate[tile(t), :] if t < HALO else None
        carry = backward(LEN - 1 - t, carry, extra)
    for s in range(SUB):
        rows = slice(s * LANES, (s + 1) * LANES)
        grad_k[rows, :] = slope[across(s), :].T.astype(BF16)
        grad_v[rows, :] = vals[across(s), :].T.astype(BF16)


def leave_kernel(
    arrived, own_out, gate, local, vt, head, par, cot, grad_k, grad_v, grad_short, grad_q,
    x, state, long_out, last, extra_gate, slope, vals, query, gone,
):
    x[...] = arrived[...].astype(F32)
    query_part(own_out, vt, par, cot, query, extra_gate, grad_short, x, state, long_out, last)
    leaving = pltpu.make_async_copy(query, grad_q, gone)
    leaving.start()
    key_part(gate, local, vt, extra_gate, head, par, grad_k, grad_v, x, state, slope, vals)
    leaving.wait()


def pole_kernel(*refs):
    *parts, out, x = refs
    x[...] = add_up([part[...].astype(F32) for part in parts])
    for s in range(SUB):
        for half in range(2):
            block = x[pl.ds(s * SUB * 2 + half, SUB, stride=2), :]
            out[half * SUB : (half + 1) * SUB, s * LANES : (s + 1) * LANES] = from_owner(block)


def call(
    kernel, name, outs, scratch, operands, flops=0, moved=0, space=pltpu.VMEM, vmem=VMEM, last=None
):
    spaces = [space] * (len(outs) - 1) + [last or space]
    return pl.pallas_call(
        kernel,
        out_shape=outs,
        in_specs=[
            pl.BlockSpec(memory_space=pltpu.SMEM if a.dtype == jnp.int32 else space)
            for a in operands
        ],
        out_specs=[pl.BlockSpec(memory_space=s) for s in spaces],
        scratch_shapes=scratch,
        compiler_params=pltpu.CompilerParams(vmem_limit_bytes=vmem),
        cost_estimate=pl.CostEstimate(flops=flops, bytes_accessed=moved, transcendentals=0),
        name=name,
    )(*operands)


def shape(rows, dtype=F32, lanes=LANES):
    return jax.ShapeDtypeStruct((rows, lanes), dtype)


def per_device(q_in, k_in, v_in, cotangent, taps_short, residues, rates):
    channels, length = q_in.shape
    count = lax.axis_size("seq")
    index = lax.axis_index("seq")
    chans = lax.axis_size("chan")
    assert (channels, length, count) == (SUB * LANES, LEN, SUB * SUB)
    scale = (length * count) ** (-0.5)
    full, edge, halo = SUB * LEN, SUB * EDGE, SUB * HALO

    operands = (k_in, v_in, q_in, cotangent, rates.T, residues.T, taps_short.T)
    outs = [shape(full)] * 4 + [shape(SUB * 40), shape(2 * edge)]
    outs.append(shape(count * ROWS_OUT, BF16))
    vt, gate, gated, local, par, head, message = call(
        first_kernel,
        "first",
        outs,
        [
            *(pltpu.VMEM(a.shape, a.dtype) for a in (*operands, *outs)),
            pltpu.VMEM((full, LANES), F32),
            pltpu.VMEM((full, LANES), F32),
            pltpu.VMEM((9, full // 4 + SUB, LANES), F32),
            pltpu.VMEM((SUB * SUB * ROWS_OUT, LANES), F32),
            pltpu.VMEM((count * ROWS_OUT, LANES), F32),
            pltpu.SemaphoreType.DMA((len(operands),)),
            pltpu.SemaphoreType.DMA((len(outs) + 1,)),
        ],
        operands,
        flops=48 * 10**6,
        moved=4 * 10**6,
        space=pltpu.HBM,
        vmem=VMEM_FIRST,
    )

    def exchange(x, rows):
        x = x.reshape(count, rows // 2, 2, LANES)
        return lax.all_to_all(x, "seq", split_axis=0, concat_axis=0, tiled=True)

    arrived = exchange(message, ROWS_OUT).reshape(count * ROWS_OUT, LANES)
    head = lax.ppermute(head, "seq", [(i + 1, i) for i in range(count - 1)])
    (own_out,) = call(
        forward_kernel,
        "forward",
        [shape(full)],
        [],
        (gated, par),
        flops=10 * 10**6,
        moved=10**6,
    )
    arrived, own_out, head = lax.optimization_barrier((arrived, own_out, head))
    (back,) = call(
        functools.partial(owner_kernel, count, scale),
        "owner",
        [shape(count * ROWS_BACK, BF16)],
        [
            pltpu.VMEM(((count + 1) * ROWS_OUT, LANES), F32),
            pltpu.VMEM((count * ROWS_BACK, LANES), F32),
            pltpu.VMEM((3, count, SUB * LANES), F32),
            pltpu.VMEM((count * SUB, LANES), F32),
            pltpu.VMEM((SUB, LANES), F32),
        ],
        (index.reshape(1), arrived, rates.T, residues.T, taps_short.T),
        flops=2 * 10**6,
        moved=10**6,
    )
    returned = exchange(back, ROWS_BACK)
    poles = returned[:, 2].reshape(2 * count, LANES)
    returned = returned.reshape(count * ROWS_BACK, LANES)

    others = [
        lax.ppermute(poles, "chan", [(i, i ^ bits) for i in range(chans)]) for bits in (3, 1, 2)
    ]

    grad_k, grad_v, grad_short, grad_q = call(
        leave_kernel,
        "leave",
        [shape(channels, BF16)] * 2 + [shape(TAPS, F32, channels), shape(channels, BF16)],
        [
            pltpu.VMEM((count * ROWS_BACK, LANES), F32),
            pltpu.VMEM((SUB * POLES, LANES), F32),
            pltpu.VMEM((full, LANES), F32),
            pltpu.VMEM((edge, LANES), F32),
            pltpu.VMEM((halo, LANES), F32),
            pltpu.VMEM((full, LANES), F32),
            pltpu.VMEM((full, LANES), F32),
            pltpu.VMEM((channels, LANES), BF16),
            pltpu.SemaphoreType.DMA,
        ],
        (returned, own_out, gate, local, vt, head, par, cotangent),
        flops=13 * 10**6,
        moved=3 * 10**6,
        last=pltpu.HBM,
    )
    grad_k, *others = lax.optimization_barrier((grad_k, *others))
    (grad_residues,) = call(
        pole_kernel,
        "poles",
        [shape(POLES, F32, channels)],
        [pltpu.VMEM((2 * count, LANES), F32)],
        (poles, *others),
        flops=10**5,
        moved=10**5,
    )
    return grad_q, grad_k, grad_v, grad_short.T, grad_residues.T


def solution(mesh):
    streams = P("chan", "seq")
    return jax.shard_map(
        per_device,
        mesh=mesh,
        in_specs=(streams,) * 4 + (P("chan", None), P(), P()),
        out_specs=(streams,) * 3 + (P("chan", None), P()),
        check_vma=False,
    )
```
